256 devices in a mesh: ax: 4 (over y_hi, core), az: 64 (over y_lo, x, z).
Axes of the slice: x: 4, y: 4 (y_hi: 2, y_lo: 2; y = y_hi * 2 + y_lo), z: 8, core: 2. Of those that a mesh axis runs over, the one named last changes fastest.
Arguments:
- state: float32 [5, 16, 2560, 128], P(None, 'ax', 'az'), may hold values from -4 to 8, as said below
- shock_flags: int32 [2, 16, 2560, 128], P(None, 'ax', 'az'), may hold values from 0 to 1
Outputs:
- increment: float32 [5, 16, 2560, 128], P(None, 'ax', 'az')
The draws below stay inside these ranges and needn't reach their ends.
Inputs may be any that keep to these rules, and one draw needn't show every extreme that they name: `state`: density in 0.8 to 1.25 and pressure in 0.8 to 1.25 in every cell.
All inputs are finite; a program needn't handle non-finite values.
Results may differ from the reference program's by a relative error of at most 0.0003.
Values sent between devices are 32-bit elements; how exact they have to be, the bound alone decides.
A program may use at most 64 MiB of HBM per device.

```python
import math
import jax
import jax.numpy as jnp
from jax import lax

NR = 128
NT = 2560
NRING = 16
KEEP = 32
NA = 16


def draw_state(key, part):
    key = jax.random.fold_in(key, 11)
    keys = jax.random.split(key, 5)
    shape = (NA, NT, NR)
    radial = jnp.arange(NR, dtype=jnp.int32)[None, None, :]
    inside = radial < NR // 3
    core = jnp.where(inside, 0.6, 0.0).astype(jnp.float32)
    theta = (jnp.arange(NT, dtype=jnp.float32)[None, :, None] + 0.5) * (2.0 * math.pi / NT)
    cross = jnp.where(inside, 0.6, 0.0).astype(jnp.float32)
    density = jax.random.uniform(keys[0], shape, jnp.float32, 0.8, 1.25)
    axial_v = core + 0.3 * jnp.clip(jax.random.normal(keys[1], shape, jnp.float32), -3.0, 3.0)
    radial_v = cross * jnp.cos(theta) + 0.3 * jnp.clip(jax.random.normal(keys[2], shape, jnp.float32), -3.0, 3.0)
    swirl_v = -cross * jnp.sin(theta) + 0.3 * jnp.clip(jax.random.normal(keys[3], shape, jnp.float32), -3.0, 3.0)
    pressure = jax.random.uniform(keys[4], shape, jnp.float32, 0.8, 1.25)
    energy = pressure / 0.4 + 0.5 * density * (axial_v * axial_v + radial_v * radial_v + swirl_v * swirl_v)
    return jnp.stack([density, density * axial_v, density * radial_v, density * swirl_v, energy])


def draw_shock_flags(key, part):
    key = jax.random.fold_in(key, 23)
    radial = jnp.arange(NR, dtype=jnp.int32)[None, None, None, :]
    axial = jnp.arange(NA, dtype=jnp.int32)[None, :, None, None]
    band = jnp.abs(radial - NR // 3) < NR // 10 + 2
    percent = jnp.where(band, 20 + 60 * axial // NA, 4)
    rolls = jax.random.randint(key, (2, NA, NT, NR), 0, 100, dtype=jnp.int32)
    return jnp.where(rolls < percent, 1, 0).astype(jnp.int32)


def setup_inputs(seed: int = 0) -> dict:
    key_of = jax.random.split(jax.random.key(seed), 3)
    return {
        "state": draw_state(jax.random.fold_in(key_of[2], 71), 0),
        "shock_flags": draw_shock_flags(jax.random.fold_in(key_of[2], 71), 0),
    }


split_speed = 3.0
small_eps = 1e-6
time_step = 4e-3


def pressure_of(conserved):
    return 0.4 * (conserved[4] - 0.5 * (conserved[1] * conserved[1] + conserved[2] * conserved[2] + conserved[3] * conserved[3]) / conserved[0])


def euler_flux(conserved, component):
    velocity = conserved[1 + component] / conserved[0]
    pressure = pressure_of(conserved)
    parts = [conserved[0] * velocity, conserved[1] * velocity, conserved[2] * velocity, conserved[3] * velocity, (conserved[4] + pressure) * velocity]
    parts[1 + component] = parts[1 + component] + pressure
    return jnp.stack(parts)


def weno_side(far_left, left, centre, right, far_right):
    cand_zero = (2.0 * far_left - 7.0 * left + 11.0 * centre) / 6.0
    cand_one = (-left + 5.0 * centre + 2.0 * right) / 6.0
    cand_two = (2.0 * centre + 5.0 * right - far_right) / 6.0
    smooth_zero = 13.0 / 12.0 * (far_left - 2.0 * left + centre) ** 2 + 0.25 * (far_left - 4.0 * left + 3.0 * centre) ** 2
    smooth_one = 13.0 / 12.0 * (left - 2.0 * centre + right) ** 2 + 0.25 * (left - right) ** 2
    smooth_two = 13.0 / 12.0 * (centre - 2.0 * right + far_right) ** 2 + 0.25 * (3.0 * centre - 4.0 * right + far_right) ** 2
    weight_zero = 0.1 / (small_eps + smooth_zero) ** 2
    weight_one = 0.6 / (small_eps + smooth_one) ** 2
    weight_two = 0.3 / (small_eps + smooth_two) ** 2
    return (weight_zero * cand_zero + weight_one * cand_one + weight_two * cand_two) / (weight_zero + weight_one + weight_two)


def face_flux(conserved, flag_field, axis_dim, cell_count, component):
    fluxes = euler_flux(conserved, component)
    plus_part = 0.5 * (fluxes + split_speed * conserved)
    minus_part = 0.5 * (fluxes - split_speed * conserved)

    def take(field, offset, along):
        return lax.slice_in_dim(field, 2 + offset, 3 + offset + cell_count, axis=along)

    plus_face = weno_side(take(plus_part, -2, axis_dim), take(plus_part, -1, axis_dim), take(plus_part, 0, axis_dim), take(plus_part, 1, axis_dim), take(plus_part, 2, axis_dim))
    minus_face = weno_side(take(minus_part, 3, axis_dim), take(minus_part, 2, axis_dim), take(minus_part, 1, axis_dim), take(minus_part, 0, axis_dim), take(minus_part, -1, axis_dim))
    central = (-take(fluxes, -1, axis_dim) + 7.0 * take(fluxes, 0, axis_dim) + 7.0 * take(fluxes, 1, axis_dim) - take(fluxes, 2, axis_dim)) / 12.0
    switch = take(flag_field, -2, axis_dim - 1)
    for offset in range(-1, 4):
        switch = jnp.maximum(switch, take(flag_field, offset, axis_dim - 1))
    return jnp.where(switch[None] > 0.5, plus_face + minus_face, central)


def tendency(padded, ghost, dtheta):
    axial_n = padded.shape[1] - 6
    turn_n = padded.shape[2] - 6
    strip_axial = padded[:, :, 3:3 + turn_n]
    axial_faces = face_flux(strip_axial[:5], strip_axial[5], 1, axial_n, 0)
    axial_diff = axial_faces[:, 1:] - axial_faces[:, :-1]
    strip_turn = padded[:, 3:3 + axial_n]
    turn_faces = face_flux(strip_turn[:5], strip_turn[5], 2, turn_n, 2)
    turn_diff = turn_faces[:, :, 1:] - turn_faces[:, :, :-1]
    inner = padded[:5, 3:3 + axial_n, 3:3 + turn_n]
    radial = euler_flux(inner, 1)
    radial_ghost = euler_flux(ghost[..., None], 1)
    radial_pad = jnp.concatenate([radial_ghost, radial, radial[..., -1:]], axis=3)
    radial_diff = 0.5 * (radial_pad[..., 2:] - radial_pad[..., :-2])
    swirl = inner[3] / inner[0]
    pressure = pressure_of(inner)
    zeros_field = jnp.zeros_like(pressure)
    source = jnp.stack([zeros_field, zeros_field, inner[3] * swirl + pressure, -inner[2] * swirl, zeros_field])
    radius = jnp.arange(inner.shape[3], dtype=jnp.float32) + 0.5
    return -axial_diff - radial_diff - (radial - source) / radius - turn_diff / (radius * dtheta)


def cycle_filter(conserved):
    cycles = conserved[..., :NRING]
    spectrum = jnp.fft.rfft(cycles, axis=2)
    modes = jnp.arange(NT // 2 + 1, dtype=jnp.int32)[:, None]
    kept = modes <= KEEP * (jnp.arange(NRING, dtype=jnp.int32)[None, :] + 1)
    smooth = jnp.fft.irfft(spectrum * kept, n=NT, axis=2)
    return jnp.concatenate([smooth.astype(conserved.dtype), conserved[..., NRING:]], axis=3)


def section_rate(conserved, flags):
    signs = jnp.array([1.0, 1.0, -1.0, -1.0, 1.0], dtype=conserved.dtype)[:, None, None]
    padded = jnp.concatenate([conserved, flags.astype(conserved.dtype)[None]], axis=0)
    padded = jnp.pad(padded, ((0, 0), (0, 0), (3, 3), (0, 0)), mode="wrap")
    padded = jnp.pad(padded, ((0, 0), (3, 3), (0, 0), (0, 0)), mode="edge")
    ghost = jnp.roll(conserved[:, :, :, 0], NT // 2, axis=2) * signs

    def one_row(row):
        block = lax.dynamic_slice_in_dim(padded, row, 7, axis=1)
        ghost_row = lax.dynamic_slice_in_dim(ghost, row, 1, axis=1)
        return tendency(block, ghost_row, 2.0 * math.pi / NT)

    rates = lax.map(one_row, jnp.arange(NA, dtype=jnp.int32))
    return jnp.transpose(rates[:, :, 0], (1, 0, 2, 3))


def reference(state, shock_flags):
    first = cycle_filter(state + time_step * section_rate(state, shock_flags[0]))
    second = cycle_filter(0.75 * state + 0.25 * (first + time_step * section_rate(first, shock_flags[1])))
    return second - state
```

```python
import math

import jax
import jax.numpy as jnp
import numpy as np
from jax import lax
from jax.experimental import pallas as pl
from jax.experimental.pallas import tpu as pltpu
from jax.sharding import PartitionSpec as P

NRING = 16
KEEP = 32


split_speed = 3.0
small_eps = 1e-06
time_step = 0.004


def with_halo(shard, sides, width):
    for axis, dim in sides:
        devices, length = (lax.axis_size(axis), shard.shape[dim])
        up = [(i, (i + 1) % devices) for i in range(devices)]
        down = [(j, i) for i, j in up]
        last = lax.slice_in_dim(shard, length - width, length, axis=dim)
        leading = lax.slice_in_dim(shard, 0, width, axis=dim)
        before = lax.ppermute(last, axis, up)
        after = lax.ppermute(leading, axis, down)
        shard = jnp.concatenate([before, shard, after], axis=dim)
    return shard


def passed_along(shard, axis, by):
    devices = lax.axis_size(axis)
    return lax.ppermute(shard, axis, [(i, (i + by) % devices) for i in range(devices)])


def pressure_of(conserved):
    return 0.4 * (
        conserved[4]
        - 0.5
        * (conserved[1] * conserved[1] + conserved[2] * conserved[2] + conserved[3] * conserved[3])
        / conserved[0]
    )


def euler_flux(conserved, component):
    velocity = conserved[1 + component] / conserved[0]
    pressure = pressure_of(conserved)
    parts = [
        conserved[0] * velocity,
        conserved[1] * velocity,
        conserved[2] * velocity,
        conserved[3] * velocity,
        (conserved[4] + pressure) * velocity,
    ]
    parts[1 + component] = parts[1 + component] + pressure
    return jnp.stack(parts)


def weno_side(far_left, left, centre, right, far_right):
    cand_zero = (2.0 * far_left - 7.0 * left + 11.0 * centre) / 6.0
    cand_one = (-left + 5.0 * centre + 2.0 * right) / 6.0
    cand_two = (2.0 * centre + 5.0 * right - far_right) / 6.0
    smooth_zero = (
        13.0 / 12.0 * (far_left - 2.0 * left + centre) ** 2
        + 0.25 * (far_left - 4.0 * left + 3.0 * centre) ** 2
    )
    smooth_one = 13.0 / 12.0 * (left - 2.0 * centre + right) ** 2 + 0.25 * (left - right) ** 2
    smooth_two = (
        13.0 / 12.0 * (centre - 2.0 * right + far_right) ** 2
        + 0.25 * (3.0 * centre - 4.0 * right + far_right) ** 2
    )
    weight_zero = 0.1 / (small_eps + smooth_zero) ** 2
    weight_one = 0.6 / (small_eps + smooth_one) ** 2
    weight_two = 0.3 / (small_eps + smooth_two) ** 2
    return (weight_zero * cand_zero + weight_one * cand_one + weight_two * cand_two) / (
        weight_zero + weight_one + weight_two
    )


def face_flux(conserved, flag_field, axis_dim, cell_count, component):
    fluxes = euler_flux(conserved, component)
    plus_part = 0.5 * (fluxes + split_speed * conserved)
    minus_part = 0.5 * (fluxes - split_speed * conserved)

    def take(field, offset, along):
        return lax.slice_in_dim(field, 2 + offset, 3 + offset + cell_count, axis=along)

    plus_face = weno_side(
        take(plus_part, -2, axis_dim),
        take(plus_part, -1, axis_dim),
        take(plus_part, 0, axis_dim),
        take(plus_part, 1, axis_dim),
        take(plus_part, 2, axis_dim),
    )
    minus_face = weno_side(
        take(minus_part, 3, axis_dim),
        take(minus_part, 2, axis_dim),
        take(minus_part, 1, axis_dim),
        take(minus_part, 0, axis_dim),
        take(minus_part, -1, axis_dim),
    )
    central = (
        -take(fluxes, -1, axis_dim)
        + 7.0 * take(fluxes, 0, axis_dim)
        + 7.0 * take(fluxes, 1, axis_dim)
        - take(fluxes, 2, axis_dim)
    ) / 12.0
    switch = take(flag_field, -2, axis_dim - 1)
    for offset in range(-1, 4):
        switch = jnp.maximum(switch, take(flag_field, offset, axis_dim - 1))
    return jnp.where(switch[None] > 0.5, plus_face + minus_face, central)


def tendency(strip_axial, strip_turn, ghost, dtheta):
    axial_n = strip_axial.shape[1] - 6
    turn_n = strip_turn.shape[2] - 6
    axial_faces = face_flux(strip_axial[:5], strip_axial[5], 1, axial_n, 0)
    axial_diff = axial_faces[:, 1:] - axial_faces[:, :-1]
    turn_faces = face_flux(strip_turn[:5], strip_turn[5], 2, turn_n, 2)
    turn_diff = turn_faces[:, :, 1:] - turn_faces[:, :, :-1]
    inner = strip_turn[:5, :, 3 : 3 + turn_n]
    radial = euler_flux(inner, 1)
    radial_ghost = euler_flux(ghost[..., None], 1)
    radial_pad = jnp.concatenate([radial_ghost, radial, radial[..., -1:]], axis=3)
    radial_diff = 0.5 * (radial_pad[..., 2:] - radial_pad[..., :-2])
    swirl = inner[3] / inner[0]
    pressure = pressure_of(inner)
    zeros_field = jnp.zeros_like(pressure)
    source = jnp.stack(
        [zeros_field, zeros_field, inner[3] * swirl + pressure, -inner[2] * swirl, zeros_field]
    )
    radius = jnp.arange(inner.shape[3], dtype=jnp.float32) + 0.5
    return -axial_diff - radial_diff - (radial - source) / radius - turn_diff / (radius * dtheta)


def filter_tables():
    d, k1 = np.arange(64), np.arange(33)
    angle = 2 * np.pi * np.outer(k1, d) / 64
    fwd = np.zeros((80, 64))
    fwd[:33], fwd[40:73] = np.cos(angle), -np.sin(angle)
    inv = np.zeros((64, 80))
    inv[:, :33], inv[:, 40:73] = np.cos(angle.T), -np.sin(angle.T)
    twiddle = np.zeros((4, 40, 256))
    m_in, m_out = np.arange(40), np.arange(-3, 43)
    scale = np.where((k1 == 0) | (k1 == 32), 1.0, 2.0)[:, None] / 2560
    for v in range(5):
        angle = 2 * np.pi * np.outer(k1, m_in) / 2560
        twiddle[0, :33, v * 40 : v * 40 + 40] = np.cos(angle)
        twiddle[1, :33, v * 40 : v * 40 + 40] = -np.sin(angle)
        angle = 2 * np.pi * np.outer(k1, m_out) / 2560
        twiddle[2, :33, v * 46 : v * 46 + 46] = np.cos(angle) * scale
        twiddle[3, :33, v * 46 : v * 46 + 46] = np.sin(angle) * scale
    band = np.zeros((16, 4, 40, 256))
    delta = m_out[None, :] - m_in[:, None]
    for j in range(16):
        if j % 2:
            q = (j + 1) // 2
            modes, extra = np.arange(-q, q), -q
        else:
            q = j // 2
            modes, extra = np.arange(-q, q + 1), q
        kept = sum(np.exp(2j * np.pi * k * delta / 40) for k in modes)
        twin = np.exp(2j * np.pi * extra * delta / 40)
        band[j, 0, :, :46], band[j, 1, :, :46] = kept.real, kept.imag
        band[j, 2, :, :46], band[j, 3, :, :46] = twin.real, twin.imag
    return [a.astype(np.float32) for a in (fwd, inv, twiddle, band)]


def matmul(a, b):
    return jnp.dot(a, b, precision=lax.Precision.HIGHEST, preferred_element_type=jnp.float32)


def spread(send, recv, me, send_sem, recv_sem):
    def one(i, carry):
        to = lax.rem(me + i, 64)
        pltpu.make_async_remote_copy(
            src_ref=send.at[to],
            dst_ref=recv.at[me],
            send_sem=send_sem,
            recv_sem=recv_sem,
            device_id={"az": to},
            device_id_type=pl.DeviceIdType.MESH,
        ).start()
        return carry

    lax.fori_loop(1, 64, one, 0)
    recv[pl.ds(me, 1)] = send[pl.ds(me, 1)]


def arrived(buffer, sem):
    rows = buffer.at[pl.ds(0, 63)]
    pltpu.make_async_copy(rows, rows, sem).wait()


def filter_kernel(
    lines, fwd, inv, twiddle, band, out, send, recv, back, ret, mine, mix, send_sem, recv_sem, sem
):
    me = lax.axis_index("az")
    load = pltpu.make_async_copy(band.at[lax.rem(me, 16)], mine, sem)
    load.start()
    barrier = pltpu.get_barrier_semaphore()

    def greet(i, carry):
        pl.semaphore_signal(
            barrier,
            inc=1,
            device_id={"az": lax.rem(me + i, 64)},
            device_id_type=pl.DeviceIdType.MESH,
        )
        return carry

    lax.fori_loop(1, 64, greet, 0)
    send[:, 0, :] = lines[:, :128]
    send[:, 1, :] = lines[:, 128:]
    pl.semaphore_wait(barrier, 63)
    spread(send, recv, me, send_sem.at[0], recv_sem.at[0])
    load.wait()
    mix[...] = jnp.zeros_like(mix)
    for part in range(2):
        re, im = mine[2 * part], mine[2 * part + 1]
        for v in range(5):
            c = pltpu.roll(re, 46 * v, 1) if v else re
            s = pltpu.roll(im, 46 * v, 1) if v else im
            row = 512 * part + 40 * v
            mix[row : row + 40, :256] = c
            mix[row : row + 40, 256:] = s
            mix[row + 256 : row + 296, :256] = -s
            mix[row + 256 : row + 296, 256:] = c
    arrived(recv, recv_sem.at[0])
    x = jnp.concatenate([recv[:, 0, :], recv[:, 1, :]], axis=1)
    a = matmul(fwd[...], x)
    re, im = a[:40], a[40:]
    re, im = re * twiddle[0] - im * twiddle[1], re * twiddle[1] + im * twiddle[0]
    special = jnp.where(lax.rem(me, 2) == 1, 0, 32)
    own = (lax.broadcasted_iota(jnp.int32, (40, 256), 0) == special).astype(jnp.float32)
    z = matmul(jnp.concatenate([re, im, re * own, im * own], axis=1), mix[...])
    re, im = z[:, :256], z[:, 256:]
    re, im = re * twiddle[2] - im * twiddle[3], re * twiddle[3] + im * twiddle[2]
    y = matmul(inv[...], jnp.concatenate([re, im], axis=0))
    back[:, 0, :] = y[:, :128]
    back[:, 1, :] = y[:, 128:]
    spread(back, ret, me, send_sem.at[1], recv_sem.at[1])
    arrived(ret, recv_sem.at[1])
    out[:, :128] = ret[:, 0, :]
    out[:, 128:] = ret[:, 1, :]
    arrived(send, send_sem.at[0])
    arrived(back, send_sem.at[1])


def cycle_filter(conserved, tables, collective):
    cycles = conserved[..., :NRING]
    lines = jnp.transpose(cycles, (1, 3, 0, 2)).reshape(64, 200)
    lines = jnp.pad(lines, ((0, 0), (0, 56)))
    vmem = pl.BlockSpec(memory_space=pltpu.VMEM)
    message = pltpu.VMEM((64, 2, 128), jnp.float32)
    smooth = pl.pallas_call(
        filter_kernel,
        out_shape=jax.ShapeDtypeStruct((64, 256), jnp.float32),
        in_specs=[vmem] * 4 + [pl.BlockSpec(memory_space=pl.ANY)],
        out_specs=vmem,
        scratch_shapes=[
            message,
            message,
            message,
            message,
            pltpu.VMEM((4, 40, 256), jnp.float32),
            pltpu.VMEM((1024, 512), jnp.float32),
            pltpu.SemaphoreType.DMA((2,)),
            pltpu.SemaphoreType.DMA((2,)),
            pltpu.SemaphoreType.DMA,
        ],
        compiler_params=pltpu.CompilerParams(
            collective_id=collective, has_side_effects=True, vmem_limit_bytes=48 * 1024 * 1024
        ),
    )(lines, *tables)
    smooth = smooth[:, :230].reshape(4, NRING, 5, 46)[..., 3:43]
    smooth_cycles = jnp.transpose(smooth, (2, 0, 3, 1))
    return jnp.concatenate([smooth_cycles, conserved[..., NRING:]], axis=3)


def section_rate(conserved, flags):
    turn_n = conserved.shape[2]
    signs = jnp.array([1.0, 1.0, -1.0, -1.0, 1.0], dtype=jnp.float32)[:, None, None]
    stacked = jnp.concatenate([conserved, flags.astype(jnp.float32)[None]], axis=0)
    padded = with_halo(stacked, (("ax", 1), ("az", 2)), 3)
    strip_axial = padded[:, :, 3 : 3 + turn_n]
    strip_turn = padded[:, 3:-3]
    device_row = lax.axis_index("ax")
    last_row = lax.axis_size("ax") - 1
    lower_rim = jnp.broadcast_to(
        strip_axial[:, 3:4], (strip_axial.shape[0], 3) + strip_axial.shape[2:]
    )
    upper_rim = jnp.broadcast_to(
        strip_axial[:, -4:-3], (strip_axial.shape[0], 3) + strip_axial.shape[2:]
    )
    strip_axial = jnp.concatenate(
        [
            jnp.where(device_row == 0, lower_rim, strip_axial[:, :3]),
            strip_axial[:, 3:-3],
            jnp.where(device_row == last_row, upper_rim, strip_axial[:, -3:]),
        ],
        axis=1,
    )
    ghost = passed_along(conserved[:, :, :, 0] * signs, "az", lax.axis_size("az") // 2)
    return tendency(strip_axial, strip_turn, ghost, 2.0 * math.pi / (turn_n * lax.axis_size("az")))


def local(state, shock_flags):
    tables = [jnp.asarray(t) for t in filter_tables()]
    first = cycle_filter(state + time_step * section_rate(state, shock_flags[0]), tables, 0)
    second = cycle_filter(
        0.75 * state + 0.25 * (first + time_step * section_rate(first, shock_flags[1])), tables, 1
    )
    return second - state


def solution(mesh):
    in_specs = (P(None, "ax", "az", None), P(None, "ax", "az", None))
    out_specs = P(None, "ax", "az", None)
    return jax.shard_map(local, mesh=mesh, in_specs=in_specs, out_specs=out_specs, check_vma=False)
```

```python
import math

import jax
import jax.numpy as jnp
import numpy as np
from jax import lax
from jax.experimental import pallas as pl
from jax.experimental.pallas import tpu as pltpu
from jax.sharding import PartitionSpec as P

NRING = 16
MESH = pl.DeviceIdType.MESH

split_speed = 3.0
small_eps = 1e-06
time_step = 0.004


def filter_tables():
    d, k1 = np.arange(64), np.arange(33)
    angle = 2 * np.pi * np.outer(k1, d) / 64
    fwd = np.zeros((80, 64))
    fwd[:33], fwd[40:73] = np.cos(angle), -np.sin(angle)
    inv = np.zeros((64, 80))
    inv[:, :33], inv[:, 40:73] = np.cos(angle.T), -np.sin(angle.T)
    twiddle = np.zeros((4, 40, 256))
    m_in, m_out = np.arange(40), np.arange(-3, 43)
    scale = np.where((k1 == 0) | (k1 == 32), 1.0, 2.0)[:, None] / 2560
    for v in range(5):
        angle = 2 * np.pi * np.outer(k1, m_in) / 2560
        twiddle[0, :33, v * 40 : v * 40 + 40] = np.cos(angle)
        twiddle[1, :33, v * 40 : v * 40 + 40] = -np.sin(angle)
        angle = 2 * np.pi * np.outer(k1, m_out) / 2560
        twiddle[2, :33, v * 48 : v * 48 + 46] = np.cos(angle) * scale
        twiddle[3, :33, v * 48 : v * 48 + 46] = np.sin(angle) * scale
    band = np.zeros((16, 4, 40, 256))
    delta = m_out[None, :] - m_in[:, None]
    for j in range(16):
        if j % 2:
            q = (j + 1) // 2
            modes, extra = np.arange(-q, q), -q
        else:
            q = j // 2
            modes, extra = np.arange(-q, q + 1), q
        kept = sum(np.exp(2j * np.pi * k * delta / 40) for k in modes)
        twin = np.exp(2j * np.pi * extra * delta / 40)
        band[j, 0, :, :46], band[j, 1, :, :46] = kept.real, kept.imag
        band[j, 2, :, :46], band[j, 3, :, :46] = twin.real, twin.imag
    return [a.astype(np.float32) for a in (fwd, inv, twiddle, band)]


def matmul(a, b):
    return jnp.dot(a, b, precision=lax.Precision.HIGHEST, preferred_element_type=jnp.float32)


def inverse(x):
    return pltpu.reciprocal(x, approx=True)


class Rows:
    def __init__(self, cells):
        self.cells = list(cells)

    def _with(self, other, op):
        if isinstance(other, Rows):
            pairs = zip(self.cells, other.cells)
            return Rows([None if a is None or b is None else op(a, b) for a, b in pairs])
        return Rows([None if a is None else op(a, other) for a in self.cells])

    def __add__(self, other):
        return self._with(other, lambda a, b: a + b)

    def __sub__(self, other):
        return self._with(other, lambda a, b: a - b)

    def __mul__(self, other):
        return self._with(other, lambda a, b: a * b)

    def map(self, op):
        return Rows([None if a is None else op(a) for a in self.cells])

    def shifted(self, by):
        n = len(self.cells)
        return Rows([self.cells[k + by] if 0 <= k + by < n else None for k in range(n)])


def at(x, by):
    if isinstance(x, Rows):
        return x.shifted(by)
    n = x.shape[0]
    return pltpu.roll(x, (n - by) % n, 0)


def inverse_of(x):
    return x.map(inverse) if isinstance(x, Rows) else inverse(x)


def indicators(f):
    d = at(f, 1) - f
    s = d - at(d, -1)
    s_next = at(s, 1)
    e = s - s_next
    h = s * 0.5
    q = s * s * (13.0 / 12.0) + small_eps
    mid = d - h
    up = d + h
    down = mid - s
    x = inverse_of(q + up * up)
    y = inverse_of(q + mid * mid)
    z = inverse_of(q + down * down)
    return d, s, s_next, e, x * x, y * y, z * z


def faces(flux, state, switch, choose):
    half = flux * 0.5
    lift = state * (0.5 * split_speed)
    d_p, s_p, sn_p, e_p, x_p, y_p, z_p = indicators(half + lift)
    zn_p = at(z_p, 1)
    top = at(x_p * e_p, -1) * 2.0 + zn_p * e_p * 3.0
    total = at(x_p, -1) + y_p * 6.0 + zn_p * 3.0
    plus = top * inverse_of(total)
    d_m, s_m, sn_m, e_m, x_m, y_m, z_m = indicators(half - lift)
    zn_m = at(z_m, 1)
    top = at(zn_m * e_m, 1) * 2.0 + x_m * e_m * 3.0
    total = at(zn_m, 1) + at(y_m, 1) * 6.0 + x_m * 3.0
    minus = top * inverse_of(total)
    middle = flux + (d_p + d_m) * 0.5
    own = s_p + sn_m
    weno = (plus - minus - own) * (1.0 / 6.0)
    central = (own + s_m + sn_p) * (-1.0 / 12.0)
    return middle + choose(switch, weno, central)


def pick(switch, a, b):
    if isinstance(a, Rows):
        triples = zip(switch.cells, a.cells, b.cells)
        return Rows([None if s is None or p is None or q is None else jnp.where(s, p, q) for s, p, q in triples])
    return jnp.where(switch, a, b)


def largest(a, b):
    if isinstance(a, Rows):
        return a._with(b, jnp.maximum)
    return jnp.maximum(a, b)


def window(flags):
    pair = largest(flags, at(flags, 1))
    four = largest(pair, at(pair, 2))
    six = at(largest(four, at(pair, 4)), -2)
    return six.map(lambda a: a > 0.5) if isinstance(six, Rows) else six > 0.5


def fluxes(u, q, p, component):
    parts = [u[1 + component], u[1] * q, u[2] * q, u[3] * q, (u[4] + p) * q]
    parts[1 + component] = parts[1 + component] + p
    return parts


def pressure(u, inv_rho):
    return (u[4] - (u[1] * u[1] + u[2] * u[2] + u[3] * u[3]) * inv_rho * 0.5) * 0.4


def lanes(shape):
    return lax.broadcasted_iota(jnp.int32, shape, len(shape) - 1)


def radius(rows):
    return lanes((rows, 128)).astype(jnp.float32) + 0.5


def azimuthal(padded, flags, section, rate):
    scale = -1.0 / (radius(40) * (2.0 * math.pi / 2560))

    def row(r, carry):
        u = [padded[v, r] for v in range(5)]
        inv_rho = inverse(u[0])
        q = u[3] * inv_rho
        f = fluxes(u, q, pressure(u, inv_rho), 2)
        switch = window(flags[section, r])
        for v in range(5):
            face = faces(f[v], u[v], switch, pick)
            rate[v, r] = (at(face, 3)[:40] - at(face, 2)[:40]) * scale
        return carry

    lax.fori_loop(0, 4, row, 0)


def finish(own, low, high, flags, flags_low, flags_high, section, ghost, rate, combine):
    inv_r = 1.0 / radius(8)
    lane = lanes((8, 128))
    signs = [1.0, 1.0, -1.0, -1.0, 1.0]

    def chunk(c, carry):
        at8 = pl.ds(pl.multiple_of(c * 8, 8), 8)
        u = [
            Rows(
                [low[v, k, at8, :] for k in range(3)]
                + [own[v, k, at8, :] for k in range(4)]
                + [high[v, k, at8, :] for k in range(3)]
            )
            for v in range(5)
        ]
        marks = Rows(
            [flags_low[section, k, at8, :] for k in range(3)]
            + [flags[section, k, at8, :] for k in range(4)]
            + [flags_high[section, k, at8, :] for k in range(3)]
        ).map(lambda a: a.astype(jnp.float32))
        switch = window(marks)
        inv_rho = u[0].map(inverse)
        p = pressure(u, inv_rho)
        f = fluxes(u, u[1] * inv_rho, p, 0)
        columns = ghost[at8, :]
        radial, source = [], []
        for r in range(4):
            here = [u[v].cells[3 + r] for v in range(5)]
            there = [pltpu.roll(columns, (128 - (v * 4 + r)) % 128, 1) * signs[v] for v in range(5)]
            there[0] = jnp.where(lane == 0, there[0], 1.0)
            there_inv = inverse(there[0])
            g_ghost = fluxes(there, there[2] * there_inv, pressure(there, there_inv), 1)
            inv_here, p_here = inv_rho.cells[3 + r], p.cells[3 + r]
            g = fluxes(here, here[2] * inv_here, p_here, 1)
            swirl = here[3] * inv_here
            extra = [None, None, here[3] * swirl + p_here, -here[2] * swirl, None]
            terms = []
            for v in range(5):
                before = jnp.where(lane == 0, g_ghost[v], pltpu.roll(g[v], 1, 1))
                after = jnp.where(lane == 127, g[v], pltpu.roll(g[v], 127, 1))
                away = g[v] if extra[v] is None else g[v] - extra[v]
                terms.append((after - before) * 0.5 + away * inv_r)
            radial.append(terms)
        for v in range(5):
            face = faces(f[v], u[v], switch, pick).cells
            for r in range(4):
                slope = rate[v, r, at8, :] - (face[3 + r] - face[2 + r]) - radial[r][v]
                combine(v, r, at8, u[v].cells[3 + r], slope)
        return carry

    lax.fori_loop(0, 5, chunk, 0)


def ghost_columns(field, staging):
    lane = lanes((40, 128))
    packed = jnp.zeros((40, 128), jnp.float32)
    for v in range(5):
        for r in range(4):
            k = v * 4 + r
            value = field[v, r]
            packed = jnp.where(lane == k, pltpu.roll(value, k, 1) if k else value, packed)
    staging[...] = packed


def to_lines(field, send):
    for r in range(4):
        stack = [field[v, r] for v in range(5)] + [jnp.zeros((56, 128), jnp.float32)]
        turned = jnp.transpose(jnp.concatenate(stack, axis=0))[:16]
        send[16 * r : 16 * r + 16, 0, :] = turned[:, :128]
        send[16 * r : 16 * r + 16, 1, :] = turned[:, 128:]


def from_lines(ret, first):
    lines = jnp.concatenate([ret[first : first + 16, 0, :], ret[first : first + 16, 1, :]], axis=1)
    lines = jnp.concatenate([lines, jnp.zeros((112, 256), jnp.float32)], axis=0)
    turned = jnp.transpose(lines)
    return [turned[48 * v : 48 * v + 48] for v in range(5)]


def spread(send, recv, me, send_sem, recv_sem):
    def one(i, carry):
        to = lax.rem(me + i, 64)
        pltpu.make_async_remote_copy(
            src_ref=send.at[to],
            dst_ref=recv.at[me],
            send_sem=send_sem,
            recv_sem=recv_sem,
            device_id={"az": to},
            device_id_type=MESH,
        ).start()
        return carry

    lax.fori_loop(1, 64, one, 0)
    recv[pl.ds(me, 1)] = send[pl.ds(me, 1)]


def arrived(buffer, sem):
    rows = buffer.at[pl.ds(0, 63)]
    pltpu.make_async_copy(rows, rows, sem).wait()


def build_mix(mine, mix):
    mix[...] = jnp.zeros_like(mix)
    for part in range(2):
        re, im = mine[2 * part], mine[2 * part + 1]
        for v in range(5):
            c = pltpu.roll(re, 48 * v, 1) if v else re
            s = pltpu.roll(im, 48 * v, 1) if v else im
            row = 512 * part + 40 * v
            mix[row : row + 40, :256] = c
            mix[row : row + 40, 256:] = s
            mix[row + 256 : row + 296, :256] = -s
            mix[row + 256 : row + 296, 256:] = c


def project(recv, back, me, fwd, inv, twiddle, mix):
    x = jnp.concatenate([recv[:, 0, :], recv[:, 1, :]], axis=1)
    a = matmul(fwd[...], x)
    re, im = a[:40], a[40:]
    re, im = re * twiddle[0] - im * twiddle[1], re * twiddle[1] + im * twiddle[0]
    special = jnp.where(lax.rem(me, 2) == 1, 0, 32)
    own = (lax.broadcasted_iota(jnp.int32, (40, 256), 0) == special).astype(jnp.float32)
    z = matmul(jnp.concatenate([re, im, re * own, im * own], axis=1), mix[...])
    re, im = z[:, :256], z[:, 256:]
    re, im = re * twiddle[2] - im * twiddle[3], re * twiddle[3] + im * twiddle[2]
    y = matmul(inv[...], jnp.concatenate([re, im], axis=0))
    back[:, 0, :] = y[:, :128]
    back[:, 1, :] = y[:, 128:]


def kernel(
    state, flags, fwd, inv, twiddle, band, out,
    mine, mix, padded, padded_flags, rate, first, second,
    az_out, az_in, azf_out, azf_in, low, high, flow, fhigh, ghost_out, ghost_in, near_low, near_high,
    send, recv, back, ret,
    sem, az_sem, azf_sem, ax_sem, axf_sem, ghost_sem, near_sem, go_sem, come_sem,
):
    me, row = lax.axis_index("az"), lax.axis_index("ax")
    right, left = lax.rem(me + 1, 64), lax.rem(me + 63, 64)
    load = pltpu.make_async_copy(band.at[lax.rem(me, 16)], mine, sem)
    load.start()
    barrier = pltpu.get_barrier_semaphore()

    def greet(i, carry):
        peer = lax.rem(me + i, 64)
        pl.semaphore_signal(barrier, inc=1, device_id={"az": peer}, device_id_type=MESH)
        return carry

    lax.fori_loop(1, 64, greet, 0)
    for by in (1, 3):
        peer = lax.rem(row + by, 4)
        pl.semaphore_signal(barrier, inc=1, device_id={"ax": peer}, device_id_type=MESH)

    def copy(src, dst, sems, k, **place):
        return pltpu.make_async_remote_copy(
            src_ref=src,
            dst_ref=dst,
            send_sem=sems.at[0, k],
            recv_sem=sems.at[1, k],
            device_id=place,
            device_id_type=MESH,
        )

    def az_copies(section):
        return [
            copy(az_out.at[0], az_in.at[section, 0], az_sem.at[section], 0, az=right),
            copy(az_out.at[1], az_in.at[section, 1], az_sem.at[section], 1, az=left),
        ]

    def ax_copies(field, to_low, to_high, sems):
        up = copy(field.at[:, pl.ds(1, 3)], to_low, sems, 0, ax=lax.rem(row + 1, 4))
        down = copy(field.at[:, pl.ds(0, 3)], to_high, sems, 1, ax=lax.rem(row + 3, 4))
        return up, down

    def stage(field, staging, fields):
        for f in range(fields):
            for r in range(4):
                staging[0, f * 4 + r, 0:3] = field[f, r, 37:40]
                staging[1, f * 4 + r, 0:3] = field[f, r, 0:3]

    def when_up(action):
        pl.when(row < 3)(action)

    def when_down(action):
        pl.when(row > 0)(action)

    def start_ax(pair):
        when_up(pair[0].start)
        when_down(pair[1].start)

    def sent_ax(pair):
        when_up(pair[0].wait_send)
        when_down(pair[1].wait_send)

    def came_ax(pair):
        when_down(pair[0].wait_recv)
        when_up(pair[1].wait_recv)

    stage(state, az_out, 5)
    stage(flags, azf_out, 2)
    ghost_columns(state, ghost_out)
    az = az_copies(0)
    azf = [
        copy(azf_out.at[0], azf_in.at[0], azf_sem, 0, az=right),
        copy(azf_out.at[1], azf_in.at[1], azf_sem, 1, az=left),
    ]
    opposite = lax.rem(me + 32, 64)
    ghost = copy(ghost_out, ghost_in.at[0], ghost_sem.at[0], 0, az=opposite)
    ax = ax_copies(state, low.at[0], high.at[0], ax_sem.at[0])
    axf = ax_copies(flags, flow, fhigh, axf_sem)
    pl.semaphore_wait(barrier, 65)
    for item in az + azf:
        item.start()
    start_ax(ax)
    start_ax(axf)
    ghost.start()
    load.wait()
    build_mix(mine, mix)
    padded[...] = jnp.zeros_like(padded)
    padded_flags[...] = jnp.zeros_like(padded_flags)
    for v in range(5):
        for r in range(4):
            padded[v, r, 3:43] = state[v, r]
    for s in range(2):
        for r in range(4):
            padded_flags[s, r, 3:43] = flags[s, r].astype(jnp.float32)

    def fill_az(section):
        for v in range(5):
            for r in range(4):
                padded[v, r, 0:3] = az_in[section, 0, v * 4 + r, 0:3]
                padded[v, r, 43:46] = az_in[section, 1, v * 4 + r, 0:3]

    for item in az + azf:
        item.wait_send()
        item.wait_recv()
    fill_az(0)
    for s in range(2):
        for r in range(4):
            padded_flags[s, r, 0:3] = azf_in[0, s * 4 + r, 0:3].astype(jnp.float32)
            padded_flags[s, r, 43:46] = azf_in[1, s * 4 + r, 0:3].astype(jnp.float32)
    azimuthal(padded, padded_flags, 0, rate)
    came_ax(ax)
    came_ax(axf)

    def rims(field, section):
        def low_rim():
            for v in range(5):
                for k in range(3):
                    low[section, v, k] = field[v, 0]

        def high_rim():
            for v in range(5):
                for k in range(3):
                    high[section, v, k] = field[v, 3]

        pl.when(row == 0)(low_rim)
        pl.when(row == 3)(high_rim)

    def flag_low_rim():
        for s in range(2):
            for k in range(3):
                flow[s, k] = flags[s, 0]

    def flag_high_rim():
        for s in range(2):
            for k in range(3):
                fhigh[s, k] = flags[s, 3]

    rims(state, 0)
    pl.when(row == 0)(flag_low_rim)
    pl.when(row == 3)(flag_high_rim)
    ghost.wait_send()
    ghost.wait_recv()

    def combine_first(v, r, rows, here, slope):
        first[v, r, rows, :] = here + slope * time_step

    finish(state, low.at[0], high.at[0], flags, flow, fhigh, 0, ghost_in.at[0], rate, combine_first)
    sent_ax(ax)
    sent_ax(axf)

    to_lines(first, send.at[0])
    spread(send.at[0], recv.at[0], me, go_sem.at[0, 0], go_sem.at[0, 1])
    stage(first, az_out, 5)
    az = az_copies(1)
    for item in az:
        item.start()
    ax = ax_copies(first, low.at[1], high.at[1], ax_sem.at[1])
    start_ax(ax)
    for v in range(5):
        for r in range(4):
            padded[v, r, 3:43] = first[v, r]
    arrived(recv.at[0], go_sem.at[0, 1])
    project(recv.at[0], back.at[0], me, fwd, inv, twiddle, mix)
    spread(back.at[0], ret.at[0], me, come_sem.at[0, 0], come_sem.at[0, 1])
    for item in az:
        item.wait_send()
        item.wait_recv()
    fill_az(1)
    sent_ax(ax)
    came_ax(ax)
    arrived(ret.at[0], come_sem.at[0, 1])

    near = (
        copy(ret.at[0, pl.ds(16, 48)], near_low, near_sem, 0, ax=lax.rem(row + 1, 4)),
        copy(ret.at[0, pl.ds(0, 48)], near_high, near_sem, 1, ax=lax.rem(row + 3, 4)),
    )
    start_ax(near)
    inner48, inner40 = lanes((48, 128)) < NRING, lanes((40, 128)) < NRING
    for r in range(4):
        blocks = from_lines(ret.at[0], 16 * r)
        for v in range(5):
            merged = jnp.where(inner48, blocks[v], padded[v, r])
            padded[v, r] = merged
            first[v, r] = merged[3:43]
    ghost_columns(first, ghost_out)
    ghost = copy(ghost_out, ghost_in.at[1], ghost_sem.at[1], 0, az=opposite)
    ghost.start()
    azimuthal(padded, padded_flags, 1, rate)
    came_ax(near)

    def merge_low():
        for k in range(3):
            blocks = from_lines(near_low, 16 * k)
            for v in range(5):
                low[1, v, k] = jnp.where(inner40, blocks[v][3:43], low[1, v, k])

    def merge_high():
        for k in range(3):
            blocks = from_lines(near_high, 16 * k)
            for v in range(5):
                high[1, v, k] = jnp.where(inner40, blocks[v][3:43], high[1, v, k])

    when_down(merge_low)
    when_up(merge_high)
    rims(first, 1)
    ghost.wait_send()
    ghost.wait_recv()

    def combine_second(v, r, rows, here, slope):
        second[v, r, rows, :] = state[v, r, rows, :] * 0.75 + (here + slope * time_step) * 0.25

    finish(first, low.at[1], high.at[1], flags, flow, fhigh, 1, ghost_in.at[1], rate, combine_second)
    sent_ax(near)

    to_lines(second, send.at[1])
    spread(send.at[1], recv.at[1], me, go_sem.at[1, 0], go_sem.at[1, 1])
    arrived(recv.at[1], go_sem.at[1, 1])
    project(recv.at[1], back.at[1], me, fwd, inv, twiddle, mix)
    spread(back.at[1], ret.at[1], me, come_sem.at[1, 0], come_sem.at[1, 1])
    arrived(ret.at[1], come_sem.at[1, 1])
    for r in range(4):
        blocks = from_lines(ret.at[1], 16 * r)
        for v in range(5):
            out[v, r] = jnp.where(inner40, blocks[v][3:43], second[v, r]) - state[v, r]
    for section in range(2):
        arrived(send.at[section], go_sem.at[section, 0])
        arrived(back.at[section], come_sem.at[section, 0])


def local(state, shock_flags):
    tables = [jnp.asarray(t) for t in filter_tables()]
    vmem = pl.BlockSpec(memory_space=pltpu.VMEM)
    f32, i32 = jnp.float32, jnp.int32
    dma = pltpu.SemaphoreType.DMA
    return pl.pallas_call(
        kernel,
        out_shape=jax.ShapeDtypeStruct(state.shape, f32),
        in_specs=[vmem] * 5 + [pl.BlockSpec(memory_space=pl.ANY)],
        out_specs=vmem,
        scratch_shapes=[
            pltpu.VMEM((4, 40, 256), f32),
            pltpu.VMEM((1024, 512), f32),
            pltpu.VMEM((5, 4, 48, 128), f32),
            pltpu.VMEM((2, 4, 48, 128), f32),
            pltpu.VMEM((5, 4, 40, 128), f32),
            pltpu.VMEM((5, 4, 40, 128), f32),
            pltpu.VMEM((5, 4, 40, 128), f32),
            pltpu.VMEM((2, 20, 4, 128), f32),
            pltpu.VMEM((2, 2, 20, 4, 128), f32),
            pltpu.VMEM((2, 8, 4, 128), i32),
            pltpu.VMEM((2, 8, 4, 128), i32),
            pltpu.VMEM((2, 5, 3, 40, 128), f32),
            pltpu.VMEM((2, 5, 3, 40, 128), f32),
            pltpu.VMEM((2, 3, 40, 128), i32),
            pltpu.VMEM((2, 3, 40, 128), i32),
            pltpu.VMEM((40, 128), f32),
            pltpu.VMEM((2, 40, 128), f32),
            pltpu.VMEM((48, 2, 128), f32),
            pltpu.VMEM((48, 2, 128), f32),
            pltpu.VMEM((2, 64, 2, 128), f32),
            pltpu.VMEM((2, 64, 2, 128), f32),
            pltpu.VMEM((2, 64, 2, 128), f32),
            pltpu.VMEM((2, 64, 2, 128), f32),
            dma,
            dma((2, 2, 2)),
            dma((2, 2)),
            dma((2, 2, 2)),
            dma((2, 2)),
            dma((2, 2, 1)),
            dma((2, 2)),
            dma((2, 2)),
            dma((2, 2)),
        ],
        compiler_params=pltpu.CompilerParams(
            collective_id=0, has_side_effects=True, vmem_limit_bytes=48 * 1024 * 1024
        ),
    )(state, shock_flags, *tables)


def solution(mesh):
    in_specs = (P(None, "ax", "az", None), P(None, "ax", "az", None))
    out_specs = P(None, "ax", "az", None)
    return jax.shard_map(local, mesh=mesh, in_specs=in_specs, out_specs=out_specs, check_vma=False)
```

```python
import math

import jax
import jax.numpy as jnp
import numpy as np
from jax import lax
from jax.experimental import pallas as pl
from jax.experimental.pallas import tpu as pltpu
from jax.sharding import PartitionSpec as P

NRING = 16
MESH = pl.DeviceIdType.MESH

split_speed = 3.0
small_eps = 1e-06
time_step = 0.004


def filter_tables():
    d, k1 = np.arange(64), np.arange(33)
    angle = 2 * np.pi * np.outer(k1, d) / 64
    fwd = np.zeros((80, 64))
    fwd[:33], fwd[40:73] = np.cos(angle), -np.sin(angle)
    inv = np.zeros((64, 80))
    inv[:, :33], inv[:, 40:73] = np.cos(angle.T), -np.sin(angle.T)
    twiddle = np.zeros((4, 40, 256))
    m_in, m_out = np.arange(40), np.arange(-3, 43)
    scale = np.where((k1 == 0) | (k1 == 32), 1.0, 2.0)[:, None] / 2560
    for v in range(5):
        angle = 2 * np.pi * np.outer(k1, m_in) / 2560
        twiddle[0, :33, v * 40 : v * 40 + 40] = np.cos(angle)
        twiddle[1, :33, v * 40 : v * 40 + 40] = -np.sin(angle)
        angle = 2 * np.pi * np.outer(k1, m_out) / 2560
        twiddle[2, :33, v * 48 : v * 48 + 46] = np.cos(angle) * scale
        twiddle[3, :33, v * 48 : v * 48 + 46] = np.sin(angle) * scale
    band = np.zeros((16, 4, 40, 256))
    delta = m_out[None, :] - m_in[:, None]
    for j in range(16):
        if j % 2:
            q = (j + 1) // 2
            modes, extra = np.arange(-q, q), -q
        else:
            q = j // 2
            modes, extra = np.arange(-q, q + 1), q
        kept = sum(np.exp(2j * np.pi * k * delta / 40) for k in modes)
        twin = np.exp(2j * np.pi * extra * delta / 40)
        band[j, 0, :, :46], band[j, 1, :, :46] = kept.real, kept.imag
        band[j, 2, :, :46], band[j, 3, :, :46] = twin.real, twin.imag
    return [a.astype(np.float32) for a in (fwd, inv, twiddle, band)]


def split(x):
    high = x.astype(jnp.bfloat16)
    return high, (x - high.astype(jnp.float32)).astype(jnp.bfloat16)


def dot(a, b):
    return jnp.dot(a, b, preferred_element_type=jnp.float32)


def by_left(a_high, a_low, b):
    high, low = split(b)
    return dot(a_high, high) + (dot(a_high, low) + dot(a_low, high))


def by_right(a, b_high, b_low):
    high, low = split(a)
    rows = a.shape[0]
    both = dot(jnp.concatenate([high, low], axis=0), b_high)
    return both[:rows] + (both[rows:] + dot(high, b_low))


def inverse(x):
    return pltpu.reciprocal(x, approx=True)


class Rows:
    def __init__(self, cells):
        self.cells = list(cells)

    def _with(self, other, op):
        if isinstance(other, Rows):
            pairs = zip(self.cells, other.cells)
            return Rows([None if a is None or b is None else op(a, b) for a, b in pairs])
        return Rows([None if a is None else op(a, other) for a in self.cells])

    def __add__(self, other):
        return self._with(other, lambda a, b: a + b)

    def __sub__(self, other):
        return self._with(other, lambda a, b: a - b)

    def __mul__(self, other):
        return self._with(other, lambda a, b: a * b)

    def map(self, op):
        return Rows([None if a is None else op(a) for a in self.cells])

    def shifted(self, by):
        n = len(self.cells)
        return Rows([self.cells[k + by] if 0 <= k + by < n else None for k in range(n)])


def at(x, by):
    if isinstance(x, Rows):
        return x.shifted(by)
    n = x.shape[0]
    return pltpu.roll(x, (n - by) % n, 0)


def inverse_of(x):
    return x.map(inverse) if isinstance(x, Rows) else inverse(x)


def indicators(f):
    d = at(f, 1) - f
    s = d - at(d, -1)
    s_next = at(s, 1)
    e = s - s_next
    h = s * 0.5
    q = s * s * (13.0 / 12.0) + small_eps
    mid = d - h
    up = d + h
    down = mid - s
    x = inverse_of(q + up * up)
    y = inverse_of(q + mid * mid)
    z = inverse_of(q + down * down)
    return d, s, s_next, e, x * x, y * y, z * z


def faces(flux, state, switch, choose):
    half = flux * 0.5
    lift = state * (0.5 * split_speed)
    d_p, s_p, sn_p, e_p, x_p, y_p, z_p = indicators(half + lift)
    zn_p = at(z_p, 1)
    top = at(x_p * e_p, -1) * 2.0 + zn_p * e_p * 3.0
    total = at(x_p, -1) + y_p * 6.0 + zn_p * 3.0
    plus = top * inverse_of(total)
    d_m, s_m, sn_m, e_m, x_m, y_m, z_m = indicators(half - lift)
    zn_m = at(z_m, 1)
    top = at(zn_m * e_m, 1) * 2.0 + x_m * e_m * 3.0
    total = at(zn_m, 1) + at(y_m, 1) * 6.0 + x_m * 3.0
    minus = top * inverse_of(total)
    middle = flux + (d_p + d_m) * 0.5
    own = s_p + sn_m
    weno = (plus - minus - own) * (1.0 / 6.0)
    central = (own + s_m + sn_p) * (-1.0 / 12.0)
    return middle + choose(switch, weno, central)


def pick(switch, a, b):
    if isinstance(a, Rows):
        triples = zip(switch.cells, a.cells, b.cells)
        return Rows([None if s is None or p is None or q is None else jnp.where(s, p, q) for s, p, q in triples])
    return jnp.where(switch, a, b)


def largest(a, b):
    if isinstance(a, Rows):
        return a._with(b, jnp.maximum)
    return jnp.maximum(a, b)


def window(flags):
    pair = largest(flags, at(flags, 1))
    four = largest(pair, at(pair, 2))
    six = at(largest(four, at(pair, 4)), -2)
    return six.map(lambda a: a > 0.5) if isinstance(six, Rows) else six > 0.5


def fluxes(u, q, p, component):
    parts = [u[1 + component], u[1] * q, u[2] * q, u[3] * q, (u[4] + p) * q]
    parts[1 + component] = parts[1 + component] + p
    return parts


def pressure(u, inv_rho):
    return (u[4] - (u[1] * u[1] + u[2] * u[2] + u[3] * u[3]) * inv_rho * 0.5) * 0.4


def lanes(shape):
    return lax.broadcasted_iota(jnp.int32, shape, len(shape) - 1)


def radius(rows):
    return lanes((rows, 128)).astype(jnp.float32) + 0.5


def azimuthal(padded, flags, section, rate):
    scale = -1.0 / (radius(40) * (2.0 * math.pi / 2560))

    def row(r, carry):
        u = [padded[v, r] for v in range(5)]
        inv_rho = inverse(u[0])
        q = u[3] * inv_rho
        f = fluxes(u, q, pressure(u, inv_rho), 2)
        switch = window(flags[section, r])
        for v in range(5):
            face = faces(f[v], u[v], switch, pick)
            rate[v, r] = (at(face, 3)[:40] - at(face, 2)[:40]) * scale
        return carry

    lax.fori_loop(0, 4, row, 0)


def finish(own, low, high, flags, flags_low, flags_high, section, ghost, rate, combine):
    inv_r = 1.0 / radius(8)
    lane = lanes((8, 128))
    signs = [1.0, 1.0, -1.0, -1.0, 1.0]

    def chunk(c, carry):
        at8 = pl.ds(pl.multiple_of(c * 8, 8), 8)
        u = [
            Rows(
                [low[v, k, at8, :] for k in range(3)]
                + [own[v, k, at8, :] for k in range(4)]
                + [high[v, k, at8, :] for k in range(3)]
            )
            for v in range(5)
        ]
        marks = Rows(
            [flags_low[section, k, at8, :] for k in range(3)]
            + [flags[section, k, at8, :] for k in range(4)]
            + [flags_high[section, k, at8, :] for k in range(3)]
        ).map(lambda a: a.astype(jnp.float32))
        switch = window(marks)
        inv_rho = u[0].map(inverse)
        p = pressure(u, inv_rho)
        f = fluxes(u, u[1] * inv_rho, p, 0)
        columns = ghost[at8, :]
        radial, source = [], []
        for r in range(4):
            here = [u[v].cells[3 + r] for v in range(5)]
            there = [pltpu.roll(columns, (128 - (v * 4 + r)) % 128, 1) * signs[v] for v in range(5)]
            there[0] = jnp.where(lane == 0, there[0], 1.0)
            there_inv = inverse(there[0])
            g_ghost = fluxes(there, there[2] * there_inv, pressure(there, there_inv), 1)
            inv_here, p_here = inv_rho.cells[3 + r], p.cells[3 + r]
            g = fluxes(here, here[2] * inv_here, p_here, 1)
            swirl = here[3] * inv_here
            extra = [None, None, here[3] * swirl + p_here, -here[2] * swirl, None]
            terms = []
            for v in range(5):
                before = jnp.where(lane == 0, g_ghost[v], pltpu.roll(g[v], 1, 1))
                after = jnp.where(lane == 127, g[v], pltpu.roll(g[v], 127, 1))
                away = g[v] if extra[v] is None else g[v] - extra[v]
                terms.append((after - before) * 0.5 + away * inv_r)
            radial.append(terms)
        for v in range(5):
            face = faces(f[v], u[v], switch, pick).cells
            for r in range(4):
                slope = rate[v, r, at8, :] - (face[3 + r] - face[2 + r]) - radial[r][v]
                combine(v, r, at8, u[v].cells[3 + r], slope)
        return carry

    lax.fori_loop(0, 5, chunk, 0)


def ghost_columns(field, staging):
    lane = lanes((40, 128))
    packed = jnp.zeros((40, 128), jnp.float32)
    for v in range(5):
        for r in range(4):
            k = v * 4 + r
            value = field[v, r]
            packed = jnp.where(lane == k, pltpu.roll(value, k, 1) if k else value, packed)
    staging[...] = packed


def to_lines(field, send):
    for r in range(4):
        stack = [field[v, r] for v in range(5)] + [jnp.zeros((56, 128), jnp.float32)]
        turned = jnp.transpose(jnp.concatenate(stack, axis=0))[:16]
        send[16 * r : 16 * r + 16, 0, :] = turned[:, :128]
        send[16 * r : 16 * r + 16, 1, :] = turned[:, 128:]


def from_lines(ret, first):
    lines = jnp.concatenate([ret[first : first + 16, 0, :], ret[first : first + 16, 1, :]], axis=1)
    lines = jnp.concatenate([lines, jnp.zeros((112, 256), jnp.float32)], axis=0)
    turned = jnp.transpose(lines)
    return [turned[48 * v : 48 * v + 48] for v in range(5)]


def others(me):
    y, x, z = me // 32, lax.rem(me // 8, 4), lax.rem(me, 8)
    ys = {d: lax.rem(y + d, 2) * 32 for d in (1, 0)}
    xs = {d: lax.rem(x + d, 4) * 8 for d in (2, 1, 3, 0)}
    zs = {d: lax.rem(z + d, 8) for d in (4, 3, 5, 2, 6, 1, 7, 0)}
    steps = [(dy, dx, dz) for dz in zs for dx in xs for dy in ys]
    steps.sort(key=lambda s: -(s[0] + min(s[1], 4 - s[1]) + min(s[2], 8 - s[2])))
    return [ys[dy] + xs[dx] + zs[dz] for dy, dx, dz in steps[:-1]]


def spread(send, recv, me, peers, send_sem, recv_sem):
    for to in peers:
        pltpu.make_async_remote_copy(
            src_ref=send.at[to],
            dst_ref=recv.at[me],
            send_sem=send_sem,
            recv_sem=recv_sem,
            device_id={"az": to},
            device_id_type=MESH,
        ).start()
    recv[pl.ds(me, 1)] = send[pl.ds(me, 1)]


def arrived(buffer, sem):
    rows = buffer.at[pl.ds(0, 63)]
    pltpu.make_async_copy(rows, rows, sem).wait()


def build_mix(mine, mix_high, mix_low):
    mix_high[...] = jnp.zeros_like(mix_high)
    mix_low[...] = jnp.zeros_like(mix_low)
    for k in range(4):
        rows = []
        for v in range(5):
            rows.append(pltpu.roll(mine[k], 48 * v, 1) if v else mine[k])
        rows.append(jnp.zeros((56, 256), jnp.float32))
        mix_high[k], mix_low[k] = split(jnp.concatenate(rows, axis=0))


def project(recv, back, me, fwd, inv, twiddle, mix_high, mix_low):
    x = jnp.concatenate([recv[:, 0, :], recv[:, 1, :]], axis=1)
    a = by_left(fwd[0], fwd[1], x)
    re, im = a[:40], a[40:]
    re, im = re * twiddle[0] - im * twiddle[1], re * twiddle[1] + im * twiddle[0]
    odd = lax.rem(me, 2) == 1
    first_row = lax.broadcasted_iota(jnp.int32, (8, 256), 0) == 0

    def twin_row(x):
        return jnp.where(first_row, jnp.where(odd, x[:8], x[32:40]), 0.0)

    main = jnp.concatenate([re, im], axis=0)
    twin = jnp.concatenate([twin_row(re), twin_row(im)], axis=0)
    c, s = by_right(main, mix_high[0], mix_low[0]), by_right(main, mix_high[1], mix_low[1])
    tc, ts = by_right(twin, mix_high[2], mix_low[2]), by_right(twin, mix_high[3], mix_low[3])
    re, im = c[:40] - s[40:], s[:40] + c[40:]
    t_re, t_im = tc[:8] - ts[8:], ts[:8] + tc[8:]

    def with_twin(x, t):
        top = x[:8] + jnp.where(odd, t, 0.0)
        return jnp.concatenate([top, x[8:32], x[32:40] + jnp.where(odd, 0.0, t)], axis=0)

    re, im = with_twin(re, t_re), with_twin(im, t_im)
    re, im = re * twiddle[2] - im * twiddle[3], re * twiddle[3] + im * twiddle[2]
    y = by_left(inv[0], inv[1], jnp.concatenate([re, im], axis=0))
    back[:, 0, :] = y[:, :128]
    back[:, 1, :] = y[:, 128:]


def kernel(
    state_hbm, flags_hbm, fwd_hbm, inv_hbm, twiddle_hbm, band, out,
    state, flags, fwd, inv, twiddle, mine, mix_high, mix_low, padded, padded_flags, rate, first, second,
    az_out, az_in, azf_out, azf_in, low, high, flow, fhigh, ghost_out, ghost_in, near_low, near_high,
    send, recv, back, ret,
    sem, az_sem, azf_sem, ax_sem, axf_sem, ghost_sem, near_sem, go_sem, come_sem,
):
    me, row = lax.axis_index("az"), lax.axis_index("ax")
    right, left = lax.rem(me + 1, 64), lax.rem(me + 63, 64)
    pairs = [
        (state_hbm, state),
        (flags_hbm, flags),
        (fwd_hbm, fwd),
        (inv_hbm, inv),
        (twiddle_hbm, twiddle),
        (band.at[lax.rem(me, 16)], mine),
    ]
    loads = [pltpu.make_async_copy(a, b, sem.at[k]) for k, (a, b) in enumerate(pairs)]
    for item in loads:
        item.start()
    barrier = pltpu.get_barrier_semaphore()

    peers = others(me)
    for peer in peers:
        pl.semaphore_signal(barrier, inc=1, device_id={"az": peer}, device_id_type=MESH)
    for by in (1, 3):
        peer = lax.rem(row + by, 4)
        pl.semaphore_signal(barrier, inc=1, device_id={"ax": peer}, device_id_type=MESH)

    def copy(src, dst, sems, k, **place):
        return pltpu.make_async_remote_copy(
            src_ref=src,
            dst_ref=dst,
            send_sem=sems.at[0, k],
            recv_sem=sems.at[1, k],
            device_id=place,
            device_id_type=MESH,
        )

    def az_copies(section):
        return [
            copy(az_out.at[0], az_in.at[section, 0], az_sem.at[section], 0, az=right),
            copy(az_out.at[1], az_in.at[section, 1], az_sem.at[section], 1, az=left),
        ]

    def ax_copies(field, to_low, to_high, sems):
        up = copy(field.at[:, pl.ds(1, 3)], to_low, sems, 0, ax=lax.rem(row + 1, 4))
        down = copy(field.at[:, pl.ds(0, 3)], to_high, sems, 1, ax=lax.rem(row + 3, 4))
        return up, down

    def stage(field, staging, fields):
        for f in range(fields):
            for r in range(4):
                staging[0, f * 4 + r, 0:3] = field[f, r, 37:40]
                staging[1, f * 4 + r, 0:3] = field[f, r, 0:3]

    def when_up(action):
        pl.when(row < 3)(action)

    def when_down(action):
        pl.when(row > 0)(action)

    def start_ax(pair):
        when_up(pair[0].start)
        when_down(pair[1].start)

    def sent_ax(pair):
        when_up(pair[0].wait_send)
        when_down(pair[1].wait_send)

    def came_ax(pair):
        when_down(pair[0].wait_recv)
        when_up(pair[1].wait_recv)

    loads[0].wait()
    loads[1].wait()
    stage(state, az_out, 5)
    stage(flags, azf_out, 2)
    ghost_columns(state, ghost_out)
    az = az_copies(0)
    azf = [
        copy(azf_out.at[0], azf_in.at[0], azf_sem, 0, az=right),
        copy(azf_out.at[1], azf_in.at[1], azf_sem, 1, az=left),
    ]
    opposite = lax.rem(me + 32, 64)
    ghost = copy(ghost_out, ghost_in.at[0], ghost_sem.at[0], 0, az=opposite)
    ax = ax_copies(state, low.at[0], high.at[0], ax_sem.at[0])
    axf = ax_copies(flags, flow, fhigh, axf_sem)
    pl.semaphore_wait(barrier, 65)
    for item in az + azf:
        item.start()
    start_ax(ax)
    start_ax(axf)
    ghost.start()
    for item in loads[2:]:
        item.wait()
    build_mix(mine, mix_high, mix_low)
    padded[...] = jnp.zeros_like(padded)
    padded_flags[...] = jnp.zeros_like(padded_flags)
    for v in range(5):
        for r in range(4):
            padded[v, r, 3:43] = state[v, r]
    for s in range(2):
        for r in range(4):
            padded_flags[s, r, 3:43] = flags[s, r].astype(jnp.float32)

    def fill_az(section):
        for v in range(5):
            for r in range(4):
                padded[v, r, 0:3] = az_in[section, 0, v * 4 + r, 0:3]
                padded[v, r, 43:46] = az_in[section, 1, v * 4 + r, 0:3]

    for item in az + azf:
        item.wait_send()
        item.wait_recv()
    fill_az(0)
    for s in range(2):
        for r in range(4):
            padded_flags[s, r, 0:3] = azf_in[0, s * 4 + r, 0:3].astype(jnp.float32)
            padded_flags[s, r, 43:46] = azf_in[1, s * 4 + r, 0:3].astype(jnp.float32)
    azimuthal(padded, padded_flags, 0, rate)
    came_ax(ax)
    came_ax(axf)

    def rims(field, section):
        def low_rim():
            for v in range(5):
                for k in range(3):
                    low[section, v, k] = field[v, 0]

        def high_rim():
            for v in range(5):
                for k in range(3):
                    high[section, v, k] = field[v, 3]

        pl.when(row == 0)(low_rim)
        pl.when(row == 3)(high_rim)

    def flag_low_rim():
        for s in range(2):
            for k in range(3):
                flow[s, k] = flags[s, 0]

    def flag_high_rim():
        for s in range(2):
            for k in range(3):
                fhigh[s, k] = flags[s, 3]

    rims(state, 0)
    pl.when(row == 0)(flag_low_rim)
    pl.when(row == 3)(flag_high_rim)
    ghost.wait_send()
    ghost.wait_recv()

    def combine_first(v, r, rows, here, slope):
        first[v, r, rows, :] = here + slope * time_step

    finish(state, low.at[0], high.at[0], flags, flow, fhigh, 0, ghost_in.at[0], rate, combine_first)
    sent_ax(ax)
    sent_ax(axf)

    to_lines(first, send.at[0])
    spread(send.at[0], recv.at[0], me, peers, go_sem.at[0, 0], go_sem.at[0, 1])
    stage(first, az_out, 5)
    az = az_copies(1)
    for item in az:
        item.start()
    ax = ax_copies(first, low.at[1], high.at[1], ax_sem.at[1])
    start_ax(ax)
    for v in range(5):
        for r in range(4):
            padded[v, r, 3:43] = first[v, r]
    arrived(recv.at[0], go_sem.at[0, 1])
    project(recv.at[0], back.at[0], me, fwd, inv, twiddle, mix_high, mix_low)
    spread(back.at[0], ret.at[0], me, peers, come_sem.at[0, 0], come_sem.at[0, 1])
    for item in az:
        item.wait_send()
        item.wait_recv()
    fill_az(1)
    sent_ax(ax)
    came_ax(ax)
    arrived(ret.at[0], come_sem.at[0, 1])

    near = (
        copy(ret.at[0, pl.ds(16, 48)], near_low, near_sem, 0, ax=lax.rem(row + 1, 4)),
        copy(ret.at[0, pl.ds(0, 48)], near_high, near_sem, 1, ax=lax.rem(row + 3, 4)),
    )
    start_ax(near)
    inner48, inner40 = lanes((48, 128)) < NRING, lanes((40, 128)) < NRING
    for r in range(4):
        blocks = from_lines(ret.at[0], 16 * r)
        for v in range(5):
            merged = jnp.where(inner48, blocks[v], padded[v, r])
            padded[v, r] = merged
            first[v, r] = merged[3:43]
    ghost_columns(first, ghost_out)
    ghost = copy(ghost_out, ghost_in.at[1], ghost_sem.at[1], 0, az=opposite)
    ghost.start()
    azimuthal(padded, padded_flags, 1, rate)
    came_ax(near)

    def merge_low():
        for k in range(3):
            blocks = from_lines(near_low, 16 * k)
            for v in range(5):
                low[1, v, k] = jnp.where(inner40, blocks[v][3:43], low[1, v, k])

    def merge_high():
        for k in range(3):
            blocks = from_lines(near_high, 16 * k)
            for v in range(5):
                high[1, v, k] = jnp.where(inner40, blocks[v][3:43], high[1, v, k])

    when_down(merge_low)
    when_up(merge_high)
    rims(first, 1)
    ghost.wait_send()
    ghost.wait_recv()

    def combine_second(v, r, rows, here, slope):
        second[v, r, rows, :] = state[v, r, rows, :] * 0.75 + (here + slope * time_step) * 0.25

    finish(first, low.at[1], high.at[1], flags, flow, fhigh, 1, ghost_in.at[1], rate, combine_second)
    sent_ax(near)

    to_lines(second, send.at[1])
    spread(send.at[1], recv.at[1], me, peers, go_sem.at[1, 0], go_sem.at[1, 1])
    arrived(recv.at[1], go_sem.at[1, 1])
    project(recv.at[1], back.at[1], me, fwd, inv, twiddle, mix_high, mix_low)
    spread(back.at[1], ret.at[1], me, peers, come_sem.at[1, 0], come_sem.at[1, 1])
    arrived(ret.at[1], come_sem.at[1, 1])
    for r in range(4):
        blocks = from_lines(ret.at[1], 16 * r)
        for v in range(5):
            out[v, r] = jnp.where(inner40, blocks[v][3:43], second[v, r])
    for section in range(2):
        arrived(send.at[section], go_sem.at[section, 0])
        arrived(back.at[section], come_sem.at[section, 0])


def local(state, shock_flags):
    fwd, inv, twiddle, band = filter_tables()
    tables = [jnp.stack(split(jnp.asarray(t))) for t in (fwd, inv)]
    tables += [jnp.asarray(twiddle), jnp.asarray(band)]
    vmem = pl.BlockSpec(memory_space=pltpu.VMEM)
    f32, i32 = jnp.float32, jnp.int32
    dma = pltpu.SemaphoreType.DMA
    after = pl.pallas_call(
        kernel,
        out_shape=jax.ShapeDtypeStruct(state.shape, f32),
        in_specs=[pl.BlockSpec(memory_space=pltpu.HBM)] * 6,
        out_specs=vmem,
        scratch_shapes=[
            pltpu.VMEM((5, 4, 40, 128), f32),
            pltpu.VMEM((2, 4, 40, 128), i32),
            pltpu.VMEM((2, 80, 64), jnp.bfloat16),
            pltpu.VMEM((2, 64, 80), jnp.bfloat16),
            pltpu.VMEM((4, 40, 256), f32),
            pltpu.VMEM((4, 40, 256), f32),
            pltpu.VMEM((4, 256, 256), jnp.bfloat16),
            pltpu.VMEM((4, 256, 256), jnp.bfloat16),
            pltpu.VMEM((5, 4, 48, 128), f32),
            pltpu.VMEM((2, 4, 48, 128), f32),
            pltpu.VMEM((5, 4, 40, 128), f32),
            pltpu.VMEM((5, 4, 40, 128), f32),
            pltpu.VMEM((5, 4, 40, 128), f32),
            pltpu.VMEM((2, 20, 4, 128), f32),
            pltpu.VMEM((2, 2, 20, 4, 128), f32),
            pltpu.VMEM((2, 8, 4, 128), i32),
            pltpu.VMEM((2, 8, 4, 128), i32),
            pltpu.VMEM((2, 5, 3, 40, 128), f32),
            pltpu.VMEM((2, 5, 3, 40, 128), f32),
            pltpu.VMEM((2, 3, 40, 128), i32),
            pltpu.VMEM((2, 3, 40, 128), i32),
            pltpu.VMEM((40, 128), f32),
            pltpu.VMEM((2, 40, 128), f32),
            pltpu.VMEM((48, 2, 128), f32),
            pltpu.VMEM((48, 2, 128), f32),
            pltpu.VMEM((2, 64, 2, 128), f32),
            pltpu.VMEM((2, 64, 2, 128), f32),
            pltpu.VMEM((2, 64, 2, 128), f32),
            pltpu.VMEM((2, 64, 2, 128), f32),
            dma((6,)),
            dma((2, 2, 2)),
            dma((2, 2)),
            dma((2, 2, 2)),
            dma((2, 2)),
            dma((2, 2, 1)),
            dma((2, 2)),
            dma((2, 2)),
            dma((2, 2)),
        ],
        compiler_params=pltpu.CompilerParams(
            collective_id=0, has_side_effects=True, vmem_limit_bytes=63 * 1024 * 1024
        ),
    )(state, shock_flags, *tables)
    return after - state


def solution(mesh):
    in_specs = (P(None, "ax", "az", None), P(None, "ax", "az", None))
    out_specs = P(None, "ax", "az", None)
    return jax.shard_map(local, mesh=mesh, in_specs=in_specs, out_specs=out_specs, check_vma=False)
```

```python
import math

import jax
import jax.numpy as jnp
import numpy as np
from jax import lax
from jax.experimental import pallas as pl
from jax.experimental.pallas import tpu as pltpu
from jax.sharding import PartitionSpec as P

NRING = 16
MESH = pl.DeviceIdType.MESH

split_speed = 3.0
small_eps = 1e-06
time_step = 0.004


def filter_tables():
    d, k1 = np.arange(64), np.arange(33)
    angle = 2 * np.pi * np.outer(k1, d) / 64
    fwd = np.zeros((80, 64))
    fwd[:33], fwd[40:73] = np.cos(angle), -np.sin(angle)
    inv = np.zeros((64, 80))
    inv[:, :33], inv[:, 40:73] = np.cos(angle.T), -np.sin(angle.T)
    twiddle = np.zeros((4, 40, 256))
    m_in, m_out = np.arange(40), np.arange(-3, 43)
    scale = np.where((k1 == 0) | (k1 == 32), 1.0, 2.0)[:, None] / 2560
    for v in range(5):
        angle = 2 * np.pi * np.outer(k1, m_in) / 2560
        twiddle[0, :33, v * 48 + 3 : v * 48 + 43] = np.cos(angle)
        twiddle[1, :33, v * 48 + 3 : v * 48 + 43] = -np.sin(angle)
        angle = 2 * np.pi * np.outer(k1, m_out) / 2560
        twiddle[2, :33, v * 48 : v * 48 + 46] = np.cos(angle) * scale
        twiddle[3, :33, v * 48 : v * 48 + 46] = np.sin(angle) * scale
    band = np.zeros((16, 4, 48, 256))
    delta = m_out[None, :] - m_in[:, None]
    for j in range(16):
        if j % 2:
            q = (j + 1) // 2
            modes, extra = np.arange(-q, q), -q
        else:
            q = j // 2
            modes, extra = np.arange(-q, q + 1), q
        kept = sum(np.exp(2j * np.pi * k * delta / 40) for k in modes)
        twin = np.exp(2j * np.pi * extra * delta / 40)
        for k, part in enumerate((kept.real, kept.imag, twin.real, twin.imag)):
            band[j, k, 3:43, :46] = part
    return [a.astype(np.float32) for a in (fwd, inv, twiddle, band)]


def split(x):
    high = x.astype(jnp.bfloat16)
    return high, (x - high.astype(jnp.float32)).astype(jnp.bfloat16)


def dot(a, b):
    return jnp.dot(a, b, preferred_element_type=jnp.float32)


def by_left(a_high, a_low, b):
    high, low = split(b)
    return dot(a_high, high) + (dot(a_high, low) + dot(a_low, high))


def by_right(a, b_high, b_low):
    high, low = split(a)
    rows = a.shape[0]
    both = dot(jnp.concatenate([high, low], axis=0), b_high)
    return both[:rows] + (both[rows:] + dot(high, b_low))


def inverse(x):
    return pltpu.reciprocal(x, approx=True)


class Rows:
    def __init__(self, cells):
        self.cells = list(cells)

    def _with(self, other, op):
        if isinstance(other, Rows):
            pairs = zip(self.cells, other.cells)
            return Rows([None if a is None or b is None else op(a, b) for a, b in pairs])
        return Rows([None if a is None else op(a, other) for a in self.cells])

    def __add__(self, other):
        return self._with(other, lambda a, b: a + b)

    def __sub__(self, other):
        return self._with(other, lambda a, b: a - b)

    def __mul__(self, other):
        return self._with(other, lambda a, b: a * b)

    def map(self, op):
        return Rows([None if a is None else op(a) for a in self.cells])

    def shifted(self, by):
        n = len(self.cells)
        return Rows([self.cells[k + by] if 0 <= k + by < n else None for k in range(n)])


def at(x, by):
    if isinstance(x, Rows):
        return x.shifted(by)
    axis = 1 if x.shape[1] == 256 else 0
    n = x.shape[axis]
    return pltpu.roll(x, (n - by) % n, axis)


def inverse_of(x):
    return x.map(inverse) if isinstance(x, Rows) else inverse(x)


def indicators(f):
    d = at(f, 1) - f
    s = d - at(d, -1)
    s_next = at(s, 1)
    e = s - s_next
    h = s * 0.5
    q = s * s * (13.0 / 12.0) + small_eps
    mid = d - h
    up = d + h
    down = mid - s
    x = inverse_of(q + up * up)
    y = inverse_of(q + mid * mid)
    z = inverse_of(q + down * down)
    return d, s, s_next, e, x * x, y * y, z * z


def faces(flux, state, switch, choose):
    half = flux * 0.5
    lift = state * (0.5 * split_speed)
    d_p, s_p, sn_p, e_p, x_p, y_p, z_p = indicators(half + lift)
    zn_p = at(z_p, 1)
    top = at(x_p * e_p, -1) * 2.0 + zn_p * e_p * 3.0
    total = at(x_p, -1) + y_p * 6.0 + zn_p * 3.0
    plus = top * inverse_of(total)
    d_m, s_m, sn_m, e_m, x_m, y_m, z_m = indicators(half - lift)
    zn_m = at(z_m, 1)
    top = at(zn_m * e_m, 1) * 2.0 + x_m * e_m * 3.0
    total = at(zn_m, 1) + at(y_m, 1) * 6.0 + x_m * 3.0
    minus = top * inverse_of(total)
    middle = flux + (d_p + d_m) * 0.5
    own = s_p + sn_m
    weno = (plus - minus - own) * (1.0 / 6.0)
    central = (own + s_m + sn_p) * (-1.0 / 12.0)
    return middle + choose(switch, weno, central)


def pick(switch, a, b):
    if isinstance(a, Rows):
        triples = zip(switch.cells, a.cells, b.cells)
        return Rows([None if s is None or p is None or q is None else jnp.where(s, p, q) for s, p, q in triples])
    return jnp.where(switch, a, b)


def largest(a, b):
    if isinstance(a, Rows):
        return a._with(b, jnp.maximum)
    return jnp.maximum(a, b)


def window(flags):
    pair = largest(flags, at(flags, 1))
    four = largest(pair, at(pair, 2))
    six = at(largest(four, at(pair, 4)), -2)
    return six.map(lambda a: a > 0.5) if isinstance(six, Rows) else six > 0.5


def fluxes(u, q, p, component):
    parts = [u[1 + component], u[1] * q, u[2] * q, u[3] * q, (u[4] + p) * q]
    parts[1 + component] = parts[1 + component] + p
    return parts


def pressure(u, inv_rho):
    return (u[4] - (u[1] * u[1] + u[2] * u[2] + u[3] * u[3]) * inv_rho * 0.5) * 0.4


def lanes(shape):
    return lax.broadcasted_iota(jnp.int32, shape, len(shape) - 1)


def radius(rows):
    return lanes((rows, 128)).astype(jnp.float32) + 0.5


def azimuthal(padded, flags, section, rate):
    scale = -1.0 / (radius(40) * (2.0 * math.pi / 2560))

    def row(r, carry):
        u = [padded[v, r] for v in range(5)]
        inv_rho = inverse(u[0])
        q = u[3] * inv_rho
        f = fluxes(u, q, pressure(u, inv_rho), 2)
        switch = window(flags[section, r])
        for v in range(5):
            face = faces(f[v], u[v], switch, pick)
            rate[v, r] = (at(face, 3)[:40] - at(face, 2)[:40]) * scale
        return carry

    lax.fori_loop(0, 4, row, 0)


def finish(own, low, high, flags, flags_low, flags_high, section, rate, combine):
    inv_r = 1.0 / radius(8)
    lane = lanes((8, 128))

    def chunk(c, carry):
        at8 = pl.ds(pl.multiple_of(c * 8, 8), 8)
        u = [
            Rows(
                [low[v, k, at8, :] for k in range(3)]
                + [own[v, k, at8, :] for k in range(4)]
                + [high[v, k, at8, :] for k in range(3)]
            )
            for v in range(5)
        ]
        marks = Rows(
            [flags_low[section, k, at8, :] for k in range(3)]
            + [flags[section, k, at8, :] for k in range(4)]
            + [flags_high[section, k, at8, :] for k in range(3)]
        ).map(lambda a: a.astype(jnp.float32))
        switch = window(marks)
        inv_rho = u[0].map(inverse)
        p = pressure(u, inv_rho)
        f = fluxes(u, u[1] * inv_rho, p, 0)
        radial, source = [], []
        for r in range(4):
            here = [u[v].cells[3 + r] for v in range(5)]
            inv_here, p_here = inv_rho.cells[3 + r], p.cells[3 + r]
            g = fluxes(here, here[2] * inv_here, p_here, 1)
            swirl = here[3] * inv_here
            extra = [None, None, here[3] * swirl + p_here, -here[2] * swirl, None]
            terms = []
            for v in range(5):
                before = pltpu.roll(g[v], 1, 1)
                after = jnp.where(lane == 127, g[v], pltpu.roll(g[v], 127, 1))
                away = g[v] if extra[v] is None else g[v] - extra[v]
                terms.append((after - before) * 0.5 + away * inv_r)
            radial.append(terms)
        for v in range(5):
            face = faces(f[v], u[v], switch, pick).cells
            for r in range(4):
                slope = rate[v, r, at8, :] - (face[3 + r] - face[2 + r]) - radial[r][v]
                combine(v, r, at8, u[v].cells[3 + r], slope)
        return carry

    lax.fori_loop(0, 5, chunk, 0)


def cell_of(width):
    return lax.rem(lanes((16, width)), 48)


def side_by_side(blocks):
    lane = lanes(blocks[0].shape)
    packed = blocks[0]
    for r in range(1, 4):
        packed = jnp.where(lane >= 32 * r, pltpu.roll(blocks[r], 32 * r, 1), packed)
    return packed


def pack_state(padded):
    stacks = []
    for r in range(4):
        rest = jnp.zeros((16, 128), jnp.float32)
        stacks.append(jnp.concatenate([padded[v, r] for v in range(5)] + [rest], axis=0))
    return jnp.transpose(side_by_side(stacks))


def pack_flags(padded_flags):
    stacks = []
    for r in range(4):
        rest = jnp.zeros((32, 128), jnp.float32)
        stacks.append(jnp.concatenate([padded_flags[0, r], padded_flags[1, r], rest], axis=0))
    return jnp.transpose(side_by_side(stacks))


def fold_ends(blocks, width):
    cell = cell_of(width)
    to_right = jnp.zeros((16, width), jnp.float32)
    to_left = to_right
    for r in range(4):
        moved = pltpu.roll(blocks[r], (width - 40 + 3 * r) % width, 1)
        to_right = jnp.where((cell >= 3 * r) & (cell < 3 * r + 3), moved, to_right)
        moved = pltpu.roll(blocks[r], 31 + 3 * r, 1)
        to_left = jnp.where((cell >= 34 + 3 * r) & (cell < 37 + 3 * r), moved, to_left)
    return to_right, to_left


def with_ends(block, from_left, from_right, r):
    width = block.shape[1]
    cell = cell_of(width)
    before = pltpu.roll(from_left, width - 3 * r, 1) if r else from_left
    after = pltpu.roll(from_right, 9 - 3 * r, 1) if r < 3 else from_right
    return jnp.where(cell < 3, before, jnp.where(cell < 43, block, jnp.where(cell < 46, after, 0.0)))


def replicate(x):
    x = jnp.where(lanes(x.shape) < 48, x, 0.0)
    one = jnp.concatenate([x, jnp.zeros_like(x)], axis=1)
    two = one + pltpu.roll(one, 48, 1)
    four = two + pltpu.roll(two, 96, 1)
    return four + pltpu.roll(one, 192, 1)


def primitives(u):
    parts = [u[:, :128]] + [pltpu.roll(u, 256 - 48 * k, 1)[:, :128] for k in range(1, 5)]
    inv_rho = inverse(parts[0])
    return parts, inv_rho, pressure(parts, inv_rho)


def slot(shape, k):
    lane = lanes(shape)
    return (lane >= 48 * k) & (lane < 48 * k + 48)


def packed_flux(u, q, p, component):
    own, energy = slot(u.shape, 1 + component), slot(u.shape, 4)
    return u * q + jnp.where(own, p, jnp.where(energy, p * q, 0.0))


def near_azimuthal(own, marks, section, rate):
    for r in range(4):
        u = own(r)
        parts, inv_rho, p = primitives(u)
        q = replicate(parts[3] * inv_rho)
        f = packed_flux(u, q, replicate(p), 2)
        mark = marks(r)
        switch = window(replicate(pltpu.roll(mark, 80, 1) if section else mark))
        face = faces(f, u, switch, pick)
        cycle = lax.broadcasted_iota(jnp.int32, (16, 256), 0).astype(jnp.float32) + 0.5
        rate[16 * r : 16 * r + 16, :] = (at(face, -1) - face) * (1.0 / (cycle * (2.0 * math.pi / 2560)))


def near_finish(low, own, high, outer, ghost, marks, section, rate, combine):
    blocks = [low(k) for k in range(3)] + [own(r) for r in range(4)] + [high(k) for k in range(3)]
    f, switches, radial = [], [], []
    for k, u in enumerate(blocks):
        parts, inv_rho, p = primitives(u)
        wide_p = replicate(p)
        f.append(packed_flux(u, replicate(parts[1] * inv_rho), wide_p, 0))
        mark = marks[k]
        switches.append(replicate(pltpu.roll(mark, 80, 1) if section else mark))
        if 3 <= k < 7:
            r = k - 3
            beyond = outer(r)
            row = lax.broadcasted_iota(jnp.int32, (8, 256), 0)
            negated = slot((8, 256), 2) | slot((8, 256), 3)
            mirror = jnp.broadcast_to(ghost(r), (8, 256))
            mirror = jnp.where(negated, -mirror, mirror)
            beyond = jnp.where(row == 7, mirror, beyond)
            b_parts, b_inv, b_p = primitives(beyond)
            g_beyond = packed_flux(beyond, replicate(b_parts[2] * b_inv), replicate(b_p), 1)
            g = packed_flux(u, replicate(parts[2] * inv_rho), wide_p, 1)
            q_t = replicate(parts[3] * inv_rho)
            extra = jnp.where(
                slot((16, 256), 2),
                pltpu.roll(u, 256 - 48, 1) * q_t + wide_p,
                jnp.where(slot((16, 256), 3), -pltpu.roll(u, 48, 1) * q_t, 0.0),
            )
            ring = jnp.concatenate([g, g_beyond], axis=0)
            after, before = pltpu.roll(ring, 23, 0)[:16], pltpu.roll(ring, 1, 0)[:16]
            cycle = lax.broadcasted_iota(jnp.int32, (16, 256), 0).astype(jnp.float32) + 0.5
            radial.append((after - before) * 0.5 + (g - extra) * (1.0 / cycle))
    slopes = [[[None, None], [None, None]] for _ in range(4)]
    for h in range(2):
        for w in range(2):
            part = (slice(8 * h, 8 * h + 8), slice(128 * w, 128 * w + 128))
            face = faces(
                Rows([x[part] for x in f]),
                Rows([x[part] for x in blocks]),
                window(Rows([x[part] for x in switches])),
                pick,
            ).cells
            for r in range(4):
                slopes[r][h][w] = face[2 + r] - face[3 + r]
    lane = lanes((16, 256))
    cell = lax.rem(lane, 48)
    valid = (cell >= 3) & (cell < 43) & (lane < 240)
    for r in range(4):
        rows = [jnp.concatenate(pair, axis=1) for pair in slopes[r]]
        slope = jnp.concatenate(rows, axis=0) - radial[r] + rate[16 * r : 16 * r + 16, :]
        combine(r, jnp.where(valid, slope, 0.0), valid)


def packed_rows(ref, first, count):
    return jnp.concatenate([ref[first : first + count, 0, :], ref[first : first + count, 1, :]], axis=1)


def unpack(ret):
    lines = jnp.concatenate([packed_rows(ret, 0, 64), jnp.zeros((64, 256), jnp.float32)], axis=0)
    turned = jnp.transpose(lines)

    def block(v, r):
        rows = turned[48 * v : 48 * v + 48]
        return pltpu.roll(rows, 128 - 16 * r, 1) if r else rows

    return block


def others(me):
    y, x, z = me // 32, lax.rem(me // 8, 4), lax.rem(me, 8)
    ys = {d: lax.rem(y + d, 2) * 32 for d in (1, 0)}
    xs = {d: lax.rem(x + d, 4) * 8 for d in (2, 1, 3, 0)}
    zs = {d: lax.rem(z + d, 8) for d in (4, 3, 5, 2, 6, 1, 7, 0)}
    steps = [(dy, dx, dz) for dz in zs for dx in xs for dy in ys]
    steps.sort(key=lambda s: -(s[0] + min(s[1], 4 - s[1]) + min(s[2], 8 - s[2])))
    return [ys[dy] + xs[dx] + zs[dz] for dy, dx, dz in steps[:-1]]


def spread(send, recv, me, peers, send_sem, recv_sem):
    for to in peers:
        pltpu.make_async_remote_copy(
            src_ref=send.at[to],
            dst_ref=recv.at[me],
            send_sem=send_sem,
            recv_sem=recv_sem,
            device_id={"az": to},
            device_id_type=MESH,
        ).start()
    recv[pl.ds(me, 1)] = send[pl.ds(me, 1)]


def arrived(buffer, sem):
    rows = buffer.at[pl.ds(0, 63)]
    pltpu.make_async_copy(rows, rows, sem).wait()


def build_mix(mine, mix_high, mix_low):
    mix_high[...] = jnp.zeros_like(mix_high)
    mix_low[...] = jnp.zeros_like(mix_low)
    for k in range(4):
        rows = []
        for v in range(5):
            rows.append(pltpu.roll(mine[k], 48 * v, 1) if v else mine[k])
        rows.append(jnp.zeros((16, 256), jnp.float32))
        mix_high[k], mix_low[k] = split(jnp.concatenate(rows, axis=0))


def project(recv, back, me, fwd, inv, twiddle, mix_high, mix_low):
    x = jnp.concatenate([recv[:, 0, :], recv[:, 1, :]], axis=1)
    a = by_left(fwd[0], fwd[1], x)
    re, im = a[:40], a[40:]
    re, im = re * twiddle[0] - im * twiddle[1], re * twiddle[1] + im * twiddle[0]
    odd = lax.rem(me, 2) == 1
    first_row = lax.broadcasted_iota(jnp.int32, (8, 256), 0) == 0

    def twin_row(x):
        return jnp.where(first_row, jnp.where(odd, x[:8], x[32:40]), 0.0)

    main = jnp.concatenate([re, im], axis=0)
    twin = jnp.concatenate([twin_row(re), twin_row(im)], axis=0)
    c, s = by_right(main, mix_high[0], mix_low[0]), by_right(main, mix_high[1], mix_low[1])
    tc, ts = by_right(twin, mix_high[2], mix_low[2]), by_right(twin, mix_high[3], mix_low[3])
    re, im = c[:40] - s[40:], s[:40] + c[40:]
    t_re, t_im = tc[:8] - ts[8:], ts[:8] + tc[8:]

    def with_twin(x, t):
        top = x[:8] + jnp.where(odd, t, 0.0)
        return jnp.concatenate([top, x[8:32], x[32:40] + jnp.where(odd, 0.0, t)], axis=0)

    re, im = with_twin(re, t_re), with_twin(im, t_im)
    re, im = re * twiddle[2] - im * twiddle[3], re * twiddle[3] + im * twiddle[2]
    y = by_left(inv[0], inv[1], jnp.concatenate([re, im], axis=0))
    back[:, 0, :] = y[:, :128]
    back[:, 1, :] = y[:, 128:]


def kernel(
    state_hbm, flags_hbm, fwd_hbm, inv_hbm, twiddle_hbm, band, out,
    state, flags, fwd, inv, twiddle, mine, mix_high, mix_low, padded, padded_flags, rate, first, second,
    az_out, az_in, azf_out, azf_in, low, high, flow, fhigh,
    near, near_rate, near_low, near_high, near_outer, ends_out, ends_in, marks, marks_low, marks_high,
    mark_ends_out, mark_ends_in, ghost_out, ghost_in, near2_low, near2_high,
    send, recv, back, ret,
    sem, az_sem, azf_sem, ax_sem, axf_sem, end_sem, mark_end_sem, row_sem, mark_row_sem, ghost_sem, near_sem,
    go_sem, come_sem,
):
    me, row = lax.axis_index("az"), lax.axis_index("ax")
    right, left = lax.rem(me + 1, 64), lax.rem(me + 63, 64)
    upper, lower = lax.rem(row + 1, 4), lax.rem(row + 3, 4)
    opposite = lax.rem(me + 32, 64)
    pairs = [
        (state_hbm, state),
        (flags_hbm, flags),
        (fwd_hbm, fwd),
        (inv_hbm, inv),
        (twiddle_hbm, twiddle),
        (band.at[lax.rem(me, 16)], mine),
    ]
    loads = [pltpu.make_async_copy(a, b, sem.at[k]) for k, (a, b) in enumerate(pairs)]
    for item in loads:
        item.start()
    barrier = pltpu.get_barrier_semaphore()
    peers = others(me)
    for peer in peers:
        pl.semaphore_signal(barrier, inc=1, device_id={"az": peer}, device_id_type=MESH)
    for peer in (upper, lower):
        pl.semaphore_signal(barrier, inc=1, device_id={"ax": peer}, device_id_type=MESH)

    def copy(src, dst, sems, k, **place):
        return pltpu.make_async_remote_copy(
            src_ref=src,
            dst_ref=dst,
            send_sem=sems.at[0, k],
            recv_sem=sems.at[1, k],
            device_id=place,
            device_id_type=MESH,
        )

    def along_az(source, target, sems):
        return [
            copy(source.at[0], target.at[0], sems, 0, az=right),
            copy(source.at[1], target.at[1], sems, 1, az=left),
        ]

    def along_ax(up_from, to_low, down_from, to_high, sems):
        return copy(up_from, to_low, sems, 0, ax=upper), copy(down_from, to_high, sems, 1, ax=lower)

    def wide_ax(field, to_low, to_high, sems):
        return along_ax(field.at[:, pl.ds(1, 3)], to_low, field.at[:, pl.ds(0, 3)], to_high, sems)

    def stage(field, staging, fields):
        for f in range(fields):
            for r in range(4):
                staging[0, f * 4 + r, 0:3] = field[f, r, 37:40]
                staging[1, f * 4 + r, 0:3] = field[f, r, 0:3]

    def when_up(action):
        pl.when(row < 3)(action)

    def when_down(action):
        pl.when(row > 0)(action)

    def start_ax(pair):
        when_up(pair[0].start)
        when_down(pair[1].start)

    def sent_ax(pair):
        when_up(pair[0].wait_send)
        when_down(pair[1].wait_send)

    def came_ax(pair):
        when_down(pair[0].wait_recv)
        when_up(pair[1].wait_recv)

    def start_all(items):
        for item in items:
            item.start()

    def came_all(items):
        for item in items:
            item.wait_recv()

    def sent_all(items):
        for item in items:
            item.wait_send()

    padded[...] = jnp.zeros_like(padded)
    padded_flags[...] = jnp.zeros_like(padded_flags)
    loads[0].wait()
    loads[1].wait()
    for v in range(5):
        for r in range(4):
            padded[v, r, 3:43] = state[v, r]
    for s in range(2):
        for r in range(4):
            padded_flags[s, r, 3:43] = flags[s, r].astype(jnp.float32)
    packed = pack_state(padded)
    for r in range(4):
        near[0, 16 * r : 16 * r + 16, :] = packed[32 * r : 32 * r + 16]
        near_outer[0, 8 * r : 8 * r + 8, :] = packed[32 * r + 16 : 32 * r + 24]
        ghost_out[0, r, 0:1, :] = packed[32 * r : 32 * r + 1, :128]
        ghost_out[0, r, 1:2, :] = packed[32 * r : 32 * r + 1, 128:]
    ends_out[0], ends_out[1] = fold_ends([packed[32 * r : 32 * r + 16] for r in range(4)], 256)
    packed = pack_flags(padded_flags)
    for r in range(4):
        marks[0, 16 * r : 16 * r + 16, :] = packed[32 * r : 32 * r + 16]
    mark_ends_out[0], mark_ends_out[1] = fold_ends([packed[32 * r : 32 * r + 16] for r in range(4)], 128)
    ends = along_az(ends_out, ends_in, end_sem)
    mark_ends = along_az(mark_ends_out, mark_ends_in, mark_end_sem)
    rows = along_ax(near.at[0, pl.ds(16, 48)], near_low, near.at[0, pl.ds(0, 48)], near_high, row_sem)
    mark_rows = along_ax(marks.at[0, pl.ds(16, 48)], marks_low, marks.at[0, pl.ds(0, 48)], marks_high, mark_row_sem)
    ghost = copy(ghost_out.at[0], ghost_in.at[0], ghost_sem.at[0], 0, az=opposite)
    stage(state, az_out, 5)
    stage(flags, azf_out, 2)
    az = along_az(az_out, az_in.at[0], az_sem.at[0])
    azf = along_az(azf_out, azf_in, azf_sem)
    ax = wide_ax(state, low.at[0], high.at[0], ax_sem.at[0])
    axf = wide_ax(flags, flow, fhigh, axf_sem)
    pl.semaphore_wait(barrier, 65)
    start_ax(rows)
    start_all(ends)
    ghost.start()
    start_all(mark_ends)
    start_ax(mark_rows)
    start_all(az)
    start_all(azf)
    start_ax(ax)
    start_ax(axf)
    for item in loads[2:]:
        item.wait()
    build_mix(mine, mix_high, mix_low)

    came_all(ends)
    came_all(mark_ends)
    for r in range(4):
        at_row = slice(16 * r, 16 * r + 16)
        near[1, at_row, :] = with_ends(near[0, at_row, :], ends_in[0], ends_in[1], r)
        marks[1, at_row, :] = with_ends(marks[0, at_row, :], mark_ends_in[0], mark_ends_in[1], r)

    def own_state(r):
        return near[1, 16 * r : 16 * r + 16, :]

    def own_marks(r):
        return marks[1, 16 * r : 16 * r + 16, :]

    near_azimuthal(own_state, own_marks, 0, near_rate)
    came_ax(rows)
    came_ax(mark_rows)

    def low_rim():
        for k in range(3):
            near_low[16 * k : 16 * k + 16, :] = near[1, 0:16, :]
            marks_low[16 * k : 16 * k + 16, :] = marks[1, 0:16, :]

    def high_rim():
        for k in range(3):
            near_high[16 * k : 16 * k + 16, :] = near[1, 48:64, :]
            marks_high[16 * k : 16 * k + 16, :] = marks[1, 48:64, :]

    pl.when(row == 0)(low_rim)
    pl.when(row == 3)(high_rim)
    ghost.wait_recv()

    def mark_list():
        below = [marks_low[16 * k : 16 * k + 16, :] for k in range(3)]
        above = [marks_high[16 * k : 16 * k + 16, :] for k in range(3)]
        return below + [own_marks(r) for r in range(4)] + above

    def ghost_row(section):
        return lambda r: jnp.concatenate([ghost_in[section, r, 0:1, :], ghost_in[section, r, 1:2, :]], axis=1)

    def outer_rows(section):
        return lambda r: near_outer[section, 8 * r : 8 * r + 8, :]

    def hand_in(section, r, value):
        send[section, 16 * r : 16 * r + 16, 0, :] = value[:, :128]
        send[section, 16 * r : 16 * r + 16, 1, :] = value[:, 128:]

    def near_first(r, slope, valid):
        hand_in(0, r, jnp.where(valid, own_state(r) + slope * time_step, 0.0))

    near_finish(
        lambda k: near_low[16 * k : 16 * k + 16, :],
        own_state,
        lambda k: near_high[16 * k : 16 * k + 16, :],
        outer_rows(0),
        ghost_row(0),
        mark_list(),
        0,
        near_rate,
        near_first,
    )
    spread(send.at[0], recv.at[0], me, peers, go_sem.at[0, 0], go_sem.at[0, 1])

    sent_ax(rows)
    sent_ax(mark_rows)
    sent_all(ends + mark_ends + [ghost])

    def fill_az(section):
        for v in range(5):
            for r in range(4):
                padded[v, r, 0:3] = az_in[section, 0, v * 4 + r, 0:3]
                padded[v, r, 43:46] = az_in[section, 1, v * 4 + r, 0:3]

    came_all(az)
    came_all(azf)
    fill_az(0)
    for s in range(2):
        for r in range(4):
            padded_flags[s, r, 0:3] = azf_in[0, s * 4 + r, 0:3].astype(jnp.float32)
            padded_flags[s, r, 43:46] = azf_in[1, s * 4 + r, 0:3].astype(jnp.float32)
    azimuthal(padded, padded_flags, 0, rate)
    came_ax(ax)
    came_ax(axf)

    def rims(field, section):
        def low_rim():
            for v in range(5):
                for k in range(3):
                    low[section, v, k] = field[v, 0]

        def high_rim():
            for v in range(5):
                for k in range(3):
                    high[section, v, k] = field[v, 3]

        pl.when(row == 0)(low_rim)
        pl.when(row == 3)(high_rim)

    def flag_low_rim():
        for s in range(2):
            for k in range(3):
                flow[s, k] = flags[s, 0]

    def flag_high_rim():
        for s in range(2):
            for k in range(3):
                fhigh[s, k] = flags[s, 3]

    rims(state, 0)
    pl.when(row == 0)(flag_low_rim)
    pl.when(row == 3)(flag_high_rim)

    def combine_first(v, r, rows, here, slope):
        first[v, r, rows, :] = here + slope * time_step

    finish(state, low.at[0], high.at[0], flags, flow, fhigh, 0, rate, combine_first)
    sent_all(az + azf)
    arrived(recv.at[0], go_sem.at[0, 1])
    project(recv.at[0], back.at[0], me, fwd, inv, twiddle, mix_high, mix_low)
    spread(back.at[0], ret.at[0], me, peers, come_sem.at[0, 0], come_sem.at[0, 1])
    stage(first, az_out, 5)
    az = along_az(az_out, az_in.at[1], az_sem.at[1])
    start_all(az)
    ax2 = wide_ax(first, low.at[1], high.at[1], ax_sem.at[1])
    start_ax(ax2)
    for v in range(5):
        for r in range(4):
            padded[v, r, 3:43] = first[v, r]
    packed = pack_state(padded)
    for r in range(4):
        near_outer[1, 8 * r : 8 * r + 8, :] = packed[32 * r + 16 : 32 * r + 24]
    arrived(ret.at[0], come_sem.at[0, 1])

    rows = along_ax(ret.at[0, pl.ds(16, 48)], near2_low, ret.at[0, pl.ds(0, 48)], near2_high, near_sem)
    start_ax(rows)
    for r in range(4):
        ghost_out[1, r] = ret[0, 16 * r]
    ghost = copy(ghost_out.at[1], ghost_in.at[1], ghost_sem.at[1], 0, az=opposite)
    ghost.start()

    def own_first(r):
        return packed_rows(ret.at[0], 16 * r, 16)

    near_azimuthal(own_first, own_marks, 1, near_rate)
    came_ax(rows)

    def low_rim_two():
        for k in range(3):
            near2_low[16 * k : 16 * k + 16] = ret[0, 0:16]

    def high_rim_two():
        for k in range(3):
            near2_high[16 * k : 16 * k + 16] = ret[0, 48:64]

    pl.when(row == 0)(low_rim_two)
    pl.when(row == 3)(high_rim_two)
    ghost.wait_recv()

    def near_second(r, slope, valid):
        value = own_state(r) * 0.75 + (own_first(r) + slope * time_step) * 0.25
        hand_in(1, r, jnp.where(valid, value, 0.0))

    near_finish(
        lambda k: packed_rows(near2_low, 16 * k, 16),
        own_first,
        lambda k: packed_rows(near2_high, 16 * k, 16),
        outer_rows(1),
        ghost_row(1),
        mark_list(),
        1,
        near_rate,
        near_second,
    )
    spread(send.at[1], recv.at[1], me, peers, go_sem.at[1, 0], go_sem.at[1, 1])

    inner40 = lanes((40, 128)) < NRING
    sent_ax(ax)
    sent_ax(axf)
    sent_ax(ax2)
    block = unpack(ret.at[0])
    for r in range(4):
        for v in range(5):
            first[v, r] = jnp.where(inner40, block(v, r)[3:43], first[v, r])
    came_all(az)
    sent_all(az + [ghost])
    fill_az(1)
    azimuthal(padded, padded_flags, 1, rate)
    arrived(recv.at[1], go_sem.at[1, 1])
    project(recv.at[1], back.at[1], me, fwd, inv, twiddle, mix_high, mix_low)
    spread(back.at[1], ret.at[1], me, peers, come_sem.at[1, 0], come_sem.at[1, 1])
    came_ax(ax2)
    rims(first, 1)

    def combine_second(v, r, rows, here, slope):
        second[v, r, rows, :] = state[v, r, rows, :] * 0.75 + (here + slope * time_step) * 0.25

    finish(first, low.at[1], high.at[1], flags, flow, fhigh, 1, rate, combine_second)
    sent_ax(rows)
    for section in range(2):
        arrived(send.at[section], go_sem.at[section, 0])
    arrived(back.at[0], come_sem.at[0, 0])
    arrived(ret.at[1], come_sem.at[1, 1])
    block = unpack(ret.at[1])
    for r in range(4):
        for v in range(5):
            out[v, r] = jnp.where(inner40, block(v, r)[3:43], second[v, r])
    arrived(back.at[1], come_sem.at[1, 0])


def local(state, shock_flags):
    fwd, inv, twiddle, band = filter_tables()
    tables = [jnp.stack(split(jnp.asarray(t))) for t in (fwd, inv)]
    tables += [jnp.asarray(twiddle), jnp.asarray(band)]
    vmem = pl.BlockSpec(memory_space=pltpu.VMEM)
    f32, i32 = jnp.float32, jnp.int32
    dma = pltpu.SemaphoreType.DMA
    in_hbm = [pltpu.with_memory_space_constraint(x, pltpu.HBM) for x in (state, shock_flags, *tables)]
    after = pl.pallas_call(
        kernel,
        out_shape=jax.ShapeDtypeStruct(state.shape, f32),
        in_specs=[pl.BlockSpec(memory_space=pltpu.HBM)] * 6,
        out_specs=vmem,
        scratch_shapes=[
            pltpu.VMEM((5, 4, 40, 128), f32),
            pltpu.VMEM((2, 4, 40, 128), i32),
            pltpu.VMEM((2, 80, 64), jnp.bfloat16),
            pltpu.VMEM((2, 64, 80), jnp.bfloat16),
            pltpu.VMEM((4, 40, 256), f32),
            pltpu.VMEM((4, 48, 256), f32),
            pltpu.VMEM((4, 256, 256), jnp.bfloat16),
            pltpu.VMEM((4, 256, 256), jnp.bfloat16),
            pltpu.VMEM((5, 4, 48, 128), f32),
            pltpu.VMEM((2, 4, 48, 128), f32),
            pltpu.VMEM((5, 4, 40, 128), f32),
            pltpu.VMEM((5, 4, 40, 128), f32),
            pltpu.VMEM((5, 4, 40, 128), f32),
            pltpu.VMEM((2, 20, 4, 128), f32),
            pltpu.VMEM((2, 2, 20, 4, 128), f32),
            pltpu.VMEM((2, 8, 4, 128), i32),
            pltpu.VMEM((2, 8, 4, 128), i32),
            pltpu.VMEM((2, 5, 3, 40, 128), f32),
            pltpu.VMEM((2, 5, 3, 40, 128), f32),
            pltpu.VMEM((2, 3, 40, 128), i32),
            pltpu.VMEM((2, 3, 40, 128), i32),
            pltpu.VMEM((2, 64, 256), f32),
            pltpu.VMEM((64, 256), f32),
            pltpu.VMEM((48, 256), f32),
            pltpu.VMEM((48, 256), f32),
            pltpu.VMEM((2, 32, 256), f32),
            pltpu.VMEM((2, 16, 256), f32),
            pltpu.VMEM((2, 16, 256), f32),
            pltpu.VMEM((2, 64, 128), f32),
            pltpu.VMEM((48, 128), f32),
            pltpu.VMEM((48, 128), f32),
            pltpu.VMEM((2, 16, 128), f32),
            pltpu.VMEM((2, 16, 128), f32),
            pltpu.VMEM((2, 4, 2, 128), f32),
            pltpu.VMEM((2, 4, 2, 128), f32),
            pltpu.VMEM((48, 2, 128), f32),
            pltpu.VMEM((48, 2, 128), f32),
            pltpu.VMEM((2, 64, 2, 128), f32),
            pltpu.VMEM((2, 64, 2, 128), f32),
            pltpu.VMEM((2, 64, 2, 128), f32),
            pltpu.VMEM((2, 64, 2, 128), f32),
            dma((6,)),
            dma((2, 2, 2)),
            dma((2, 2)),
            dma((2, 2, 2)),
            dma((2, 2)),
            dma((2, 2)),
            dma((2, 2)),
            dma((2, 2)),
            dma((2, 2)),
            dma((2, 2, 1)),
            dma((2, 2)),
            dma((2, 2)),
            dma((2, 2)),
        ],
        compiler_params=pltpu.CompilerParams(
            collective_id=0, has_side_effects=True, vmem_limit_bytes=40 * 1024 * 1024
        ),
    )(*in_hbm)
    return after - state


def solution(mesh):
    in_specs = (P(None, "ax", "az", None), P(None, "ax", "az", None))
    out_specs = P(None, "ax", "az", None)
    return jax.shard_map(local, mesh=mesh, in_specs=in_specs, out_specs=out_specs, check_vma=False)
```

```python
import math

import jax
import jax.numpy as jnp
import numpy as np
from jax import lax
from jax.experimental import pallas as pl
from jax.experimental.pallas import tpu as pltpu
from jax.sharding import PartitionSpec as P

NRING = 16
MESH = pl.DeviceIdType.MESH

split_speed = 3.0
small_eps = 1e-06
time_step = 0.004


def filter_tables():
    d, k1 = np.arange(64), np.arange(33)
    angle = 2 * np.pi * np.outer(k1, d) / 64
    fwd = np.zeros((80, 64))
    fwd[:33], fwd[40:73] = np.cos(angle), -np.sin(angle)
    inv = np.zeros((64, 80))
    inv[:, :33], inv[:, 40:73] = np.cos(angle.T), -np.sin(angle.T)
    twiddle = np.zeros((4, 40, 256))
    m_in, m_out = np.arange(40), np.arange(-3, 43)
    scale = np.where((k1 == 0) | (k1 == 32), 1.0, 2.0)[:, None] / 2560
    for v in range(5):
        angle = 2 * np.pi * np.outer(k1, m_in) / 2560
        twiddle[0, :33, v * 48 + 3 : v * 48 + 43] = np.cos(angle)
        twiddle[1, :33, v * 48 + 3 : v * 48 + 43] = -np.sin(angle)
        angle = 2 * np.pi * np.outer(k1, m_out) / 2560
        twiddle[2, :33, v * 48 : v * 48 + 46] = np.cos(angle) * scale
        twiddle[3, :33, v * 48 : v * 48 + 46] = np.sin(angle) * scale
    band = np.zeros((16, 4, 48, 256))
    delta = m_out[None, :] - m_in[:, None]
    for j in range(16):
        if j % 2:
            q = (j + 1) // 2
            modes, extra = np.arange(-q, q), -q
        else:
            q = j // 2
            modes, extra = np.arange(-q, q + 1), q
        kept = sum(np.exp(2j * np.pi * k * delta / 40) for k in modes)
        twin = np.exp(2j * np.pi * extra * delta / 40)
        for k, part in enumerate((kept.real, kept.imag, twin.real, twin.imag)):
            band[j, k, 3:43, :46] = part
    return [a.astype(np.float32) for a in (fwd, inv, twiddle, band)]


def split(x):
    high = x.astype(jnp.bfloat16)
    return high, (x - high.astype(jnp.float32)).astype(jnp.bfloat16)


def dot(a, b):
    return jnp.dot(a, b, preferred_element_type=jnp.float32)


def by_left(a_high, a_low, b):
    high, low = split(b)
    return dot(a_high, high) + (dot(a_high, low) + dot(a_low, high))


def by_right(a, b_high, b_low):
    high, low = split(a)
    rows = a.shape[0]
    both = dot(jnp.concatenate([high, low], axis=0), b_high)
    return both[:rows] + (both[rows:] + dot(high, b_low))


def inverse(x):
    return pltpu.reciprocal(x, approx=True)


class Rows:
    def __init__(self, cells):
        self.cells = list(cells)

    def _with(self, other, op):
        if isinstance(other, Rows):
            pairs = zip(self.cells, other.cells)
            return Rows([None if a is None or b is None else op(a, b) for a, b in pairs])
        return Rows([None if a is None else op(a, other) for a in self.cells])

    def __add__(self, other):
        return self._with(other, lambda a, b: a + b)

    def __sub__(self, other):
        return self._with(other, lambda a, b: a - b)

    def __mul__(self, other):
        return self._with(other, lambda a, b: a * b)

    def map(self, op):
        return Rows([None if a is None else op(a) for a in self.cells])

    def shifted(self, by):
        n = len(self.cells)
        return Rows([self.cells[k + by] if 0 <= k + by < n else None for k in range(n)])


def at(x, by):
    if isinstance(x, Rows):
        return x.shifted(by)
    axis = 1 if x.shape[1] == 256 else 0
    n = x.shape[axis]
    return pltpu.roll(x, (n - by) % n, axis)


def inverse_of(x):
    return x.map(inverse) if isinstance(x, Rows) else inverse(x)


def indicators(f):
    d = at(f, 1) - f
    s = d - at(d, -1)
    s_next = at(s, 1)
    e = s - s_next
    h = s * 0.5
    q = s * s * (13.0 / 12.0) + small_eps
    mid = d - h
    up = d + h
    down = mid - s
    x = inverse_of(q + up * up)
    y = inverse_of(q + mid * mid)
    z = inverse_of(q + down * down)
    return d, s, s_next, e, x * x, y * y, z * z


def faces(flux, state, switch, choose):
    half = flux * 0.5
    lift = state * (0.5 * split_speed)
    d_p, s_p, sn_p, e_p, x_p, y_p, z_p = indicators(half + lift)
    zn_p = at(z_p, 1)
    top = at(x_p * e_p, -1) * 2.0 + zn_p * e_p * 3.0
    total = at(x_p, -1) + y_p * 6.0 + zn_p * 3.0
    plus = top * inverse_of(total)
    d_m, s_m, sn_m, e_m, x_m, y_m, z_m = indicators(half - lift)
    zn_m = at(z_m, 1)
    top = at(zn_m * e_m, 1) * 2.0 + x_m * e_m * 3.0
    total = at(zn_m, 1) + at(y_m, 1) * 6.0 + x_m * 3.0
    minus = top * inverse_of(total)
    middle = flux + (d_p + d_m) * 0.5
    own = s_p + sn_m
    weno = (plus - minus - own) * (1.0 / 6.0)
    central = (own + s_m + sn_p) * (-1.0 / 12.0)
    return middle + choose(switch, weno, central)


def pick(switch, a, b):
    if isinstance(a, Rows):
        triples = zip(switch.cells, a.cells, b.cells)
        return Rows([None if s is None or p is None or q is None else jnp.where(s, p, q) for s, p, q in triples])
    return jnp.where(switch, a, b)


def largest(a, b):
    if isinstance(a, Rows):
        return a._with(b, jnp.maximum)
    return jnp.maximum(a, b)


def window(flags):
    pair = largest(flags, at(flags, 1))
    four = largest(pair, at(pair, 2))
    six = at(largest(four, at(pair, 4)), -2)
    return six.map(lambda a: a > 0.5) if isinstance(six, Rows) else six > 0.5


def fluxes(u, q, p, component):
    parts = [u[1 + component], u[1] * q, u[2] * q, u[3] * q, (u[4] + p) * q]
    parts[1 + component] = parts[1 + component] + p
    return parts


def pressure(u, inv_rho):
    return (u[4] - (u[1] * u[1] + u[2] * u[2] + u[3] * u[3]) * inv_rho * 0.5) * 0.4


def lanes(shape):
    return lax.broadcasted_iota(jnp.int32, shape, len(shape) - 1)


def radius(rows):
    return lanes((rows, 128)).astype(jnp.float32) + 0.5


def azimuthal(padded, flags, section, rate):
    scale = -1.0 / (radius(40) * (2.0 * math.pi / 2560))

    def row(r, carry):
        u = [padded[v, r] for v in range(5)]
        inv_rho = inverse(u[0])
        q = u[3] * inv_rho
        f = fluxes(u, q, pressure(u, inv_rho), 2)
        switch = window(flags[section, r])
        for v in range(5):
            face = faces(f[v], u[v], switch, pick)
            rate[v, r] = (at(face, 3)[:40] - at(face, 2)[:40]) * scale
        return carry

    lax.fori_loop(0, 4, row, 0)


def finish(own, low, high, flags, flags_low, flags_high, section, rate, combine):
    inv_r = 1.0 / radius(8)
    lane = lanes((8, 128))

    def chunk(c, carry):
        at8 = pl.ds(pl.multiple_of(c * 8, 8), 8)
        u = [
            Rows(
                [low[v, k, at8, :] for k in range(3)]
                + [own[v, k, at8, :] for k in range(4)]
                + [high[v, k, at8, :] for k in range(3)]
            )
            for v in range(5)
        ]
        marks = Rows(
            [flags_low[section, k, at8, :] for k in range(3)]
            + [flags[section, k, at8, :] for k in range(4)]
            + [flags_high[section, k, at8, :] for k in range(3)]
        ).map(lambda a: a.astype(jnp.float32))
        switch = window(marks)
        inv_rho = u[0].map(inverse)
        p = pressure(u, inv_rho)
        f = fluxes(u, u[1] * inv_rho, p, 0)
        radial, source = [], []
        for r in range(4):
            here = [u[v].cells[3 + r] for v in range(5)]
            inv_here, p_here = inv_rho.cells[3 + r], p.cells[3 + r]
            g = fluxes(here, here[2] * inv_here, p_here, 1)
            swirl = here[3] * inv_here
            extra = [None, None, here[3] * swirl + p_here, -here[2] * swirl, None]
            terms = []
            for v in range(5):
                before = pltpu.roll(g[v], 1, 1)
                after = jnp.where(lane == 127, g[v], pltpu.roll(g[v], 127, 1))
                away = g[v] if extra[v] is None else g[v] - extra[v]
                terms.append((after - before) * 0.5 + away * inv_r)
            radial.append(terms)
        for v in range(5):
            face = faces(f[v], u[v], switch, pick).cells
            for r in range(4):
                slope = rate[v, r, at8, :] - (face[3 + r] - face[2 + r]) - radial[r][v]
                combine(v, r, at8, u[v].cells[3 + r], slope)
        return carry

    lax.fori_loop(0, 5, chunk, 0)


def cell_of(width):
    return lax.rem(lanes((16, width)), 48)


def side_by_side(blocks):
    lane = lanes(blocks[0].shape)
    packed = blocks[0]
    for r in range(1, 4):
        packed = jnp.where(lane >= 32 * r, pltpu.roll(blocks[r], 32 * r, 1), packed)
    return packed


def pack_state(padded):
    stacks = []
    for r in range(4):
        rest = jnp.zeros((16, 128), jnp.float32)
        stacks.append(jnp.concatenate([padded[v, r] for v in range(5)] + [rest], axis=0))
    return jnp.transpose(side_by_side(stacks))


def pack_flags(padded_flags):
    stacks = []
    for r in range(4):
        rest = jnp.zeros((32, 128), jnp.float32)
        stacks.append(jnp.concatenate([padded_flags[0, r], padded_flags[1, r], rest], axis=0))
    return jnp.transpose(side_by_side(stacks))


def fold_ends(blocks, width):
    cell = cell_of(width)
    to_right = jnp.zeros((16, width), jnp.float32)
    to_left = to_right
    for r in range(4):
        moved = pltpu.roll(blocks[r], (width - 40 + 3 * r) % width, 1)
        to_right = jnp.where((cell >= 3 * r) & (cell < 3 * r + 3), moved, to_right)
        moved = pltpu.roll(blocks[r], 31 + 3 * r, 1)
        to_left = jnp.where((cell >= 34 + 3 * r) & (cell < 37 + 3 * r), moved, to_left)
    return to_right, to_left


def with_ends(block, from_left, from_right, r):
    width = block.shape[1]
    cell = cell_of(width)
    before = pltpu.roll(from_left, width - 3 * r, 1) if r else from_left
    after = pltpu.roll(from_right, 9 - 3 * r, 1) if r < 3 else from_right
    return jnp.where(cell < 3, before, jnp.where(cell < 43, block, jnp.where(cell < 46, after, 0.0)))


def replicate(x):
    x = jnp.where(lanes(x.shape) < 48, x, 0.0)
    one = jnp.concatenate([x, jnp.zeros_like(x)], axis=1)
    two = one + pltpu.roll(one, 48, 1)
    four = two + pltpu.roll(two, 96, 1)
    return four + pltpu.roll(one, 192, 1)


def primitives(u):
    parts = [u[:, :128]] + [pltpu.roll(u, 256 - 48 * k, 1)[:, :128] for k in range(1, 5)]
    inv_rho = inverse(parts[0])
    return parts, inv_rho, pressure(parts, inv_rho)


def slot(shape, k):
    lane = lanes(shape)
    return (lane >= 48 * k) & (lane < 48 * k + 48)


def packed_flux(u, q, p, component):
    own, energy = slot(u.shape, 1 + component), slot(u.shape, 4)
    return u * q + jnp.where(own, p, jnp.where(energy, p * q, 0.0))


def near_azimuthal(own, marks, section, rate):
    for r in range(4):
        u = own(r)
        parts, inv_rho, p = primitives(u)
        q = replicate(parts[3] * inv_rho)
        f = packed_flux(u, q, replicate(p), 2)
        mark = marks(r)
        switch = window(replicate(pltpu.roll(mark, 80, 1) if section else mark))
        face = faces(f, u, switch, pick)
        cycle = lax.broadcasted_iota(jnp.int32, (16, 256), 0).astype(jnp.float32) + 0.5
        rate[16 * r : 16 * r + 16, :] = (at(face, -1) - face) * (1.0 / (cycle * (2.0 * math.pi / 2560)))


def near_finish(low, own, high, outer, ghost, marks, section, rate, combine):
    blocks = [low(k) for k in range(3)] + [own(r) for r in range(4)] + [high(k) for k in range(3)]
    f, switches, radial = [], [], []
    for k, u in enumerate(blocks):
        parts, inv_rho, p = primitives(u)
        wide_p = replicate(p)
        f.append(packed_flux(u, replicate(parts[1] * inv_rho), wide_p, 0))
        mark = marks[k]
        switches.append(replicate(pltpu.roll(mark, 80, 1) if section else mark))
        if 3 <= k < 7:
            r = k - 3
            beyond = outer(r)
            row = lax.broadcasted_iota(jnp.int32, (8, 256), 0)
            negated = slot((8, 256), 2) | slot((8, 256), 3)
            mirror = jnp.broadcast_to(ghost(r), (8, 256))
            mirror = jnp.where(negated, -mirror, mirror)
            beyond = jnp.where(row == 7, mirror, beyond)
            b_parts, b_inv, b_p = primitives(beyond)
            g_beyond = packed_flux(beyond, replicate(b_parts[2] * b_inv), replicate(b_p), 1)
            g = packed_flux(u, replicate(parts[2] * inv_rho), wide_p, 1)
            q_t = replicate(parts[3] * inv_rho)
            extra = jnp.where(
                slot((16, 256), 2),
                pltpu.roll(u, 256 - 48, 1) * q_t + wide_p,
                jnp.where(slot((16, 256), 3), -pltpu.roll(u, 48, 1) * q_t, 0.0),
            )
            ring = jnp.concatenate([g, g_beyond], axis=0)
            after, before = pltpu.roll(ring, 23, 0)[:16], pltpu.roll(ring, 1, 0)[:16]
            cycle = lax.broadcasted_iota(jnp.int32, (16, 256), 0).astype(jnp.float32) + 0.5
            radial.append((after - before) * 0.5 + (g - extra) * (1.0 / cycle))
    slopes = [[[None, None], [None, None]] for _ in range(4)]
    for h in range(2):
        for w in range(2):
            part = (slice(8 * h, 8 * h + 8), slice(128 * w, 128 * w + 128))
            face = faces(
                Rows([x[part] for x in f]),
                Rows([x[part] for x in blocks]),
                window(Rows([x[part] for x in switches])),
                pick,
            ).cells
            for r in range(4):
                slopes[r][h][w] = face[2 + r] - face[3 + r]
    lane = lanes((16, 256))
    cell = lax.rem(lane, 48)
    valid = (cell >= 3) & (cell < 43) & (lane < 240)
    for r in range(4):
        rows = [jnp.concatenate(pair, axis=1) for pair in slopes[r]]
        slope = jnp.concatenate(rows, axis=0) - radial[r] + rate[16 * r : 16 * r + 16, :]
        combine(r, jnp.where(valid, slope, 0.0), valid)


def packed_rows(ref, first, count):
    return jnp.concatenate([ref[first : first + count, 0, :], ref[first : first + count, 1, :]], axis=1)


def unpack(ret):
    lines = jnp.concatenate([packed_rows(ret, 0, 64), jnp.zeros((64, 256), jnp.float32)], axis=0)
    turned = jnp.transpose(lines)

    def block(v, r):
        rows = turned[48 * v : 48 * v + 48]
        return pltpu.roll(rows, 128 - 16 * r, 1) if r else rows

    return block


def others(me):
    y, x, z = me // 32, lax.rem(me // 8, 4), lax.rem(me, 8)
    ys = {d: lax.rem(y + d, 2) * 32 for d in (1, 0)}
    xs = {d: lax.rem(x + d, 4) * 8 for d in (2, 1, 3, 0)}
    zs = {d: lax.rem(z + d, 8) for d in (4, 3, 5, 2, 6, 1, 7, 0)}
    steps = [(dy, dx, dz) for dz in zs for dx in xs for dy in ys]
    steps.sort(key=lambda s: -(s[0] + min(s[1], 4 - s[1]) + min(s[2], 8 - s[2])))
    return [ys[dy] + xs[dx] + zs[dz] for dy, dx, dz in steps[:-1]]


def spread(send, recv, me, peers, send_sem, recv_sem):
    for to in peers:
        pltpu.make_async_remote_copy(
            src_ref=send.at[to],
            dst_ref=recv.at[me],
            send_sem=send_sem,
            recv_sem=recv_sem,
            device_id={"az": to},
            device_id_type=MESH,
        ).start()
    recv[pl.ds(me, 1)] = send[pl.ds(me, 1)]


def arrived(buffer, sem):
    rows = buffer.at[pl.ds(0, 63)]
    pltpu.make_async_copy(rows, rows, sem).wait()


def build_mix(mine, mix_high, mix_low):
    mix_high[...] = jnp.zeros_like(mix_high)
    mix_low[...] = jnp.zeros_like(mix_low)
    for k in range(4):
        rows = []
        for v in range(5):
            rows.append(pltpu.roll(mine[k], 48 * v, 1) if v else mine[k])
        rows.append(jnp.zeros((16, 256), jnp.float32))
        mix_high[k], mix_low[k] = split(jnp.concatenate(rows, axis=0))


def project(recv, back, me, fwd, inv, twiddle, mix_high, mix_low):
    x = jnp.concatenate([recv[:, 0, :], recv[:, 1, :]], axis=1)
    a = by_left(fwd[0], fwd[1], x)
    re, im = a[:40], a[40:]
    re, im = re * twiddle[0] - im * twiddle[1], re * twiddle[1] + im * twiddle[0]
    odd = lax.rem(me, 2) == 1
    first_row = lax.broadcasted_iota(jnp.int32, (8, 256), 0) == 0

    def twin_row(x):
        return jnp.where(first_row, jnp.where(odd, x[:8], x[32:40]), 0.0)

    main = jnp.concatenate([re, im], axis=0)
    twin = jnp.concatenate([twin_row(re), twin_row(im)], axis=0)
    c, s = by_right(main, mix_high[0], mix_low[0]), by_right(main, mix_high[1], mix_low[1])
    tc, ts = by_right(twin, mix_high[2], mix_low[2]), by_right(twin, mix_high[3], mix_low[3])
    re, im = c[:40] - s[40:], s[:40] + c[40:]
    t_re, t_im = tc[:8] - ts[8:], ts[:8] + tc[8:]

    def with_twin(x, t):
        top = x[:8] + jnp.where(odd, t, 0.0)
        return jnp.concatenate([top, x[8:32], x[32:40] + jnp.where(odd, 0.0, t)], axis=0)

    re, im = with_twin(re, t_re), with_twin(im, t_im)
    re, im = re * twiddle[2] - im * twiddle[3], re * twiddle[3] + im * twiddle[2]
    y = by_left(inv[0], inv[1], jnp.concatenate([re, im], axis=0))
    back[:, 0, :] = y[:, :128]
    back[:, 1, :] = y[:, 128:]


def kernel(
    state_hbm, flags_hbm, fwd_hbm, inv_hbm, twiddle_hbm, band, out,
    state, flags, fwd, inv, twiddle, mine, mix_high, mix_low, padded, padded_flags, rate, first, second,
    az_out, az_in, azf_out, azf_in, low, high, flow, fhigh,
    near, near_rate, near_low, near_high, near_outer, ends_out, ends_in, marks, marks_low, marks_high,
    mark_ends_out, mark_ends_in, ghost_out, ghost_in, near2_low, near2_high,
    send, recv, back, ret,
    sem, az_sem, azf_sem, ax_sem, axf_sem, end_sem, mark_end_sem, row_sem, mark_row_sem, ghost_sem, near_sem,
    go_sem, come_sem,
):
    me, row = lax.axis_index("az"), lax.axis_index("ax")
    right, left = lax.rem(me + 1, 64), lax.rem(me + 63, 64)
    upper, lower = lax.rem(row + 1, 4), lax.rem(row + 3, 4)
    opposite = lax.rem(me + 32, 64)
    pairs = [
        (state_hbm, state),
        (flags_hbm, flags),
        (fwd_hbm, fwd),
        (inv_hbm, inv),
        (twiddle_hbm, twiddle),
        (band.at[lax.rem(me, 16)], mine),
    ]
    loads = [pltpu.make_async_copy(a, b, sem.at[k]) for k, (a, b) in enumerate(pairs)]
    for item in loads:
        item.start()
    barrier = pltpu.get_barrier_semaphore()
    peers = others(me)
    for peer in peers:
        pl.semaphore_signal(barrier, inc=1, device_id={"az": peer}, device_id_type=MESH)
    for peer in (upper, lower):
        pl.semaphore_signal(barrier, inc=1, device_id={"ax": peer}, device_id_type=MESH)

    def copy(src, dst, sems, k, **place):
        return pltpu.make_async_remote_copy(
            src_ref=src,
            dst_ref=dst,
            send_sem=sems.at[0, k],
            recv_sem=sems.at[1, k],
            device_id=place,
            device_id_type=MESH,
        )

    def along_az(source, target, sems):
        return [
            copy(source.at[0], target.at[0], sems, 0, az=right),
            copy(source.at[1], target.at[1], sems, 1, az=left),
        ]

    def along_ax(up_from, to_low, down_from, to_high, sems):
        return copy(up_from, to_low, sems, 0, ax=upper), copy(down_from, to_high, sems, 1, ax=lower)

    def wide_ax(field, to_low, to_high, sems):
        return along_ax(field.at[:, pl.ds(1, 3)], to_low, field.at[:, pl.ds(0, 3)], to_high, sems)

    def stage(field, staging, fields):
        for f in range(fields):
            for r in range(4):
                staging[0, f * 4 + r, 0:3] = field[f, r, 37:40]
                staging[1, f * 4 + r, 0:3] = field[f, r, 0:3]

    def when_up(action):
        pl.when(row < 3)(action)

    def when_down(action):
        pl.when(row > 0)(action)

    def start_ax(pair):
        when_up(pair[0].start)
        when_down(pair[1].start)

    def sent_ax(pair):
        when_up(pair[0].wait_send)
        when_down(pair[1].wait_send)

    def came_ax(pair):
        when_down(pair[0].wait_recv)
        when_up(pair[1].wait_recv)

    def start_all(items):
        for item in items:
            item.start()

    def came_all(items):
        for item in items:
            item.wait_recv()

    def sent_all(items):
        for item in items:
            item.wait_send()

    padded[...] = jnp.zeros_like(padded)
    padded_flags[...] = jnp.zeros_like(padded_flags)
    loads[0].wait()
    loads[1].wait()
    for v in range(5):
        for r in range(4):
            padded[v, r, 3:43] = state[v, r]
    for s in range(2):
        for r in range(4):
            padded_flags[s, r, 3:43] = flags[s, r].astype(jnp.float32)
    packed = pack_state(padded)
    for r in range(4):
        near[0, 16 * r : 16 * r + 16, :] = packed[32 * r : 32 * r + 16]
        near_outer[0, 8 * r : 8 * r + 8, :] = packed[32 * r + 16 : 32 * r + 24]
        ghost_out[0, r, 0:1, :] = packed[32 * r : 32 * r + 1, :128]
        ghost_out[0, r, 1:2, :] = packed[32 * r : 32 * r + 1, 128:]
    ends_out[0], ends_out[1] = fold_ends([packed[32 * r : 32 * r + 16] for r in range(4)], 256)
    packed = pack_flags(padded_flags)
    for r in range(4):
        marks[0, 16 * r : 16 * r + 16, :] = packed[32 * r : 32 * r + 16]
    mark_ends_out[0], mark_ends_out[1] = fold_ends([packed[32 * r : 32 * r + 16] for r in range(4)], 128)
    ends = along_az(ends_out, ends_in, end_sem)
    mark_ends = along_az(mark_ends_out, mark_ends_in, mark_end_sem)
    rows = along_ax(near.at[0, pl.ds(16, 48)], near_low, near.at[0, pl.ds(0, 48)], near_high, row_sem)
    mark_rows = along_ax(marks.at[0, pl.ds(16, 48)], marks_low, marks.at[0, pl.ds(0, 48)], marks_high, mark_row_sem)
    ghost = copy(ghost_out.at[0], ghost_in.at[0], ghost_sem.at[0], 0, az=opposite)
    stage(state, az_out, 5)
    stage(flags, azf_out, 2)
    az = along_az(az_out, az_in.at[0], az_sem.at[0])
    azf = along_az(azf_out, azf_in, azf_sem)
    ax = wide_ax(state, low.at[0], high.at[0], ax_sem.at[0])
    axf = wide_ax(flags, flow, fhigh, axf_sem)
    pl.semaphore_wait(barrier, 65)
    start_ax(rows)
    start_all(ends)
    ghost.start()
    start_all(mark_ends)
    start_ax(mark_rows)
    start_all(az)
    start_all(azf)
    start_ax(ax)
    start_ax(axf)
    for item in loads[2:]:
        item.wait()
    build_mix(mine, mix_high, mix_low)

    came_all(ends)
    came_all(mark_ends)
    for r in range(4):
        at_row = slice(16 * r, 16 * r + 16)
        near[1, at_row, :] = with_ends(near[0, at_row, :], ends_in[0], ends_in[1], r)
        marks[1, at_row, :] = with_ends(marks[0, at_row, :], mark_ends_in[0], mark_ends_in[1], r)

    def own_state(r):
        return near[1, 16 * r : 16 * r + 16, :]

    def own_marks(r):
        return marks[1, 16 * r : 16 * r + 16, :]

    near_azimuthal(own_state, own_marks, 0, near_rate)
    came_ax(rows)
    came_ax(mark_rows)

    def low_rim():
        for k in range(3):
            near_low[16 * k : 16 * k + 16, :] = near[1, 0:16, :]
            marks_low[16 * k : 16 * k + 16, :] = marks[1, 0:16, :]

    def high_rim():
        for k in range(3):
            near_high[16 * k : 16 * k + 16, :] = near[1, 48:64, :]
            marks_high[16 * k : 16 * k + 16, :] = marks[1, 48:64, :]

    pl.when(row == 0)(low_rim)
    pl.when(row == 3)(high_rim)
    ghost.wait_recv()

    def mark_list():
        below = [marks_low[16 * k : 16 * k + 16, :] for k in range(3)]
        above = [marks_high[16 * k : 16 * k + 16, :] for k in range(3)]
        return below + [own_marks(r) for r in range(4)] + above

    def ghost_row(section):
        return lambda r: jnp.concatenate([ghost_in[section, r, 0:1, :], ghost_in[section, r, 1:2, :]], axis=1)

    def outer_rows(section):
        return lambda r: near_outer[section, 8 * r : 8 * r + 8, :]

    def hand_in(section, r, value):
        send[section, 16 * r : 16 * r + 16, 0, :] = value[:, :128]
        send[section, 16 * r : 16 * r + 16, 1, :] = value[:, 128:]

    def near_first(r, slope, valid):
        hand_in(0, r, jnp.where(valid, own_state(r) + slope * time_step, 0.0))

    near_finish(
        lambda k: near_low[16 * k : 16 * k + 16, :],
        own_state,
        lambda k: near_high[16 * k : 16 * k + 16, :],
        outer_rows(0),
        ghost_row(0),
        mark_list(),
        0,
        near_rate,
        near_first,
    )
    spread(send.at[0], recv.at[0], me, peers, go_sem.at[0, 0], go_sem.at[0, 1])

    sent_ax(rows)
    sent_ax(mark_rows)
    sent_all(ends + mark_ends + [ghost])

    def fill_az(section):
        for v in range(5):
            for r in range(4):
                padded[v, r, 0:3] = az_in[section, 0, v * 4 + r, 0:3]
                padded[v, r, 43:46] = az_in[section, 1, v * 4 + r, 0:3]

    came_all(az)
    came_all(azf)
    fill_az(0)
    for s in range(2):
        for r in range(4):
            padded_flags[s, r, 0:3] = azf_in[0, s * 4 + r, 0:3].astype(jnp.float32)
            padded_flags[s, r, 43:46] = azf_in[1, s * 4 + r, 0:3].astype(jnp.float32)
    azimuthal(padded, padded_flags, 0, rate)
    came_ax(ax)
    came_ax(axf)

    def rims(field, section):
        def low_rim():
            for v in range(5):
                for k in range(3):
                    low[section, v, k] = field[v, 0]

        def high_rim():
            for v in range(5):
                for k in range(3):
                    high[section, v, k] = field[v, 3]

        pl.when(row == 0)(low_rim)
        pl.when(row == 3)(high_rim)

    def flag_low_rim():
        for s in range(2):
            for k in range(3):
                flow[s, k] = flags[s, 0]

    def flag_high_rim():
        for s in range(2):
            for k in range(3):
                fhigh[s, k] = flags[s, 3]

    rims(state, 0)
    pl.when(row == 0)(flag_low_rim)
    pl.when(row == 3)(flag_high_rim)

    def combine_first(v, r, rows, here, slope):
        first[v, r, rows, :] = here + slope * time_step

    finish(state, low.at[0], high.at[0], flags, flow, fhigh, 0, rate, combine_first)
    sent_all(az + azf)
    arrived(recv.at[0], go_sem.at[0, 1])
    project(recv.at[0], back.at[0], me, fwd, inv, twiddle, mix_high, mix_low)
    places = peers + [me]
    owner_row = me // 16
    leads_up, leads_down = (row < 3) & (owner_row > 0), (row > 0) & (owner_row < 3)
    leads_ghost = lax.rem(me, 16) == 0

    def hand_out(places):
        for to in places:
            copy(back.at[0, to], ret.at[0, me], come_sem, 0, az=to).start()

    def hand_up(places):
        for to in places:
            copy(back.at[0, to], near2_low.at[me - 16], near_sem, 0, ax=upper, az=to).start()

    def hand_down(places):
        for to in places:
            copy(back.at[0, to], near2_high.at[me], near_sem, 1, ax=lower, az=to).start()

    def hand_ghost():
        for to in peers:
            copy(back.at[0, lax.rem(to + 32, 64)], ghost_in.at[1, owner_row], ghost_sem.at[1], 0, az=to).start()
        ghost_in[1, pl.ds(owner_row, 1)] = back[0, pl.ds(opposite, 1)]

    hand_out(peers[:32])
    pl.when(leads_up)(lambda: hand_up(places[:32]))
    pl.when(leads_down)(lambda: hand_down(places[:32]))
    hand_out(peers[32:])
    pl.when(leads_up)(lambda: hand_up(places[32:]))
    pl.when(leads_down)(lambda: hand_down(places[32:]))
    pl.when(leads_ghost)(hand_ghost)
    ret[0, pl.ds(me, 1)] = back[0, pl.ds(me, 1)]
    stage(first, az_out, 5)
    az = along_az(az_out, az_in.at[1], az_sem.at[1])
    start_all(az)
    ax2 = wide_ax(first, low.at[1], high.at[1], ax_sem.at[1])
    start_ax(ax2)
    for v in range(5):
        for r in range(4):
            padded[v, r, 3:43] = first[v, r]
    packed = pack_state(padded)
    for r in range(4):
        near_outer[1, 8 * r : 8 * r + 8, :] = packed[32 * r + 16 : 32 * r + 24]
    arrived(ret.at[0], come_sem.at[1, 0])


    def own_first(r):
        return packed_rows(ret.at[0], 16 * r, 16)

    near_azimuthal(own_first, own_marks, 1, near_rate)
    when_down(pltpu.make_async_copy(near2_low, near2_low, near_sem.at[1, 0]).wait)
    when_up(pltpu.make_async_copy(near2_high, near2_high, near_sem.at[1, 1]).wait)

    def low_rim_two():
        for k in range(3):
            near2_low[16 * k : 16 * k + 16] = ret[0, 0:16]

    def high_rim_two():
        for k in range(3):
            near2_high[16 * k : 16 * k + 16] = ret[0, 48:64]

    pl.when(row == 0)(low_rim_two)
    pl.when(row == 3)(high_rim_two)
    mirrored, ghost_arrived = ghost_in.at[1], ghost_sem.at[1, 1, 0]

    def ghost_but_own():
        part = mirrored.at[pl.ds(0, 3)]
        pltpu.make_async_copy(part, part, ghost_arrived).wait()

    pl.when(leads_ghost)(ghost_but_own)
    pl.when(jnp.logical_not(leads_ghost))(pltpu.make_async_copy(mirrored, mirrored, ghost_arrived).wait)

    def near_second(r, slope, valid):
        value = own_state(r) * 0.75 + (own_first(r) + slope * time_step) * 0.25
        hand_in(1, r, jnp.where(valid, value, 0.0))

    near_finish(
        lambda k: packed_rows(near2_low, 16 * k, 16),
        own_first,
        lambda k: packed_rows(near2_high, 16 * k, 16),
        outer_rows(1),
        ghost_row(1),
        mark_list(),
        1,
        near_rate,
        near_second,
    )
    spread(send.at[1], recv.at[1], me, peers, go_sem.at[1, 0], go_sem.at[1, 1])

    inner40 = lanes((40, 128)) < NRING
    sent_ax(ax)
    sent_ax(axf)
    sent_ax(ax2)
    block = unpack(ret.at[0])
    for r in range(4):
        for v in range(5):
            first[v, r] = jnp.where(inner40, block(v, r)[3:43], first[v, r])
    came_all(az)
    sent_all(az)
    fill_az(1)
    azimuthal(padded, padded_flags, 1, rate)
    arrived(recv.at[1], go_sem.at[1, 1])
    project(recv.at[1], back.at[1], me, fwd, inv, twiddle, mix_high, mix_low)
    spread(back.at[1], ret.at[1], me, peers, come_sem.at[0, 1], come_sem.at[1, 1])
    came_ax(ax2)
    rims(first, 1)

    def combine_second(v, r, rows, here, slope):
        second[v, r, rows, :] = state[v, r, rows, :] * 0.75 + (here + slope * time_step) * 0.25

    finish(first, low.at[1], high.at[1], flags, flow, fhigh, 1, rate, combine_second)
    for section in range(2):
        arrived(send.at[section], go_sem.at[section, 0])
    arrived(back.at[0], come_sem.at[0, 0])

    def whole(buffer, s):
        return pltpu.make_async_copy(buffer, buffer, s)

    pl.when(leads_up)(whole(back.at[0], near_sem.at[0, 0]).wait)
    pl.when(leads_down)(whole(back.at[0], near_sem.at[0, 1]).wait)
    pl.when(leads_ghost)(lambda: arrived(back.at[0], ghost_sem.at[1, 0, 0]))
    arrived(ret.at[1], come_sem.at[1, 1])
    block = unpack(ret.at[1])
    for r in range(4):
        for v in range(5):
            out[v, r] = jnp.where(inner40, block(v, r)[3:43], second[v, r])
    arrived(back.at[1], come_sem.at[0, 1])


def local(state, shock_flags):
    fwd, inv, twiddle, band = filter_tables()
    tables = [jnp.stack(split(jnp.asarray(t))) for t in (fwd, inv)]
    tables += [jnp.asarray(twiddle), jnp.asarray(band)]
    vmem = pl.BlockSpec(memory_space=pltpu.VMEM)
    f32, i32 = jnp.float32, jnp.int32
    dma = pltpu.SemaphoreType.DMA
    in_hbm = [pltpu.with_memory_space_constraint(x, pltpu.HBM) for x in (state, shock_flags, *tables)]
    after = pl.pallas_call(
        kernel,
        out_shape=jax.ShapeDtypeStruct(state.shape, f32),
        in_specs=[pl.BlockSpec(memory_space=pltpu.HBM)] * 6,
        out_specs=vmem,
        scratch_shapes=[
            pltpu.VMEM((5, 4, 40, 128), f32),
            pltpu.VMEM((2, 4, 40, 128), i32),
            pltpu.VMEM((2, 80, 64), jnp.bfloat16),
            pltpu.VMEM((2, 64, 80), jnp.bfloat16),
            pltpu.VMEM((4, 40, 256), f32),
            pltpu.VMEM((4, 48, 256), f32),
            pltpu.VMEM((4, 256, 256), jnp.bfloat16),
            pltpu.VMEM((4, 256, 256), jnp.bfloat16),
            pltpu.VMEM((5, 4, 48, 128), f32),
            pltpu.VMEM((2, 4, 48, 128), f32),
            pltpu.VMEM((5, 4, 40, 128), f32),
            pltpu.VMEM((5, 4, 40, 128), f32),
            pltpu.VMEM((5, 4, 40, 128), f32),
            pltpu.VMEM((2, 20, 4, 128), f32),
            pltpu.VMEM((2, 2, 20, 4, 128), f32),
            pltpu.VMEM((2, 8, 4, 128), i32),
            pltpu.VMEM((2, 8, 4, 128), i32),
            pltpu.VMEM((2, 5, 3, 40, 128), f32),
            pltpu.VMEM((2, 5, 3, 40, 128), f32),
            pltpu.VMEM((2, 3, 40, 128), i32),
            pltpu.VMEM((2, 3, 40, 128), i32),
            pltpu.VMEM((2, 64, 256), f32),
            pltpu.VMEM((64, 256), f32),
            pltpu.VMEM((48, 256), f32),
            pltpu.VMEM((48, 256), f32),
            pltpu.VMEM((2, 32, 256), f32),
            pltpu.VMEM((2, 16, 256), f32),
            pltpu.VMEM((2, 16, 256), f32),
            pltpu.VMEM((2, 64, 128), f32),
            pltpu.VMEM((48, 128), f32),
            pltpu.VMEM((48, 128), f32),
            pltpu.VMEM((2, 16, 128), f32),
            pltpu.VMEM((2, 16, 128), f32),
            pltpu.VMEM((2, 4, 2, 128), f32),
            pltpu.VMEM((2, 4, 2, 128), f32),
            pltpu.VMEM((48, 2, 128), f32),
            pltpu.VMEM((48, 2, 128), f32),
            pltpu.VMEM((2, 64, 2, 128), f32),
            pltpu.VMEM((2, 64, 2, 128), f32),
            pltpu.VMEM((2, 64, 2, 128), f32),
            pltpu.VMEM((2, 64, 2, 128), f32),
            dma((6,)),
            dma((2, 2, 2)),
            dma((2, 2)),
            dma((2, 2, 2)),
            dma((2, 2)),
            dma((2, 2)),
            dma((2, 2)),
            dma((2, 2)),
            dma((2, 2)),
            dma((2, 2, 1)),
            dma((2, 2)),
            dma((2, 2)),
            dma((2, 2)),
        ],
        compiler_params=pltpu.CompilerParams(
            collective_id=0, has_side_effects=True, vmem_limit_bytes=40 * 1024 * 1024
        ),
    )(*in_hbm)
    return after - state


def solution(mesh):
    in_specs = (P(None, "ax", "az", None), P(None, "ax", "az", None))
    out_specs = P(None, "ax", "az", None)
    return jax.shard_map(local, mesh=mesh, in_specs=in_specs, out_specs=out_specs, check_vma=False)
```

```python
import math

import jax
import jax.numpy as jnp
import numpy as np
from jax import lax
from jax.experimental import pallas as pl
from jax.experimental.pallas import tpu as pltpu
from jax.sharding import PartitionSpec as P

NRING = 16
MESH = pl.DeviceIdType.MESH

split_speed = 3.0
small_eps = 1e-06
time_step = 0.004


def filter_tables():
    d, k1 = np.arange(64), np.arange(33)
    angle = 2 * np.pi * np.outer(k1, d) / 64
    fwd = np.zeros((80, 64))
    fwd[:33], fwd[40:73] = np.cos(angle), -np.sin(angle)
    inv = np.zeros((64, 80))
    inv[:, :33], inv[:, 40:73] = np.cos(angle.T), -np.sin(angle.T)
    twiddle = np.zeros((4, 40, 256))
    m_in, m_out = np.arange(40), np.arange(-3, 43)
    scale = np.where((k1 == 0) | (k1 == 32), 1.0, 2.0)[:, None] / 2560
    for v in range(5):
        angle = 2 * np.pi * np.outer(k1, m_in) / 2560
        twiddle[0, :33, v * 48 + 3 : v * 48 + 43] = np.cos(angle)
        twiddle[1, :33, v * 48 + 3 : v * 48 + 43] = -np.sin(angle)
        angle = 2 * np.pi * np.outer(k1, m_out) / 2560
        twiddle[2, :33, v * 48 : v * 48 + 46] = np.cos(angle) * scale
        twiddle[3, :33, v * 48 : v * 48 + 46] = np.sin(angle) * scale
    band = np.zeros((16, 4, 48, 256))
    delta = m_out[None, :] - m_in[:, None]
    for j in range(16):
        if j % 2:
            q = (j + 1) // 2
            modes, extra = np.arange(-q, q), -q
        else:
            q = j // 2
            modes, extra = np.arange(-q, q + 1), q
        kept = sum(np.exp(2j * np.pi * k * delta / 40) for k in modes)
        twin = np.exp(2j * np.pi * extra * delta / 40)
        for k, part in enumerate((kept.real, kept.imag, twin.real, twin.imag)):
            band[j, k, 3:43, :46] = part
    return [a.astype(np.float32) for a in (fwd, inv, twiddle, band)]


def split(x):
    high = x.astype(jnp.bfloat16)
    return high, (x - high.astype(jnp.float32)).astype(jnp.bfloat16)


def dot(a, b):
    return jnp.dot(a, b, preferred_element_type=jnp.float32)


def by_left(a_high, a_low, b):
    high, low = split(b)
    return dot(a_high, high) + (dot(a_high, low) + dot(a_low, high))


def by_right(a, b_high, b_low):
    high, low = split(a)
    rows = a.shape[0]
    both = dot(jnp.concatenate([high, low], axis=0), b_high)
    return both[:rows] + (both[rows:] + dot(high, b_low))


def inverse(x):
    return pltpu.reciprocal(x, approx=True)


class Rows:
    def __init__(self, cells):
        self.cells = list(cells)

    def _with(self, other, op):
        if isinstance(other, Rows):
            pairs = zip(self.cells, other.cells)
            return Rows([None if a is None or b is None else op(a, b) for a, b in pairs])
        return Rows([None if a is None else op(a, other) for a in self.cells])

    def __add__(self, other):
        return self._with(other, lambda a, b: a + b)

    def __sub__(self, other):
        return self._with(other, lambda a, b: a - b)

    def __mul__(self, other):
        return self._with(other, lambda a, b: a * b)

    def map(self, op):
        return Rows([None if a is None else op(a) for a in self.cells])

    def shifted(self, by):
        n = len(self.cells)
        return Rows([self.cells[k + by] if 0 <= k + by < n else None for k in range(n)])


def at(x, by):
    if isinstance(x, Rows):
        return x.shifted(by)
    axis = 1 if x.shape[1] == 256 else 0
    n = x.shape[axis]
    return pltpu.roll(x, (n - by) % n, axis)


def inverse_of(x):
    return x.map(inverse) if isinstance(x, Rows) else inverse(x)


def indicators(f):
    d = at(f, 1) - f
    s = d - at(d, -1)
    s_next = at(s, 1)
    e = s - s_next
    h = s * 0.5
    q = s * s * (13.0 / 12.0) + small_eps
    mid = d - h
    up = d + h
    down = mid - s
    x = inverse_of(q + up * up)
    y = inverse_of(q + mid * mid)
    z = inverse_of(q + down * down)
    return d, s, s_next, e, x * x, y * y, z * z


def faces(flux, state, switch, choose):
    half = flux * 0.5
    lift = state * (0.5 * split_speed)
    d_p, s_p, sn_p, e_p, x_p, y_p, z_p = indicators(half + lift)
    zn_p = at(z_p, 1)
    top = at(x_p * e_p, -1) * 2.0 + zn_p * e_p * 3.0
    total = at(x_p, -1) + y_p * 6.0 + zn_p * 3.0
    plus = top * inverse_of(total)
    d_m, s_m, sn_m, e_m, x_m, y_m, z_m = indicators(half - lift)
    zn_m = at(z_m, 1)
    top = at(zn_m * e_m, 1) * 2.0 + x_m * e_m * 3.0
    total = at(zn_m, 1) + at(y_m, 1) * 6.0 + x_m * 3.0
    minus = top * inverse_of(total)
    middle = flux + (d_p + d_m) * 0.5
    own = s_p + sn_m
    weno = (plus - minus - own) * (1.0 / 6.0)
    central = (own + s_m + sn_p) * (-1.0 / 12.0)
    return middle + choose(switch, weno, central)


def pick(switch, a, b):
    if isinstance(a, Rows):
        triples = zip(switch.cells, a.cells, b.cells)
        return Rows([None if s is None or p is None or q is None else jnp.where(s, p, q) for s, p, q in triples])
    return jnp.where(switch, a, b)


def largest(a, b):
    if isinstance(a, Rows):
        return a._with(b, jnp.maximum)
    return jnp.maximum(a, b)


def peak(flags):
    pair = largest(flags, at(flags, 1))
    four = largest(pair, at(pair, 2))
    return at(largest(four, at(pair, 4)), -2)


def window(flags):
    six = peak(flags)
    return six.map(lambda a: a > 0.5) if isinstance(six, Rows) else six > 0.5


def fluxes(u, q, p, component):
    parts = [u[1 + component], u[1] * q, u[2] * q, u[3] * q, (u[4] + p) * q]
    parts[1 + component] = parts[1 + component] + p
    return parts


def pressure(u, inv_rho):
    return (u[4] - (u[1] * u[1] + u[2] * u[2] + u[3] * u[3]) * inv_rho * 0.5) * 0.4


def lanes(shape):
    return lax.broadcasted_iota(jnp.int32, shape, len(shape) - 1)


def radius(rows):
    return lanes((rows, 128)).astype(jnp.float32) + 0.5


def azimuthal(padded, flags, section, rate):
    scale = -1.0 / (radius(40) * (2.0 * math.pi / 2560))

    def row(r, carry):
        u = [padded[v, r] for v in range(5)]
        inv_rho = inverse(u[0])
        q = u[3] * inv_rho
        f = fluxes(u, q, pressure(u, inv_rho), 2)
        switch = window(flags[section, r])
        for v in range(5):
            face = faces(f[v], u[v], switch, pick)
            rate[v, r] = (at(face, 3)[:40] - at(face, 2)[:40]) * scale
        return carry

    lax.fori_loop(0, 4, row, 0)


def finish(own, low, high, flags, flags_low, flags_high, section, rate, combine):
    inv_r = 1.0 / radius(8)
    lane = lanes((8, 128))

    def chunk(c, carry):
        at8 = pl.ds(pl.multiple_of(c * 8, 8), 8)
        u = [
            Rows(
                [low[v, k, at8, :] for k in range(3)]
                + [own[v, k, at8, :] for k in range(4)]
                + [high[v, k, at8, :] for k in range(3)]
            )
            for v in range(5)
        ]
        marks = Rows(
            [flags_low[section, k, at8, :] for k in range(3)]
            + [flags[section, k, at8, :] for k in range(4)]
            + [flags_high[section, k, at8, :] for k in range(3)]
        ).map(lambda a: a.astype(jnp.float32))
        switch = window(marks)
        inv_rho = u[0].map(inverse)
        p = pressure(u, inv_rho)
        f = fluxes(u, u[1] * inv_rho, p, 0)
        radial, source = [], []
        for r in range(4):
            here = [u[v].cells[3 + r] for v in range(5)]
            inv_here, p_here = inv_rho.cells[3 + r], p.cells[3 + r]
            g = fluxes(here, here[2] * inv_here, p_here, 1)
            swirl = here[3] * inv_here
            extra = [None, None, here[3] * swirl + p_here, -here[2] * swirl, None]
            terms = []
            for v in range(5):
                before = pltpu.roll(g[v], 1, 1)
                after = jnp.where(lane == 127, g[v], pltpu.roll(g[v], 127, 1))
                away = g[v] if extra[v] is None else g[v] - extra[v]
                terms.append((after - before) * 0.5 + away * inv_r)
            radial.append(terms)
        for v in range(5):
            face = faces(f[v], u[v], switch, pick).cells
            for r in range(4):
                slope = rate[v, r, at8, :] - (face[3 + r] - face[2 + r]) - radial[r][v]
                combine(v, r, at8, u[v].cells[3 + r], slope)
        return carry

    lax.fori_loop(0, 5, chunk, 0)


def cell_of(width):
    return lax.rem(lanes((16, width)), 48)


def side_by_side(blocks):
    lane = lanes(blocks[0].shape)
    packed = blocks[0]
    for r in range(1, 4):
        packed = jnp.where(lane >= 32 * r, pltpu.roll(blocks[r], 32 * r, 1), packed)
    return packed


def pack_state(padded):
    stacks = []
    for r in range(4):
        rest = jnp.zeros((16, 128), jnp.float32)
        stacks.append(jnp.concatenate([padded[v, r] for v in range(5)] + [rest], axis=0))
    return jnp.transpose(side_by_side(stacks))


def pack_flags(padded_flags):
    stacks = []
    for r in range(4):
        rest = jnp.zeros((32, 128), jnp.float32)
        stacks.append(jnp.concatenate([padded_flags[0, r], padded_flags[1, r], rest], axis=0))
    return jnp.transpose(side_by_side(stacks))


def fold_ends(blocks, width):
    cell = cell_of(width)
    to_right = jnp.zeros((16, width), jnp.float32)
    to_left = to_right
    for r in range(4):
        moved = pltpu.roll(blocks[r], (width - 40 + 3 * r) % width, 1)
        to_right = jnp.where((cell >= 3 * r) & (cell < 3 * r + 3), moved, to_right)
        moved = pltpu.roll(blocks[r], 31 + 3 * r, 1)
        to_left = jnp.where((cell >= 34 + 3 * r) & (cell < 37 + 3 * r), moved, to_left)
    return to_right, to_left


def with_ends(block, from_left, from_right, r):
    width = block.shape[1]
    cell = cell_of(width)
    before = pltpu.roll(from_left, width - 3 * r, 1) if r else from_left
    after = pltpu.roll(from_right, 9 - 3 * r, 1) if r < 3 else from_right
    return jnp.where(cell < 3, before, jnp.where(cell < 43, block, jnp.where(cell < 46, after, 0.0)))


def replicate(x):
    x = jnp.where(lanes(x.shape) < 48, x, 0.0)
    one = jnp.concatenate([x, jnp.zeros_like(x)], axis=1)
    two = one + pltpu.roll(one, 48, 1)
    four = two + pltpu.roll(two, 96, 1)
    return four + pltpu.roll(one, 192, 1)


def primitives(u):
    parts = [u[:, :128]] + [pltpu.roll(u, 256 - 48 * k, 1)[:, :128] for k in range(1, 5)]
    inv_rho = inverse(parts[0])
    return parts, inv_rho, pressure(parts, inv_rho)


def slot(shape, k):
    lane = lanes(shape)
    return (lane >= 48 * k) & (lane < 48 * k + 48)


def packed_flux(u, q, p, component):
    own, energy = slot(u.shape, 1 + component), slot(u.shape, 4)
    return u * q + jnp.where(own, p, jnp.where(energy, p * q, 0.0))


def near_azimuthal(own, marks, section, rate):
    for r in range(4):
        u = own(r)
        parts, inv_rho, p = primitives(u)
        q = replicate(parts[3] * inv_rho)
        f = packed_flux(u, q, replicate(p), 2)
        mark = marks(r)
        switch = window(replicate(pltpu.roll(mark, 80, 1) if section else mark))
        face = faces(f, u, switch, pick)
        cycle = lax.broadcasted_iota(jnp.int32, (16, 256), 0).astype(jnp.float32) + 0.5
        rate[16 * r : 16 * r + 16, :] = (at(face, -1) - face) * (1.0 / (cycle * (2.0 * math.pi / 2560)))


def near_finish(low, own, high, outer, ghost, marks, section, rate, combine):
    blocks = [low(k) for k in range(3)] + [own(r) for r in range(4)] + [high(k) for k in range(3)]
    f, switches, radial = [], [], []
    for k, u in enumerate(blocks):
        parts, inv_rho, p = primitives(u)
        wide_p = replicate(p)
        f.append(packed_flux(u, replicate(parts[1] * inv_rho), wide_p, 0))
        mark = marks[k]
        switches.append(replicate(pltpu.roll(mark, 80, 1) if section else mark))
        if 3 <= k < 7:
            r = k - 3
            beyond = outer(r)
            row = lax.broadcasted_iota(jnp.int32, (8, 256), 0)
            negated = slot((8, 256), 2) | slot((8, 256), 3)
            mirror = jnp.broadcast_to(ghost(r), (8, 256))
            mirror = jnp.where(negated, -mirror, mirror)
            beyond = jnp.where(row == 7, mirror, beyond)
            b_parts, b_inv, b_p = primitives(beyond)
            g_beyond = packed_flux(beyond, replicate(b_parts[2] * b_inv), replicate(b_p), 1)
            g = packed_flux(u, replicate(parts[2] * inv_rho), wide_p, 1)
            q_t = replicate(parts[3] * inv_rho)
            extra = jnp.where(
                slot((16, 256), 2),
                pltpu.roll(u, 256 - 48, 1) * q_t + wide_p,
                jnp.where(slot((16, 256), 3), -pltpu.roll(u, 48, 1) * q_t, 0.0),
            )
            ring = jnp.concatenate([g, g_beyond], axis=0)
            after, before = pltpu.roll(ring, 23, 0)[:16], pltpu.roll(ring, 1, 0)[:16]
            cycle = lax.broadcasted_iota(jnp.int32, (16, 256), 0).astype(jnp.float32) + 0.5
            radial.append((after - before) * 0.5 + (g - extra) * (1.0 / cycle))
    slopes = [[[None, None], [None, None]] for _ in range(4)]
    for h in range(2):
        for w in range(2):
            part = (slice(8 * h, 8 * h + 8), slice(128 * w, 128 * w + 128))
            face = faces(
                Rows([x[part] for x in f]),
                Rows([x[part] for x in blocks]),
                window(Rows([x[part] for x in switches])),
                pick,
            ).cells
            for r in range(4):
                slopes[r][h][w] = face[2 + r] - face[3 + r]
    lane = lanes((16, 256))
    cell = lax.rem(lane, 48)
    valid = (cell >= 3) & (cell < 43) & (lane < 240)
    for r in range(4):
        rows = [jnp.concatenate(pair, axis=1) for pair in slopes[r]]
        slope = jnp.concatenate(rows, axis=0) - radial[r] + rate[16 * r : 16 * r + 16, :]
        combine(r, jnp.where(valid, slope, 0.0), valid)


def packed_rows(ref, first, count):
    rows = pl.ds(first, count)
    return jnp.concatenate([ref[rows, 0, :], ref[rows, 1, :]], axis=1)


def place_of(r, group):
    return 32 * (r % 2) + 8 * (r // 2 + 2 * group)


def build_selectors(apart, copies):
    to, source = lanes((256, 640)), lax.broadcasted_iota(jnp.int32, (256, 640), 0)
    cell = lax.rem(to, 128)
    hit = (cell < 48) & (source == cell + 48 * (to // 128))
    apart[...] = jnp.where(hit, 1.0, 0.0).astype(jnp.bfloat16)
    to, source = lanes((128, 256)), lax.broadcasted_iota(jnp.int32, (128, 256), 0)
    hit = (source == lax.rem(to, 48)) & (to < 240)
    copies[...] = jnp.where(hit, 1.0, 0.0).astype(jnp.bfloat16)


def select(values, selector):
    high, low = split(values)
    both = dot(jnp.concatenate([high, low], axis=0), selector)
    n = values.shape[0]
    return both[:n] + both[n:]


def line_rates(own_line, lines, extra, cycle, target, apart, copies):
    lane = lanes((16, 256))
    cell = lax.rem(lane, 48)
    valid = (cell >= 3) & (cell < 43) & (lane < 240)
    radius_here = jnp.full((16, 256), cycle, jnp.int32).astype(jnp.float32) + 0.5
    inv_r = 1.0 / radius_here
    inv_rh = 1.0 / (radius_here * (2.0 * math.pi / 2560))

    def chunk(c):
        first = c * 16
        own = packed_rows(own_line, first, 16)
        blocks = [packed_rows(lines.at[k], first, 16) for k in range(3)] + [own]
        blocks += [packed_rows(lines.at[k], first, 16) for k in range(3, 6)]
        blocks += [packed_rows(lines.at[k], first, 16) for k in (6, 7)]
        apart_parts = select(jnp.concatenate(blocks, axis=0), apart[...])
        parts = [apart_parts[:, 128 * k : 128 * k + 128] for k in range(5)]
        inv_rho = inverse(jnp.where(parts[0] == 0.0, 1.0, parts[0]))
        p = pressure(parts, inv_rho)
        q_x, q_r, q_t = [parts[k] * inv_rho for k in (1, 2, 3)]
        stacked = jnp.concatenate([p, q_x[:112], q_r[48:64], q_r[112:], q_t[48:64]], axis=0)
        spread_out = select(stacked, copies[...])
        wide = [spread_out[16 * k : 16 * k + 16] for k in range(20)]
        wide_p = wide[:9]
        f = [packed_flux(blocks[k], wide[9 + k], wide_p[k], 0) for k in range(7)]
        q_r, q_t = wide[16], wide[19]
        g = packed_flux(own, q_r, wide_p[3], 1)
        turn = packed_flux(own, q_t, wide_p[3], 2)
        drag = jnp.where(
            slot((16, 256), 2),
            pltpu.roll(own, 256 - 48, 1) * q_t + wide_p[3],
            jnp.where(slot((16, 256), 3), -pltpu.roll(own, 48, 1) * q_t, 0.0),
        )
        sides = [packed_flux(blocks[7 + k], wide[17 + k], wide_p[7 + k], 1) for k in range(2)]
        blocks = blocks[:7]
        rows = pl.ds(first, 16)
        marks = jnp.concatenate([extra[rows, 2, :], extra[rows, 3, :]], axis=1)
        marks = [marks, pltpu.roll(marks, 256 - 48, 1), pltpu.roll(marks, 256 - 96, 1)]
        marks = jnp.concatenate([m[:, :128] for m in marks], axis=0).astype(jnp.bfloat16)
        marks = dot(marks, copies[...]) > 0.5
        below, above, around = marks[:16], marks[16:32], marks[32:]
        halves = []
        for h in range(2):
            pair = []
            for w in range(2):
                part = (slice(8 * h, 8 * h + 8), slice(128 * w, 128 * w + 128))
                face = faces(
                    Rows([x[part] for x in f]),
                    Rows([x[part] for x in blocks]),
                    Rows([None, None, below[part], above[part], None, None, None]),
                    pick,
                ).cells
                pair.append(face[2] - face[3])
            halves.append(jnp.concatenate(pair, axis=1))
        face = faces(turn, own, around, pick)
        slope = jnp.concatenate(halves, axis=0) + (at(face, -1) - face) * inv_rh
        slope = slope - ((sides[1] - sides[0]) * 0.5 + (g - drag) * inv_r)
        before = jnp.concatenate([extra[rows, 0, :], extra[rows, 1, :]], axis=1)
        value = jnp.where(valid, before * 0.75 + (own + slope * time_step) * 0.25, 0.0)
        target[rows, 0, :] = value[:, :128]
        target[rows, 1, :] = value[:, 128:]

    for c in range(4):
        chunk(c)


def unpack(rows):
    n = rows.shape[0]
    turned = jnp.transpose(jnp.concatenate([rows, jnp.zeros((128 - n, 256), jnp.float32)], axis=0))

    def block(v, k):
        cells = turned[48 * v : 48 * v + 48]
        return pltpu.roll(cells, (128 - k) % 128, 1) if k % 128 else cells

    return block


def others(me):
    y, x, z = me // 32, lax.rem(me // 8, 4), lax.rem(me, 8)
    ys = {d: lax.rem(y + d, 2) * 32 for d in (1, 0)}
    xs = {d: lax.rem(x + d, 4) * 8 for d in (2, 1, 3, 0)}
    zs = {d: lax.rem(z + d, 8) for d in (4, 3, 5, 2, 6, 1, 7, 0)}
    steps = [(dy, dx, dz) for dz in zs for dx in xs for dy in ys]
    steps.sort(key=lambda s: -(s[0] + min(s[1], 4 - s[1]) + min(s[2], 8 - s[2])))
    return [ys[dy] + xs[dx] + zs[dz] for dy, dx, dz in steps[:-1]]


def spread(send, recv, me, peers, send_sem, recv_sem):
    for to in peers:
        pltpu.make_async_remote_copy(
            src_ref=send.at[to],
            dst_ref=recv.at[me],
            send_sem=send_sem,
            recv_sem=recv_sem,
            device_id={"az": to},
            device_id_type=MESH,
        ).start()
    recv[pl.ds(me, 1)] = send[pl.ds(me, 1)]


def arrived(buffer, sem):
    rows = buffer.at[pl.ds(0, 63)]
    pltpu.make_async_copy(rows, rows, sem).wait()


def build_mix(mine, mix_high, mix_low):
    mix_high[...] = jnp.zeros_like(mix_high)
    mix_low[...] = jnp.zeros_like(mix_low)
    for k in range(4):
        rows = []
        for v in range(5):
            rows.append(pltpu.roll(mine[k], 48 * v, 1) if v else mine[k])
        rows.append(jnp.zeros((16, 256), jnp.float32))
        mix_high[k], mix_low[k] = split(jnp.concatenate(rows, axis=0))


def project(recv, back, me, fwd, inv, twiddle, mix_high, mix_low):
    x = jnp.concatenate([recv[:, 0, :], recv[:, 1, :]], axis=1)
    a = by_left(fwd[0], fwd[1], x)
    re, im = a[:40], a[40:]
    re, im = re * twiddle[0] - im * twiddle[1], re * twiddle[1] + im * twiddle[0]
    odd = lax.rem(me, 2) == 1
    first_row = lax.broadcasted_iota(jnp.int32, (8, 256), 0) == 0

    def twin_row(x):
        return jnp.where(first_row, jnp.where(odd, x[:8], x[32:40]), 0.0)

    main = jnp.concatenate([re, im], axis=0)
    twin = jnp.concatenate([twin_row(re), twin_row(im)], axis=0)
    c, s = by_right(main, mix_high[0], mix_low[0]), by_right(main, mix_high[1], mix_low[1])
    tc, ts = by_right(twin, mix_high[2], mix_low[2]), by_right(twin, mix_high[3], mix_low[3])
    re, im = c[:40] - s[40:], s[:40] + c[40:]
    t_re, t_im = tc[:8] - ts[8:], ts[:8] + tc[8:]

    def with_twin(x, t):
        top = x[:8] + jnp.where(odd, t, 0.0)
        return jnp.concatenate([top, x[8:32], x[32:40] + jnp.where(odd, 0.0, t)], axis=0)

    re, im = with_twin(re, t_re), with_twin(im, t_im)
    re, im = re * twiddle[2] - im * twiddle[3], re * twiddle[3] + im * twiddle[2]
    y = by_left(inv[0], inv[1], jnp.concatenate([re, im], axis=0))
    back[:, 0, :] = y[:, :128]
    back[:, 1, :] = y[:, 128:]


def kernel(
    state_hbm, flags_hbm, fwd_hbm, inv_hbm, twiddle_hbm, band, out,
    state, flags, fwd, inv, twiddle, mine, mix_high, mix_low, padded, padded_flags, rate, first, second,
    az_out, az_in, azf_out, azf_in, low, high, flow, fhigh,
    near, near_rate, near_low, near_high, near_outer, ends_out, ends_in, marks, marks_low, marks_high,
    mark_ends_out, mark_ends_in, ghost_out, ghost_in,
    send, recv, back, ret, lines, extra_out, extra_in, outer_out, rim_in, apart, copies,
    sem, az_sem, azf_sem, ax_sem, axf_sem, end_sem, mark_end_sem, row_sem, mark_row_sem, ghost_sem,
    go_sem, come_sem, line_sem, extra_sem, outer_sem, rim_sem,
):
    me, row = lax.axis_index("az"), lax.axis_index("ax")
    right, left = lax.rem(me + 1, 64), lax.rem(me + 63, 64)
    upper, lower = lax.rem(row + 1, 4), lax.rem(row + 3, 4)
    opposite = lax.rem(me + 32, 64)
    z, x, y = lax.rem(me, 8), lax.rem(me // 8, 4), me // 32
    level, cycle = y + 2 * lax.rem(x, 2), 8 * (x // 2) + z
    pairs = [
        (state_hbm, state),
        (flags_hbm, flags),
        (fwd_hbm, fwd),
        (inv_hbm, inv),
        (twiddle_hbm, twiddle),
        (band.at[cycle], mine),
    ]
    loads = [pltpu.make_async_copy(a, b, sem.at[k]) for k, (a, b) in enumerate(pairs)]
    for item in loads:
        item.start()
    barrier = pltpu.get_barrier_semaphore()
    peers = others(me)
    for peer in peers:
        pl.semaphore_signal(barrier, inc=1, device_id={"az": peer}, device_id_type=MESH)
    for peer in (upper, lower):
        pl.semaphore_signal(barrier, inc=1, device_id={"ax": peer}, device_id_type=MESH)

    def copy(src, dst, sems, k, **place):
        return pltpu.make_async_remote_copy(
            src_ref=src,
            dst_ref=dst,
            send_sem=sems.at[0, k],
            recv_sem=sems.at[1, k],
            device_id=place,
            device_id_type=MESH,
        )

    def along_az(source, target, sems):
        return [
            copy(source.at[0], target.at[0], sems, 0, az=right),
            copy(source.at[1], target.at[1], sems, 1, az=left),
        ]

    def along_ax(up_from, to_low, down_from, to_high, sems):
        return copy(up_from, to_low, sems, 0, ax=upper), copy(down_from, to_high, sems, 1, ax=lower)

    def wide_ax(field, to_low, to_high, sems):
        return along_ax(field.at[:, pl.ds(1, 3)], to_low, field.at[:, pl.ds(0, 3)], to_high, sems)

    def stage(field, staging, fields):
        for f in range(fields):
            for r in range(4):
                staging[0, f * 4 + r, 0:3] = field[f, r, 37:40]
                staging[1, f * 4 + r, 0:3] = field[f, r, 0:3]

    def when_up(action):
        pl.when(row < 3)(action)

    def when_down(action):
        pl.when(row > 0)(action)

    def start_ax(pair):
        when_up(pair[0].start)
        when_down(pair[1].start)

    def sent_ax(pair):
        when_up(pair[0].wait_send)
        when_down(pair[1].wait_send)

    def came_ax(pair):
        when_down(pair[0].wait_recv)
        when_up(pair[1].wait_recv)

    def start_all(items):
        for item in items:
            item.start()

    def came_all(items):
        for item in items:
            item.wait_recv()

    def sent_all(items):
        for item in items:
            item.wait_send()

    padded[...] = jnp.zeros_like(padded)
    padded_flags[...] = jnp.zeros_like(padded_flags)
    loads[0].wait()
    loads[1].wait()
    for v in range(5):
        for r in range(4):
            padded[v, r, 3:43] = state[v, r]
    for s in range(2):
        for r in range(4):
            padded_flags[s, r, 3:43] = flags[s, r].astype(jnp.float32)
    packed = pack_state(padded)
    for r in range(4):
        near[0, 16 * r : 16 * r + 16, :] = packed[32 * r : 32 * r + 16]
        near_outer[0, 8 * r : 8 * r + 8, :] = packed[32 * r + 16 : 32 * r + 24]
        ghost_out[0, r, 0:1, :] = packed[32 * r : 32 * r + 1, :128]
        ghost_out[0, r, 1:2, :] = packed[32 * r : 32 * r + 1, 128:]
    ends_out[0], ends_out[1] = fold_ends([packed[32 * r : 32 * r + 16] for r in range(4)], 256)
    packed = pack_flags(padded_flags)
    for r in range(4):
        marks[0, 16 * r : 16 * r + 16, :] = packed[32 * r : 32 * r + 16]
    mark_ends_out[0], mark_ends_out[1] = fold_ends([packed[32 * r : 32 * r + 16] for r in range(4)], 128)
    ends = along_az(ends_out, ends_in, end_sem)
    mark_ends = along_az(mark_ends_out, mark_ends_in, mark_end_sem)
    rows = along_ax(near.at[0, pl.ds(16, 48)], near_low, near.at[0, pl.ds(0, 48)], near_high, row_sem)
    mark_rows = along_ax(marks.at[0, pl.ds(16, 48)], marks_low, marks.at[0, pl.ds(0, 48)], marks_high, mark_row_sem)
    ghost = copy(ghost_out.at[0], ghost_in.at[0], ghost_sem.at[0], 0, az=opposite)
    stage(state, az_out, 5)
    stage(flags, azf_out, 2)
    az = along_az(az_out, az_in.at[0], az_sem.at[0])
    azf = along_az(azf_out, azf_in, azf_sem)
    ax = wide_ax(state, low.at[0], high.at[0], ax_sem.at[0])
    axf = wide_ax(flags, flow, fhigh, axf_sem)
    pl.semaphore_wait(barrier, 65)
    start_ax(rows)
    start_all(ends)
    ghost.start()
    start_all(mark_ends)
    start_ax(mark_rows)
    start_all(az)
    start_all(azf)
    start_ax(ax)
    start_ax(axf)
    for item in loads[2:]:
        item.wait()
    build_mix(mine, mix_high, mix_low)
    build_selectors(apart, copies)

    came_all(ends)
    came_all(mark_ends)
    for r in range(4):
        at_row = slice(16 * r, 16 * r + 16)
        near[1, at_row, :] = with_ends(near[0, at_row, :], ends_in[0], ends_in[1], r)
        marks[1, at_row, :] = with_ends(marks[0, at_row, :], mark_ends_in[0], mark_ends_in[1], r)

    def own_state(r):
        return near[1, 16 * r : 16 * r + 16, :]

    def own_marks(r):
        return marks[1, 16 * r : 16 * r + 16, :]

    near_azimuthal(own_state, own_marks, 0, near_rate)
    came_ax(rows)
    came_ax(mark_rows)

    def low_rim():
        for k in range(3):
            near_low[16 * k : 16 * k + 16, :] = near[1, 0:16, :]
            marks_low[16 * k : 16 * k + 16, :] = marks[1, 0:16, :]

    def high_rim():
        for k in range(3):
            near_high[16 * k : 16 * k + 16, :] = near[1, 48:64, :]
            marks_high[16 * k : 16 * k + 16, :] = marks[1, 48:64, :]

    pl.when(row == 0)(low_rim)
    pl.when(row == 3)(high_rim)
    ghost.wait_recv()

    def mark_list():
        below = [marks_low[16 * k : 16 * k + 16, :] for k in range(3)]
        above = [marks_high[16 * k : 16 * k + 16, :] for k in range(3)]
        return below + [own_marks(r) for r in range(4)] + above

    def ghost_row(section):
        return lambda r: jnp.concatenate([ghost_in[section, r, 0:1, :], ghost_in[section, r, 1:2, :]], axis=1)

    def outer_rows(section):
        return lambda r: near_outer[section, 8 * r : 8 * r + 8, :]

    def hand_in(section, r, value):
        for group in range(2):
            first_place = place_of(r, group)
            for h in range(2):
                part = value[8 * group : 8 * group + 8, 128 * h : 128 * h + 128]
                send[section, first_place : first_place + 8, h, :] = part

    def near_first(r, slope, valid):
        hand_in(0, r, jnp.where(valid, own_state(r) + slope * time_step, 0.0))

    near_finish(
        lambda k: near_low[16 * k : 16 * k + 16, :],
        own_state,
        lambda k: near_high[16 * k : 16 * k + 16, :],
        outer_rows(0),
        ghost_row(0),
        mark_list(),
        0,
        near_rate,
        near_first,
    )
    spread(send.at[0], recv.at[0], me, peers, go_sem.at[0, 0], go_sem.at[0, 1])

    tall = Rows(mark_list()).map(lambda a: replicate(pltpu.roll(a, 80, 1)))
    axial_marks = peak(tall).cells
    for r in range(4):
        low_part, high_part, turn_part = axial_marks[2 + r], axial_marks[3 + r], peak(tall.cells[3 + r])
        own_slot = [slot((16, 256), k) for k in range(3)]
        row_marks = jnp.where(own_slot[1], high_part, jnp.where(own_slot[2], turn_part, 0.0))
        row_marks = jnp.where(own_slot[0], low_part, row_marks)
        whole_row = [own_state(r)[:, :128], own_state(r)[:, 128:], row_marks[:, :128], row_marks[:, 128:]]
        for group in range(2):
            first_place = place_of(r, group)
            for k in range(4):
                extra_out[first_place : first_place + 8, k, :] = whole_row[k][8 * group : 8 * group + 8]
    spread(extra_out, extra_in, me, peers, extra_sem.at[0], extra_sem.at[1])

    sent_ax(rows)
    sent_ax(mark_rows)
    sent_all(ends + mark_ends + [ghost])

    def fill_az(section):
        for v in range(5):
            for r in range(4):
                padded[v, r, 0:3] = az_in[section, 0, v * 4 + r, 0:3]
                padded[v, r, 43:46] = az_in[section, 1, v * 4 + r, 0:3]

    came_all(az)
    came_all(azf)
    fill_az(0)
    for s in range(2):
        for r in range(4):
            padded_flags[s, r, 0:3] = azf_in[0, s * 4 + r, 0:3].astype(jnp.float32)
            padded_flags[s, r, 43:46] = azf_in[1, s * 4 + r, 0:3].astype(jnp.float32)
    azimuthal(padded, padded_flags, 0, rate)
    came_ax(ax)
    came_ax(axf)

    def rims(field, section):
        def low_rim():
            for v in range(5):
                for k in range(3):
                    low[section, v, k] = field[v, 0]

        def high_rim():
            for v in range(5):
                for k in range(3):
                    high[section, v, k] = field[v, 3]

        pl.when(row == 0)(low_rim)
        pl.when(row == 3)(high_rim)

    def flag_low_rim():
        for s in range(2):
            for k in range(3):
                flow[s, k] = flags[s, 0]

    def flag_high_rim():
        for s in range(2):
            for k in range(3):
                fhigh[s, k] = flags[s, 3]

    rims(state, 0)
    pl.when(row == 0)(flag_low_rim)
    pl.when(row == 3)(flag_high_rim)

    def combine_first(v, r, rows, here, slope):
        first[v, r, rows, :] = here + slope * time_step

    finish(state, low.at[0], high.at[0], flags, flow, fhigh, 0, rate, combine_first)
    sent_all(az + azf)
    for v in range(5):
        for r in range(4):
            padded[v, r, 3:43] = first[v, r]
    packed = pack_state(padded)
    for r in range(4):
        outer_out[r, 0:1, :] = packed[32 * r + 16 : 32 * r + 17, :128]
        outer_out[r, 1:2, :] = packed[32 * r + 16 : 32 * r + 17, 128:]
    for r in range(4):
        last = place_of(r, 1) + 7
        beyond = copy(outer_out.at[r], lines.at[7, me], outer_sem, 0, az=last)
        pl.when(me != last)(beyond.start)
    is_last, is_first = cycle == 15, cycle == 0

    def keep_outer():
        lines[7, pl.ds(me, 1)] = outer_out[pl.ds(level, 1)]

    pl.when(is_last)(keep_outer)
    stage(first, az_out, 5)
    az = along_az(az_out, az_in.at[1], az_sem.at[1])
    start_all(az)
    arrived(recv.at[0], go_sem.at[0, 1])
    project(recv.at[0], back.at[0], me, fwd, inv, twiddle, mix_high, mix_low)

    column = 16 * (x // 2) + z
    meets = []
    for step in range(1, 4):
        over, under = level + step, level + 4 - step
        to_row, to_level = row + over // 4, lax.rem(over, 4)
        to = 32 * lax.rem(to_level, 2) + 8 * (to_level // 2) + column
        item = copy(back.at[0], lines.at[3 - step], line_sem, 3 - step, ax=to_row, az=to)
        has_over, has_under = (row < 3) | (over < 4), (row > 0) | (under >= 4)
        meets.append((item, has_over, has_under))
        to_row, to_level = row - 1 + under // 4, lax.rem(under, 4)
        to = 32 * lax.rem(to_level, 2) + 8 * (to_level // 2) + column
        item = copy(back.at[0], lines.at[2 + step], line_sem, 2 + step, ax=to_row, az=to)
        meets.append((item, has_under, has_over))
    base = 32 * lax.rem(level, 2) + 8 * (level // 2)
    ahead, behind = cycle + 1, cycle + 15
    to = base + 16 * (ahead // 8) + lax.rem(ahead, 8)
    item = copy(back.at[0], lines.at[6], line_sem, 6, az=to)
    not_first, not_last = jnp.logical_not(is_first), jnp.logical_not(is_last)
    meets.append((item, not_last, not_first))
    behind = lax.rem(behind, 16)
    to = base + 16 * (behind // 8) + lax.rem(behind, 8)
    item = copy(back.at[0], lines.at[7], line_sem, 7, az=to)
    meets.append((item, not_first, not_last))
    for item, sends, _ in meets:
        pl.when(sends)(item.start)

    def hand_rim():
        for to in peers:
            copy(back.at[0, to], rim_in.at[level], rim_sem, 0, az=to).start()
        rim_in[pl.ds(level, 1)] = back[0, pl.ds(me, 1)]

    pl.when(is_last)(hand_rim)

    def mirror():
        lane = lanes((64, 128))
        for h in range(2):
            flipped = (lane + 128 * h >= 96) & (lane + 128 * h < 192)
            turned = jnp.concatenate([back[0, 32:64, h, :], back[0, 0:32, h, :]], axis=0)
            lines[6, :, h, :] = jnp.where(flipped, -turned, turned)

    pl.when(is_first)(mirror)
    arrived(extra_in, extra_sem.at[1])
    for item, _, comes in meets:
        pl.when(comes)(item.wait_recv)
    pl.when(is_last)(lambda: arrived(lines.at[7], outer_sem.at[1, 0]))
    for r in range(3):

        def clamp_low():
            for step in range(r + 1, 4):
                lines[3 - step] = lines[3 - r] if r else back[0]

        def clamp_high():
            for step in range(r + 1, 4):
                lines[2 + step] = lines[2 + r] if r else back[0]

        pl.when((row == 0) & (level == r))(clamp_low)
        pl.when((row == 3) & (level == 3 - r))(clamp_high)
    ax2 = wide_ax(first, low.at[1], high.at[1], ax_sem.at[1])
    start_ax(ax2)
    line_rates(back.at[0], lines, extra_in, cycle, recv.at[1], apart, copies)
    project(recv.at[1], back.at[1], me, fwd, inv, twiddle, mix_high, mix_low)
    spread(back.at[1], ret, me, peers, come_sem.at[0], come_sem.at[1])

    sent_ax(ax)
    sent_ax(axf)
    came_all(az)
    sent_all(az)
    fill_az(1)
    azimuthal(padded, padded_flags, 1, rate)
    sent_ax(ax2)
    came_ax(ax2)
    rims(first, 1)

    def rim_but_own():
        part = rim_in.at[pl.ds(0, 3)]
        pltpu.make_async_copy(part, part, rim_sem.at[1, 0]).wait()

    pl.when(is_last)(rim_but_own)
    pl.when(not_last)(pltpu.make_async_copy(rim_in, rim_in, rim_sem.at[1, 0]).wait)
    block = unpack(jnp.concatenate([packed_rows(rim_in, 0, 4), jnp.zeros((4, 256), jnp.float32)], axis=0))
    lane40 = lanes((40, 128))
    for r in range(4):
        for v in range(5):
            first[v, r] = jnp.where(lane40 == 15, block(v, r - 15)[3:43], first[v, r])

    def combine_second(v, r, rows, here, slope):
        second[v, r, rows, :] = state[v, r, rows, :] * 0.75 + (here + slope * time_step) * 0.25

    finish(first, low.at[1], high.at[1], flags, flow, fhigh, 1, rate, combine_second)
    arrived(send.at[0], go_sem.at[0, 0])
    arrived(extra_out, extra_sem.at[0])
    for item, sends, _ in meets:
        pl.when(sends)(item.wait_send)
    pl.when(is_last)(lambda: arrived(back.at[0], rim_sem.at[0, 0]))

    def outers(n):
        part = outer_out.at[pl.ds(0, n)]
        pltpu.make_async_copy(part, part, outer_sem.at[0, 0]).wait()

    pl.when(is_last)(lambda: outers(3))
    pl.when(not_last)(lambda: outers(4))
    arrived(ret, come_sem.at[1])
    order = [packed_rows(ret, place_of(r, group), 8) for r in range(4) for group in range(2)]
    block = unpack(jnp.concatenate(order, axis=0))
    for r in range(4):
        for v in range(5):
            out[v, r] = jnp.where(lane40 < NRING, block(v, 16 * r)[3:43], second[v, r])
    arrived(back.at[1], come_sem.at[0])


def local(state, shock_flags):
    fwd, inv, twiddle, band = filter_tables()
    tables = [jnp.stack(split(jnp.asarray(t))) for t in (fwd, inv)]
    tables += [jnp.asarray(twiddle), jnp.asarray(band)]
    vmem = pl.BlockSpec(memory_space=pltpu.VMEM)
    f32, i32 = jnp.float32, jnp.int32
    dma = pltpu.SemaphoreType.DMA
    in_hbm = [pltpu.with_memory_space_constraint(x, pltpu.HBM) for x in (state, shock_flags, *tables)]
    after = pl.pallas_call(
        kernel,
        out_shape=jax.ShapeDtypeStruct(state.shape, f32),
        in_specs=[pl.BlockSpec(memory_space=pltpu.HBM)] * 6,
        out_specs=vmem,
        scratch_shapes=[
            pltpu.VMEM((5, 4, 40, 128), f32),
            pltpu.VMEM((2, 4, 40, 128), i32),
            pltpu.VMEM((2, 80, 64), jnp.bfloat16),
            pltpu.VMEM((2, 64, 80), jnp.bfloat16),
            pltpu.VMEM((4, 40, 256), f32),
            pltpu.VMEM((4, 48, 256), f32),
            pltpu.VMEM((4, 256, 256), jnp.bfloat16),
            pltpu.VMEM((4, 256, 256), jnp.bfloat16),
            pltpu.VMEM((5, 4, 48, 128), f32),
            pltpu.VMEM((2, 4, 48, 128), f32),
            pltpu.VMEM((5, 4, 40, 128), f32),
            pltpu.VMEM((5, 4, 40, 128), f32),
            pltpu.VMEM((5, 4, 40, 128), f32),
            pltpu.VMEM((2, 20, 4, 128), f32),
            pltpu.VMEM((2, 2, 20, 4, 128), f32),
            pltpu.VMEM((2, 8, 4, 128), i32),
            pltpu.VMEM((2, 8, 4, 128), i32),
            pltpu.VMEM((2, 5, 3, 40, 128), f32),
            pltpu.VMEM((2, 5, 3, 40, 128), f32),
            pltpu.VMEM((2, 3, 40, 128), i32),
            pltpu.VMEM((2, 3, 40, 128), i32),
            pltpu.VMEM((2, 64, 256), f32),
            pltpu.VMEM((64, 256), f32),
            pltpu.VMEM((48, 256), f32),
            pltpu.VMEM((48, 256), f32),
            pltpu.VMEM((2, 32, 256), f32),
            pltpu.VMEM((2, 16, 256), f32),
            pltpu.VMEM((2, 16, 256), f32),
            pltpu.VMEM((2, 64, 128), f32),
            pltpu.VMEM((48, 128), f32),
            pltpu.VMEM((48, 128), f32),
            pltpu.VMEM((2, 16, 128), f32),
            pltpu.VMEM((2, 16, 128), f32),
            pltpu.VMEM((2, 4, 2, 128), f32),
            pltpu.VMEM((2, 4, 2, 128), f32),
            pltpu.VMEM((1, 64, 2, 128), f32),
            pltpu.VMEM((2, 64, 2, 128), f32),
            pltpu.VMEM((2, 64, 2, 128), f32),
            pltpu.VMEM((64, 2, 128), f32),
            pltpu.VMEM((8, 64, 2, 128), f32),
            pltpu.VMEM((64, 4, 128), f32),
            pltpu.VMEM((64, 4, 128), f32),
            pltpu.VMEM((4, 2, 128), f32),
            pltpu.VMEM((4, 2, 128), f32),
            pltpu.VMEM((256, 640), jnp.bfloat16),
            pltpu.VMEM((128, 256), jnp.bfloat16),
            dma((6,)),
            dma((2, 2, 2)),
            dma((2, 2)),
            dma((2, 2, 2)),
            dma((2, 2)),
            dma((2, 2)),
            dma((2, 2)),
            dma((2, 2)),
            dma((2, 2)),
            dma((2, 2, 1)),
            dma((1, 2)),
            dma((2,)),
            dma((2, 8)),
            dma((2,)),
            dma((2, 1)),
            dma((2, 1)),
        ],
        compiler_params=pltpu.CompilerParams(
            collective_id=0, has_side_effects=True, vmem_limit_bytes=40 * 1024 * 1024
        ),
    )(*in_hbm)
    return after - state


def solution(mesh):
    in_specs = (P(None, "ax", "az", None), P(None, "ax", "az", None))
    out_specs = P(None, "ax", "az", None)
    return jax.shard_map(local, mesh=mesh, in_specs=in_specs, out_specs=out_specs, check_vma=False)
```

```python
import math

import jax
import jax.numpy as jnp
import numpy as np
from jax import lax
from jax.experimental import pallas as pl
from jax.experimental.pallas import tpu as pltpu
from jax.sharding import PartitionSpec as P

NRING = 16
MESH = pl.DeviceIdType.MESH

split_speed = 3.0
small_eps = 1e-06
time_step = 0.004


def filter_tables():
    d, k1 = np.arange(64), np.arange(33)
    angle = 2 * np.pi * np.outer(k1, d) / 64
    fwd = np.zeros((80, 64))
    fwd[:33], fwd[40:73] = np.cos(angle), -np.sin(angle)
    inv = np.zeros((64, 80))
    inv[:, :33], inv[:, 40:73] = np.cos(angle.T), -np.sin(angle.T)
    twiddle = np.zeros((4, 40, 256))
    m_in, m_out = np.arange(40), np.arange(-3, 43)
    scale = np.where((k1 == 0) | (k1 == 32), 1.0, 2.0)[:, None] / 2560
    for v in range(5):
        angle = 2 * np.pi * np.outer(k1, m_in) / 2560
        twiddle[0, :33, v * 48 + 3 : v * 48 + 43] = np.cos(angle)
        twiddle[1, :33, v * 48 + 3 : v * 48 + 43] = -np.sin(angle)
        angle = 2 * np.pi * np.outer(k1, m_out) / 2560
        twiddle[2, :33, v * 48 : v * 48 + 46] = np.cos(angle) * scale
        twiddle[3, :33, v * 48 : v * 48 + 46] = np.sin(angle) * scale
    band = np.zeros((16, 4, 48, 256))
    delta = m_out[None, :] - m_in[:, None]
    for j in range(16):
        if j % 2:
            q = (j + 1) // 2
            modes, extra = np.arange(-q, q), -q
        else:
            q = j // 2
            modes, extra = np.arange(-q, q + 1), q
        kept = sum(np.exp(2j * np.pi * k * delta / 40) for k in modes)
        twin = np.exp(2j * np.pi * extra * delta / 40)
        for k, part in enumerate((kept.real, kept.imag, twin.real, twin.imag)):
            band[j, k, 3:43, :46] = part
    return [a.astype(np.float32) for a in (fwd, inv, twiddle, band)]


def split(x):
    high = x.astype(jnp.bfloat16)
    return high, (x - high.astype(jnp.float32)).astype(jnp.bfloat16)


def dot(a, b):
    return jnp.dot(a, b, preferred_element_type=jnp.float32)


def by_left(a_high, a_low, b):
    high, low = split(b)
    return dot(a_high, high) + (dot(a_high, low) + dot(a_low, high))


def by_right(a, b_high, b_low):
    high, low = split(a)
    rows = a.shape[0]
    both = dot(jnp.concatenate([high, low], axis=0), b_high)
    return both[:rows] + (both[rows:] + dot(high, b_low))


def inverse(x):
    return pltpu.reciprocal(x, approx=True)


class Rows:
    def __init__(self, cells):
        self.cells = list(cells)

    def _with(self, other, op):
        if isinstance(other, Rows):
            pairs = zip(self.cells, other.cells)
            return Rows([None if a is None or b is None else op(a, b) for a, b in pairs])
        return Rows([None if a is None else op(a, other) for a in self.cells])

    def __add__(self, other):
        return self._with(other, lambda a, b: a + b)

    def __sub__(self, other):
        return self._with(other, lambda a, b: a - b)

    def __mul__(self, other):
        return self._with(other, lambda a, b: a * b)

    def map(self, op):
        return Rows([None if a is None else op(a) for a in self.cells])

    def shifted(self, by):
        n = len(self.cells)
        return Rows([self.cells[k + by] if 0 <= k + by < n else None for k in range(n)])


def at(x, by):
    if isinstance(x, Rows):
        return x.shifted(by)
    axis = 1 if x.shape[1] == 256 else 0
    n = x.shape[axis]
    return pltpu.roll(x, (n - by) % n, axis)


def inverse_of(x):
    return x.map(inverse) if isinstance(x, Rows) else inverse(x)


def indicators(f):
    d = at(f, 1) - f
    s = d - at(d, -1)
    s_next = at(s, 1)
    e = s - s_next
    h = s * 0.5
    q = s * s * (13.0 / 12.0) + small_eps
    mid = d - h
    up = d + h
    down = mid - s
    x = inverse_of(q + up * up)
    y = inverse_of(q + mid * mid)
    z = inverse_of(q + down * down)
    return d, s, s_next, e, x * x, y * y, z * z


def faces(flux, state, switch, choose):
    half = flux * 0.5
    lift = state * (0.5 * split_speed)
    d_p, s_p, sn_p, e_p, x_p, y_p, z_p = indicators(half + lift)
    zn_p = at(z_p, 1)
    top = at(x_p * e_p, -1) * 2.0 + zn_p * e_p * 3.0
    total = at(x_p, -1) + y_p * 6.0 + zn_p * 3.0
    plus = top * inverse_of(total)
    d_m, s_m, sn_m, e_m, x_m, y_m, z_m = indicators(half - lift)
    zn_m = at(z_m, 1)
    top = at(zn_m * e_m, 1) * 2.0 + x_m * e_m * 3.0
    total = at(zn_m, 1) + at(y_m, 1) * 6.0 + x_m * 3.0
    minus = top * inverse_of(total)
    middle = flux + (d_p + d_m) * 0.5
    own = s_p + sn_m
    weno = (plus - minus - own) * (1.0 / 6.0)
    central = (own + s_m + sn_p) * (-1.0 / 12.0)
    return middle + choose(switch, weno, central)


def pick(switch, a, b):
    if isinstance(a, Rows):
        triples = zip(switch.cells, a.cells, b.cells)
        return Rows([None if s is None or p is None or q is None else jnp.where(s, p, q) for s, p, q in triples])
    return jnp.where(switch, a, b)


def largest(a, b):
    if isinstance(a, Rows):
        return a._with(b, jnp.maximum)
    return jnp.maximum(a, b)


def peak(flags):
    pair = largest(flags, at(flags, 1))
    four = largest(pair, at(pair, 2))
    return at(largest(four, at(pair, 4)), -2)


def window(flags):
    six = peak(flags)
    return six.map(lambda a: a > 0.5) if isinstance(six, Rows) else six > 0.5


def fluxes(u, q, p, component):
    parts = [u[1 + component], u[1] * q, u[2] * q, u[3] * q, (u[4] + p) * q]
    parts[1 + component] = parts[1 + component] + p
    return parts


def pressure(u, inv_rho):
    return (u[4] - (u[1] * u[1] + u[2] * u[2] + u[3] * u[3]) * inv_rho * 0.5) * 0.4


def lanes(shape):
    return lax.broadcasted_iota(jnp.int32, shape, len(shape) - 1)


def radius(rows):
    return lanes((rows, 128)).astype(jnp.float32) + 0.5


def azimuthal(padded, flags, section, rate):
    scale = -1.0 / (radius(40) * (2.0 * math.pi / 2560))

    def row(r, carry):
        u = [padded[v, r] for v in range(5)]
        inv_rho = inverse(u[0])
        q = u[3] * inv_rho
        f = fluxes(u, q, pressure(u, inv_rho), 2)
        switch = window(flags[section, r])
        for v in range(5):
            face = faces(f[v], u[v], switch, pick)
            rate[v, r] = rate[v, r] + (at(face, 3)[:40] - at(face, 2)[:40]) * scale
        return carry

    lax.fori_loop(0, 4, row, 0)


def radial_terms(own, rate):
    inv_r = 1.0 / radius(8)
    lane = lanes((8, 128))

    def chunk(c, carry):
        at8 = pl.ds(pl.multiple_of(c * 8, 8), 8)
        for r in range(4):
            here = [own[v, r, at8, :] for v in range(5)]
            inv_here = inverse(here[0])
            p_here = pressure(here, inv_here)
            g = fluxes(here, here[2] * inv_here, p_here, 1)
            swirl = here[3] * inv_here
            extra = [None, None, here[3] * swirl + p_here, -here[2] * swirl, None]
            for v in range(5):
                before = pltpu.roll(g[v], 1, 1)
                after = jnp.where(lane == 127, g[v], pltpu.roll(g[v], 127, 1))
                away = g[v] if extra[v] is None else g[v] - extra[v]
                rate[v, r, at8, :] = (before - after) * 0.5 - away * inv_r
        return carry

    lax.fori_loop(0, 5, chunk, 0)


def finish(own, low, high, flags, flags_low, flags_high, section, rate, combine):
    def chunk(c, carry):
        at8 = pl.ds(pl.multiple_of(c * 8, 8), 8)
        u = [
            Rows(
                [low[v, k, at8, :] for k in range(3)]
                + [own[v, k, at8, :] for k in range(4)]
                + [high[v, k, at8, :] for k in range(3)]
            )
            for v in range(5)
        ]
        marks = Rows(
            [flags_low[section, k, at8, :] for k in range(3)]
            + [flags[section, k, at8, :] for k in range(4)]
            + [flags_high[section, k, at8, :] for k in range(3)]
        ).map(lambda a: a.astype(jnp.float32))
        switch = window(marks)
        inv_rho = u[0].map(inverse)
        f = fluxes(u, u[1] * inv_rho, pressure(u, inv_rho), 0)
        for v in range(5):
            face = faces(f[v], u[v], switch, pick).cells
            for r in range(4):
                slope = rate[v, r, at8, :] - (face[3 + r] - face[2 + r])
                combine(v, r, at8, u[v].cells[3 + r], slope)
        return carry

    lax.fori_loop(0, 5, chunk, 0)


def cell_of(width):
    return lax.rem(lanes((16, width)), 48)


def side_by_side(blocks):
    lane = lanes(blocks[0].shape)
    packed = blocks[0]
    for r in range(1, 4):
        packed = jnp.where(lane >= 32 * r, pltpu.roll(blocks[r], 32 * r, 1), packed)
    return packed


def pack_state(padded):
    stacks = []
    for r in range(4):
        rest = jnp.zeros((16, 128), jnp.float32)
        stacks.append(jnp.concatenate([padded[v, r] for v in range(5)] + [rest], axis=0))
    return jnp.transpose(side_by_side(stacks))


def pack_flags(padded_flags):
    stacks = []
    for r in range(4):
        rest = jnp.zeros((32, 128), jnp.float32)
        stacks.append(jnp.concatenate([padded_flags[0, r], padded_flags[1, r], rest], axis=0))
    return jnp.transpose(side_by_side(stacks))


def fold_ends(blocks, width):
    cell = cell_of(width)
    to_right = jnp.zeros((16, width), jnp.float32)
    to_left = to_right
    for r in range(4):
        moved = pltpu.roll(blocks[r], (width - 40 + 3 * r) % width, 1)
        to_right = jnp.where((cell >= 3 * r) & (cell < 3 * r + 3), moved, to_right)
        moved = pltpu.roll(blocks[r], 31 + 3 * r, 1)
        to_left = jnp.where((cell >= 34 + 3 * r) & (cell < 37 + 3 * r), moved, to_left)
    return to_right, to_left


def with_ends(block, from_left, from_right, r):
    width = block.shape[1]
    cell = cell_of(width)
    before = pltpu.roll(from_left, width - 3 * r, 1) if r else from_left
    after = pltpu.roll(from_right, 9 - 3 * r, 1) if r < 3 else from_right
    return jnp.where(cell < 3, before, jnp.where(cell < 43, block, jnp.where(cell < 46, after, 0.0)))


def replicate(x):
    x = jnp.where(lanes(x.shape) < 48, x, 0.0)
    one = jnp.concatenate([x, jnp.zeros_like(x)], axis=1)
    two = one + pltpu.roll(one, 48, 1)
    four = two + pltpu.roll(two, 96, 1)
    return four + pltpu.roll(one, 192, 1)


def slot(shape, k):
    lane = lanes(shape)
    return (lane >= 48 * k) & (lane < 48 * k + 48)


def packed_flux(u, q, p, component):
    own, energy = slot(u.shape, 1 + component), slot(u.shape, 4)
    return u * q + jnp.where(own, p, jnp.where(energy, p * q, 0.0))


def near_azimuthal(own, marks, rate, apart, copies):
    blocks = [own(r) for r in range(4)]
    (_, _, q_t), p = stacked_primitives(blocks, apart)
    wide = select(jnp.concatenate([p, q_t], axis=0), copies[...])
    every = dot(jnp.concatenate([marks(r) for r in range(4)], axis=0).astype(jnp.bfloat16), copies[...])
    cycle = lax.broadcasted_iota(jnp.int32, (16, 256), 0).astype(jnp.float32) + 0.5
    inv_rh = 1.0 / (cycle * (2.0 * math.pi / 2560))
    for r, u in enumerate(blocks):
        wide_p, wide_t = wide[16 * r : 16 * r + 16], wide[64 + 16 * r : 80 + 16 * r]
        f = packed_flux(u, wide_t, wide_p, 2)
        face = faces(f, u, window(every[16 * r : 16 * r + 16]), pick)
        rate[16 * r : 16 * r + 16, :] = (at(face, -1) - face) * inv_rh


def near_finish(low, own, high, outer, ghost, marks, rate, apart, copies, combine):
    blocks = [low(k) for k in range(3)] + [own(r) for r in range(4)] + [high(k) for k in range(3)]
    row = lax.broadcasted_iota(jnp.int32, (8, 256), 0)
    negated = slot((8, 256), 2) | slot((8, 256), 3)
    beyond = []
    for r in range(4):
        mirrored = jnp.broadcast_to(ghost(r), (8, 256))
        beyond.append(jnp.where(row == 7, jnp.where(negated, -mirrored, mirrored), outer(r)))
    (q_x, q_r, q_t), p = stacked_primitives(blocks + beyond, apart)
    stacked = jnp.concatenate([p, q_x[:160], q_r[48:112], q_r[160:], q_t[48:112]], axis=0)
    wide = select(stacked, copies[...])
    every = dot(jnp.concatenate(marks, axis=0).astype(jnp.bfloat16), copies[...])
    switches = [every[16 * k : 16 * k + 16] for k in range(10)]
    f = [
        packed_flux(u, wide[192 + 16 * k : 208 + 16 * k], wide[16 * k : 16 * k + 16], 0)
        for k, u in enumerate(blocks)
    ]
    cycle = lax.broadcasted_iota(jnp.int32, (16, 256), 0).astype(jnp.float32) + 0.5
    inv_r = 1.0 / cycle
    radial = []
    for r in range(4):
        u, wide_p = blocks[3 + r], wide[48 + 16 * r : 64 + 16 * r]
        g = packed_flux(u, wide[352 + 16 * r : 368 + 16 * r], wide_p, 1)
        g_beyond = packed_flux(beyond[r], wide[416 + 8 * r : 424 + 8 * r], wide[160 + 8 * r : 168 + 8 * r], 1)
        drag = drag_of(u, wide[448 + 16 * r : 464 + 16 * r], wide_p)
        ring = jnp.concatenate([g, g_beyond], axis=0)
        after, before = pltpu.roll(ring, 23, 0)[:16], pltpu.roll(ring, 1, 0)[:16]
        radial.append((after - before) * 0.5 + (g - drag) * inv_r)
    slopes = [[[None, None], [None, None]] for _ in range(4)]
    for h in range(2):
        for w in range(2):
            part = (slice(8 * h, 8 * h + 8), slice(128 * w, 128 * w + 128))
            face = faces(
                Rows([x[part] for x in f]),
                Rows([x[part] for x in blocks]),
                window(Rows([x[part] for x in switches])),
                pick,
            ).cells
            for r in range(4):
                slopes[r][h][w] = face[2 + r] - face[3 + r]
    lane = lanes((16, 256))
    cell = lax.rem(lane, 48)
    valid = (cell >= 3) & (cell < 43) & (lane < 240)
    for r in range(4):
        rows = [jnp.concatenate(pair, axis=1) for pair in slopes[r]]
        slope = jnp.concatenate(rows, axis=0) - radial[r] + rate[16 * r : 16 * r + 16, :]
        combine(r, jnp.where(valid, slope, 0.0), valid)


def packed_rows(ref, first, count):
    rows = pl.ds(first, count)
    return jnp.concatenate([ref[rows, 0, :], ref[rows, 1, :]], axis=1)


def place_of(r, group):
    return 32 * group + 8 * r


def build_selectors(apart, copies):
    to, source = lanes((256, 640)), lax.broadcasted_iota(jnp.int32, (256, 640), 0)
    cell = lax.rem(to, 128)
    hit = (cell < 48) & (source == cell + 48 * (to // 128))
    apart[...] = jnp.where(hit, 1.0, 0.0).astype(jnp.bfloat16)
    to, source = lanes((128, 256)), lax.broadcasted_iota(jnp.int32, (128, 256), 0)
    hit = (source == lax.rem(to, 48)) & (to < 240)
    copies[...] = jnp.where(hit, 1.0, 0.0).astype(jnp.bfloat16)


def select(values, selector):
    high, low = split(values)
    both = dot(jnp.concatenate([high, low], axis=0), selector)
    n = values.shape[0]
    return both[:n] + both[n:]


def stacked_primitives(blocks, apart):
    every = select(jnp.concatenate(blocks, axis=0), apart[...])
    parts = [every[:, 128 * k : 128 * k + 128] for k in range(5)]
    inv_rho = inverse(jnp.where(parts[0] == 0.0, 1.0, parts[0]))
    return [parts[k] * inv_rho for k in (1, 2, 3)], pressure(parts, inv_rho)


def drag_of(u, q_t, p):
    turned = jnp.where(slot(u.shape, 3), -pltpu.roll(u, 48, 1) * q_t, 0.0)
    return jnp.where(slot(u.shape, 2), pltpu.roll(u, 256 - 48, 1) * q_t + p, turned)


def line_alone(own_line, extra, cycle, partial, apart, copies):
    radius_here = jnp.full((16, 256), cycle, jnp.int32).astype(jnp.float32) + 0.5
    inv_r = 1.0 / radius_here
    inv_rh = 1.0 / (radius_here * (2.0 * math.pi / 2560))
    blocks = [packed_rows(own_line, 16 * c, 16) for c in range(4)]
    (_, q_r, q_t), p = stacked_primitives(blocks, apart)
    wide = select(jnp.concatenate([p, q_r, q_t], axis=0), copies[...])
    marks = jnp.concatenate([extra[:, 2, :], extra[:, 3, :]], axis=1)
    marks = pltpu.roll(marks, 256 - 96, 1)[:, :128].astype(jnp.bfloat16)
    marks = dot(marks, copies[...]) > 0.5
    for c, own in enumerate(blocks):
        wide_p, wide_r, wide_t = [wide[64 * k + 16 * c : 64 * k + 16 * c + 16] for k in range(3)]
        g = packed_flux(own, wide_r, wide_p, 1)
        turn = packed_flux(own, wide_t, wide_p, 2)
        face = faces(turn, own, marks[16 * c : 16 * c + 16], pick)
        slope = (at(face, -1) - face) * inv_rh - (g - drag_of(own, wide_t, wide_p)) * inv_r
        partial[16 * c : 16 * c + 16, :] = slope


def line_rates(own_line, lines, extra, partial, target, apart, copies):
    lane = lanes((16, 256))
    cell = lax.rem(lane, 48)
    valid = (cell >= 3) & (cell < 43) & (lane < 240)
    for c in range(4):
        first = 16 * c
        own = packed_rows(own_line, first, 16)
        blocks = [packed_rows(lines.at[k], first, 16) for k in range(3)] + [own]
        blocks += [packed_rows(lines.at[k], first, 16) for k in range(3, 8)]
        (q_x, q_r, _), p = stacked_primitives(blocks, apart)
        stacked = jnp.concatenate([p, q_x[:112], q_r[112:]], axis=0)
        spread_out = select(stacked, copies[...])
        wide = [spread_out[16 * k : 16 * k + 16] for k in range(18)]
        f = [packed_flux(blocks[k], wide[9 + k], wide[k], 0) for k in range(7)]
        sides = [packed_flux(blocks[7 + k], wide[16 + k], wide[7 + k], 1) for k in range(2)]
        blocks = blocks[:7]
        rows = pl.ds(first, 16)
        marks = jnp.concatenate([extra[rows, 2, :], extra[rows, 3, :]], axis=1)
        marks = jnp.concatenate([marks[:, :128], pltpu.roll(marks, 256 - 48, 1)[:, :128]], axis=0)
        marks = dot(marks.astype(jnp.bfloat16), copies[...]) > 0.5
        below, above = marks[:16], marks[16:]
        halves = []
        for h in range(2):
            pair = []
            for w in range(2):
                part = (slice(8 * h, 8 * h + 8), slice(128 * w, 128 * w + 128))
                face = faces(
                    Rows([x[part] for x in f]),
                    Rows([x[part] for x in blocks]),
                    Rows([None, None, below[part], above[part], None, None, None]),
                    pick,
                ).cells
                pair.append(face[2] - face[3])
            halves.append(jnp.concatenate(pair, axis=1))
        slope = jnp.concatenate(halves, axis=0) + partial[rows, :] - (sides[1] - sides[0]) * 0.5
        before = jnp.concatenate([extra[rows, 0, :], extra[rows, 1, :]], axis=1)
        value = jnp.where(valid, before * 0.75 + (own + slope * time_step) * 0.25, 0.0)
        target[rows, 0, :] = value[:, :128]
        target[rows, 1, :] = value[:, 128:]


def unpack(rows):
    n = rows.shape[0]
    turned = jnp.transpose(jnp.concatenate([rows, jnp.zeros((128 - n, 256), jnp.float32)], axis=0))

    def block(v, k):
        cells = turned[48 * v : 48 * v + 48]
        return pltpu.roll(cells, (128 - k) % 128, 1) if k % 128 else cells

    return block


def others(me):
    y, x, z = me // 32, lax.rem(me // 8, 4), lax.rem(me, 8)
    ys = {d: lax.rem(y + d, 2) * 32 for d in (1, 0)}
    xs = {d: lax.rem(x + d, 4) * 8 for d in (2, 1, 3, 0)}
    zs = {d: lax.rem(z + d, 8) for d in (4, 3, 5, 2, 6, 1, 7, 0)}
    steps = [(dy, dx, dz) for dz in zs for dx in xs for dy in ys]
    steps.sort(key=lambda s: -(s[0] + min(s[1], 4 - s[1]) + min(s[2], 8 - s[2])))
    return [ys[dy] + xs[dx] + zs[dz] for dy, dx, dz in steps[:-1]]


def spread(send, recv, me, peers, send_sem, recv_sem):
    for to in peers:
        pltpu.make_async_remote_copy(
            src_ref=send.at[to],
            dst_ref=recv.at[me],
            send_sem=send_sem,
            recv_sem=recv_sem,
            device_id={"az": to},
            device_id_type=MESH,
        ).start()
    recv[pl.ds(me, 1)] = send[pl.ds(me, 1)]


def arrived(buffer, sem):
    rows = buffer.at[pl.ds(0, 63)]
    pltpu.make_async_copy(rows, rows, sem).wait()


def build_mix(mine, mix_high, mix_low):
    mix_high[...] = jnp.zeros_like(mix_high)
    mix_low[...] = jnp.zeros_like(mix_low)
    for k in range(4):
        rows = []
        for v in range(5):
            rows.append(pltpu.roll(mine[k], 48 * v, 1) if v else mine[k])
        rows.append(jnp.zeros((16, 256), jnp.float32))
        mix_high[k], mix_low[k] = split(jnp.concatenate(rows, axis=0))


def project(recv, back, me, fwd, inv, twiddle, mix_high, mix_low):
    x = jnp.concatenate([recv[:, 0, :], recv[:, 1, :]], axis=1)
    a = by_left(fwd[0], fwd[1], x)
    re, im = a[:40], a[40:]
    re, im = re * twiddle[0] - im * twiddle[1], re * twiddle[1] + im * twiddle[0]
    odd = lax.rem(me, 2) == 1
    first_row = lax.broadcasted_iota(jnp.int32, (8, 256), 0) == 0

    def twin_row(x):
        return jnp.where(first_row, jnp.where(odd, x[:8], x[32:40]), 0.0)

    main = jnp.concatenate([re, im], axis=0)
    twin = jnp.concatenate([twin_row(re), twin_row(im)], axis=0)
    c, s = by_right(main, mix_high[0], mix_low[0]), by_right(main, mix_high[1], mix_low[1])
    tc, ts = by_right(twin, mix_high[2], mix_low[2]), by_right(twin, mix_high[3], mix_low[3])
    re, im = c[:40] - s[40:], s[:40] + c[40:]
    t_re, t_im = tc[:8] - ts[8:], ts[:8] + tc[8:]

    def with_twin(x, t):
        top = x[:8] + jnp.where(odd, t, 0.0)
        return jnp.concatenate([top, x[8:32], x[32:40] + jnp.where(odd, 0.0, t)], axis=0)

    re, im = with_twin(re, t_re), with_twin(im, t_im)
    re, im = re * twiddle[2] - im * twiddle[3], re * twiddle[3] + im * twiddle[2]
    y = by_left(inv[0], inv[1], jnp.concatenate([re, im], axis=0))
    back[:, 0, :] = y[:, :128]
    back[:, 1, :] = y[:, 128:]


def kernel(
    state_hbm, flags_hbm, fwd_hbm, inv_hbm, twiddle_hbm, band, out,
    state, flags, fwd, inv, twiddle, mine, mix_high, mix_low, padded, padded_flags, rate, first, second,
    az_out, az_in, azf_out, azf_in, low, high, flow, fhigh,
    near, near_rate, near_low, near_high, near_outer, ends_out, ends_in, marks, marks_low, marks_high,
    mark_ends_out, mark_ends_in, ghost_out, ghost_in,
    send, recv, back, ret, lines, extra_out, extra_in, outer_out, rim_in, apart, copies,
    sem, az_sem, azf_sem, ax_sem, axf_sem, end_sem, mark_end_sem, row_sem, mark_row_sem, ghost_sem,
    go_sem, come_sem, line_sem, extra_sem, outer_sem, rim_sem,
):
    me, row = lax.axis_index("az"), lax.axis_index("ax")
    right, left = lax.rem(me + 1, 64), lax.rem(me + 63, 64)
    upper, lower = lax.rem(row + 1, 4), lax.rem(row + 3, 4)
    opposite = lax.rem(me + 32, 64)
    z, x, y = lax.rem(me, 8), lax.rem(me // 8, 4), me // 32
    level, cycle = x, 8 * y + z
    pairs = [
        (state_hbm, state),
        (flags_hbm, flags),
        (fwd_hbm, fwd),
        (inv_hbm, inv),
        (twiddle_hbm, twiddle),
        (band.at[cycle], mine),
    ]
    loads = [pltpu.make_async_copy(a, b, sem.at[k]) for k, (a, b) in enumerate(pairs)]
    for item in loads:
        item.start()
    barrier = pltpu.get_barrier_semaphore()
    peers = others(me)
    for peer in peers:
        pl.semaphore_signal(barrier, inc=1, device_id={"az": peer}, device_id_type=MESH)
    for peer in (upper, lower):
        pl.semaphore_signal(barrier, inc=1, device_id={"ax": peer}, device_id_type=MESH)

    def copy(src, dst, sems, k, **place):
        return pltpu.make_async_remote_copy(
            src_ref=src,
            dst_ref=dst,
            send_sem=sems.at[0, k],
            recv_sem=sems.at[1, k],
            device_id=place,
            device_id_type=MESH,
        )

    def along_az(source, target, sems):
        return [
            copy(source.at[0], target.at[0], sems, 0, az=right),
            copy(source.at[1], target.at[1], sems, 1, az=left),
        ]

    def along_ax(up_from, to_low, down_from, to_high, sems):
        return copy(up_from, to_low, sems, 0, ax=upper), copy(down_from, to_high, sems, 1, ax=lower)

    def wide_ax(field, to_low, to_high, sems):
        return along_ax(field.at[:, pl.ds(1, 3)], to_low, field.at[:, pl.ds(0, 3)], to_high, sems)

    def stage(field, staging, fields):
        for f in range(fields):
            for r in range(4):
                staging[0, f * 4 + r, 0:3] = field[f, r, 37:40]
                staging[1, f * 4 + r, 0:3] = field[f, r, 0:3]

    def when_up(action):
        pl.when(row < 3)(action)

    def when_down(action):
        pl.when(row > 0)(action)

    def start_ax(pair):
        when_up(pair[0].start)
        when_down(pair[1].start)

    def sent_ax(pair):
        when_up(pair[0].wait_send)
        when_down(pair[1].wait_send)

    def came_ax(pair):
        when_down(pair[0].wait_recv)
        when_up(pair[1].wait_recv)

    def start_all(items):
        for item in items:
            item.start()

    def came_all(items):
        for item in items:
            item.wait_recv()

    def sent_all(items):
        for item in items:
            item.wait_send()

    padded[...] = jnp.zeros_like(padded)
    padded_flags[...] = jnp.zeros_like(padded_flags)
    loads[0].wait()
    loads[1].wait()
    for v in range(5):
        for r in range(4):
            padded[v, r, 3:43] = state[v, r]
    for s in range(2):
        for r in range(4):
            padded_flags[s, r, 3:43] = flags[s, r].astype(jnp.float32)
    packed = pack_state(padded)
    for r in range(4):
        near[0, 16 * r : 16 * r + 16, :] = packed[32 * r : 32 * r + 16]
        near_outer[0, 8 * r : 8 * r + 8, :] = packed[32 * r + 16 : 32 * r + 24]
        ghost_out[0, r, 0:1, :] = packed[32 * r : 32 * r + 1, :128]
        ghost_out[0, r, 1:2, :] = packed[32 * r : 32 * r + 1, 128:]
    ends_out[0], ends_out[1] = fold_ends([packed[32 * r : 32 * r + 16] for r in range(4)], 256)
    packed = pack_flags(padded_flags)
    for r in range(4):
        marks[0, 16 * r : 16 * r + 16, :] = packed[32 * r : 32 * r + 16]
    mark_ends_out[0], mark_ends_out[1] = fold_ends([packed[32 * r : 32 * r + 16] for r in range(4)], 128)
    ends = along_az(ends_out, ends_in, end_sem)
    mark_ends = along_az(mark_ends_out, mark_ends_in, mark_end_sem)
    rows = along_ax(near.at[0, pl.ds(16, 48)], near_low, near.at[0, pl.ds(0, 48)], near_high, row_sem)
    mark_rows = along_ax(marks.at[0, pl.ds(16, 48)], marks_low, marks.at[0, pl.ds(0, 48)], marks_high, mark_row_sem)
    ghost = copy(ghost_out.at[0], ghost_in.at[0], ghost_sem.at[0], 0, az=opposite)
    stage(state, az_out, 5)
    stage(flags, azf_out, 2)
    az = along_az(az_out, az_in.at[0], az_sem.at[0])
    azf = along_az(azf_out, azf_in, azf_sem)
    ax = wide_ax(state, low.at[0], high.at[0], ax_sem.at[0])
    axf = wide_ax(flags, flow, fhigh, axf_sem)
    radial_terms(state, rate)
    pl.semaphore_wait(barrier, 65)
    start_ax(rows)
    start_all(ends)
    ghost.start()
    start_all(mark_ends)
    start_ax(mark_rows)
    start_all(az)
    start_all(azf)
    start_ax(ax)
    start_ax(axf)
    for item in loads[2:]:
        item.wait()
    build_mix(mine, mix_high, mix_low)
    build_selectors(apart, copies)

    came_all(ends)
    came_all(mark_ends)
    for r in range(4):
        at_row = slice(16 * r, 16 * r + 16)
        near[1, at_row, :] = with_ends(near[0, at_row, :], ends_in[0], ends_in[1], r)
        marks[1, at_row, :] = with_ends(marks[0, at_row, :], mark_ends_in[0], mark_ends_in[1], r)

    def own_state(r):
        return near[1, 16 * r : 16 * r + 16, :]

    def own_marks(r):
        return marks[1, 16 * r : 16 * r + 16, :]

    near_azimuthal(own_state, own_marks, near_rate, apart, copies)
    came_ax(rows)
    came_ax(mark_rows)

    def low_rim():
        for k in range(3):
            near_low[16 * k : 16 * k + 16, :] = near[1, 0:16, :]
            marks_low[16 * k : 16 * k + 16, :] = marks[1, 0:16, :]

    def high_rim():
        for k in range(3):
            near_high[16 * k : 16 * k + 16, :] = near[1, 48:64, :]
            marks_high[16 * k : 16 * k + 16, :] = marks[1, 48:64, :]

    pl.when(row == 0)(low_rim)
    pl.when(row == 3)(high_rim)
    ghost.wait_recv()

    def mark_list():
        below = [marks_low[16 * k : 16 * k + 16, :] for k in range(3)]
        above = [marks_high[16 * k : 16 * k + 16, :] for k in range(3)]
        return below + [own_marks(r) for r in range(4)] + above

    def ghost_row(section):
        return lambda r: jnp.concatenate([ghost_in[section, r, 0:1, :], ghost_in[section, r, 1:2, :]], axis=1)

    def outer_rows(section):
        return lambda r: near_outer[section, 8 * r : 8 * r + 8, :]

    def hand_in(section, r, value):
        for group in range(2):
            first_place = place_of(r, group)
            for h in range(2):
                part = value[8 * group : 8 * group + 8, 128 * h : 128 * h + 128]
                send[section, first_place : first_place + 8, h, :] = part

    def near_first(r, slope, valid):
        hand_in(0, r, jnp.where(valid, own_state(r) + slope * time_step, 0.0))

    near_finish(
        lambda k: near_low[16 * k : 16 * k + 16, :],
        own_state,
        lambda k: near_high[16 * k : 16 * k + 16, :],
        outer_rows(0),
        ghost_row(0),
        mark_list(),
        near_rate,
        apart,
        copies,
        near_first,
    )
    spread(send.at[0], recv.at[0], me, peers, go_sem.at[0, 0], go_sem.at[0, 1])

    tall = Rows(mark_list()).map(lambda a: replicate(pltpu.roll(a, 80, 1)))
    axial_marks = peak(tall).cells
    for r in range(4):
        low_part, high_part, turn_part = axial_marks[2 + r], axial_marks[3 + r], peak(tall.cells[3 + r])
        own_slot = [slot((16, 256), k) for k in range(3)]
        row_marks = jnp.where(own_slot[1], high_part, jnp.where(own_slot[2], turn_part, 0.0))
        row_marks = jnp.where(own_slot[0], low_part, row_marks)
        whole_row = [own_state(r)[:, :128], own_state(r)[:, 128:], row_marks[:, :128], row_marks[:, 128:]]
        for group in range(2):
            first_place = place_of(r, group)
            for k in range(4):
                extra_out[first_place : first_place + 8, k, :] = whole_row[k][8 * group : 8 * group + 8]
    spread(extra_out, extra_in, me, peers, extra_sem.at[0], extra_sem.at[1])

    sent_ax(rows)
    sent_ax(mark_rows)
    sent_all(ends + mark_ends + [ghost])

    def fill_az(section):
        for v in range(5):
            for r in range(4):
                padded[v, r, 0:3] = az_in[section, 0, v * 4 + r, 0:3]
                padded[v, r, 43:46] = az_in[section, 1, v * 4 + r, 0:3]

    came_all(az)
    came_all(azf)
    fill_az(0)
    for s in range(2):
        for r in range(4):
            padded_flags[s, r, 0:3] = azf_in[0, s * 4 + r, 0:3].astype(jnp.float32)
            padded_flags[s, r, 43:46] = azf_in[1, s * 4 + r, 0:3].astype(jnp.float32)
    azimuthal(padded, padded_flags, 0, rate)
    came_ax(ax)
    came_ax(axf)

    def rims(field, section):
        def low_rim():
            for v in range(5):
                for k in range(3):
                    low[section, v, k] = field[v, 0]

        def high_rim():
            for v in range(5):
                for k in range(3):
                    high[section, v, k] = field[v, 3]

        pl.when(row == 0)(low_rim)
        pl.when(row == 3)(high_rim)

    def flag_low_rim():
        for s in range(2):
            for k in range(3):
                flow[s, k] = flags[s, 0]

    def flag_high_rim():
        for s in range(2):
            for k in range(3):
                fhigh[s, k] = flags[s, 3]

    rims(state, 0)
    pl.when(row == 0)(flag_low_rim)
    pl.when(row == 3)(flag_high_rim)

    def combine_first(v, r, rows, here, slope):
        first[v, r, rows, :] = here + slope * time_step

    finish(state, low.at[0], high.at[0], flags, flow, fhigh, 0, rate, combine_first)
    sent_all(az + azf)
    for v in range(5):
        for r in range(4):
            padded[v, r, 3:43] = first[v, r]
    packed = pack_state(padded)
    for r in range(4):
        outer_out[r, 0:1, :] = packed[32 * r + 16 : 32 * r + 17, :128]
        outer_out[r, 1:2, :] = packed[32 * r + 16 : 32 * r + 17, 128:]
    for r in range(4):
        last = place_of(r, 1) + 7
        beyond = copy(outer_out.at[r], lines.at[7, me], outer_sem, 0, az=last)
        pl.when(me != last)(beyond.start)
    is_last, is_first = cycle == 15, cycle == 0

    def keep_outer():
        lines[7, pl.ds(me, 1)] = outer_out[pl.ds(level, 1)]

    pl.when(is_last)(keep_outer)
    arrived(recv.at[0], go_sem.at[0, 1])
    project(recv.at[0], back.at[0], me, fwd, inv, twiddle, mix_high, mix_low)

    column = 32 * y + z
    meets = []
    for step in range(1, 4):
        over, under = level + step, level + 4 - step
        to_row, to_level = row + over // 4, lax.rem(over, 4)
        to = 8 * to_level + column
        item = copy(back.at[0], lines.at[3 - step], line_sem, 3 - step, ax=to_row, az=to)
        has_over, has_under = (row < 3) | (over < 4), (row > 0) | (under >= 4)
        meets.append((item, has_over, has_under))
        to_row, to_level = row - 1 + under // 4, lax.rem(under, 4)
        to = 8 * to_level + column
        item = copy(back.at[0], lines.at[2 + step], line_sem, 2 + step, ax=to_row, az=to)
        meets.append((item, has_under, has_over))
    base = 8 * level
    ahead, behind = cycle + 1, cycle + 15
    to = base + 32 * (ahead // 8) + lax.rem(ahead, 8)
    item = copy(back.at[0], lines.at[6], line_sem, 6, az=to)
    not_first, not_last = jnp.logical_not(is_first), jnp.logical_not(is_last)
    meets.append((item, not_last, not_first))
    behind = lax.rem(behind, 16)
    to = base + 32 * (behind // 8) + lax.rem(behind, 8)
    item = copy(back.at[0], lines.at[7], line_sem, 7, az=to)
    meets.append((item, not_first, not_last))
    for item, sends, _ in meets:
        pl.when(sends)(item.start)
    stage(first, az_out, 5)
    az = along_az(az_out, az_in.at[1], az_sem.at[1])
    start_all(az)

    def hand_rim():
        for to in peers:
            copy(back.at[0, to], rim_in.at[level], rim_sem, 0, az=to).start()
        rim_in[pl.ds(level, 1)] = back[0, pl.ds(me, 1)]

    pl.when(is_last)(hand_rim)

    def mirror():
        lane = lanes((64, 128))
        for h in range(2):
            flipped = (lane + 128 * h >= 96) & (lane + 128 * h < 192)
            turned = jnp.concatenate([back[0, 32:64, h, :], back[0, 0:32, h, :]], axis=0)
            lines[6, :, h, :] = jnp.where(flipped, -turned, turned)

    pl.when(is_first)(mirror)
    arrived(extra_in, extra_sem.at[1])
    line_alone(back.at[0], extra_in, cycle, near_rate, apart, copies)
    for item, _, comes in meets:
        pl.when(comes)(item.wait_recv)
    pl.when(is_last)(lambda: arrived(lines.at[7], outer_sem.at[1, 0]))
    for r in range(3):

        def clamp_low():
            for step in range(r + 1, 4):
                lines[3 - step] = lines[3 - r] if r else back[0]

        def clamp_high():
            for step in range(r + 1, 4):
                lines[2 + step] = lines[2 + r] if r else back[0]

        pl.when((row == 0) & (level == r))(clamp_low)
        pl.when((row == 3) & (level == 3 - r))(clamp_high)
    ax2 = wide_ax(first, low.at[1], high.at[1], ax_sem.at[1])
    start_ax(ax2)
    line_rates(back.at[0], lines, extra_in, near_rate, recv.at[1], apart, copies)
    project(recv.at[1], back.at[1], me, fwd, inv, twiddle, mix_high, mix_low)
    spread(back.at[1], ret, me, peers, come_sem.at[0], come_sem.at[1])

    sent_ax(ax)
    sent_ax(axf)
    came_all(az)
    sent_all(az)
    fill_az(1)
    sent_ax(ax2)
    def rim_but_own():
        part = rim_in.at[pl.ds(0, 3)]
        pltpu.make_async_copy(part, part, rim_sem.at[1, 0]).wait()

    pl.when(is_last)(rim_but_own)
    pl.when(not_last)(pltpu.make_async_copy(rim_in, rim_in, rim_sem.at[1, 0]).wait)
    block = unpack(jnp.concatenate([packed_rows(rim_in, 0, 4), jnp.zeros((4, 256), jnp.float32)], axis=0))
    lane40 = lanes((40, 128))
    for r in range(4):
        for v in range(5):
            first[v, r] = jnp.where(lane40 == 15, block(v, r - 15)[3:43], first[v, r])

    radial_terms(first, rate)
    azimuthal(padded, padded_flags, 1, rate)
    came_ax(ax2)
    rims(first, 1)

    def combine_second(v, r, rows, here, slope):
        second[v, r, rows, :] = state[v, r, rows, :] * 0.75 + (here + slope * time_step) * 0.25

    finish(first, low.at[1], high.at[1], flags, flow, fhigh, 1, rate, combine_second)
    arrived(send.at[0], go_sem.at[0, 0])
    arrived(extra_out, extra_sem.at[0])
    for item, sends, _ in meets:
        pl.when(sends)(item.wait_send)
    pl.when(is_last)(lambda: arrived(back.at[0], rim_sem.at[0, 0]))

    def outers(n):
        part = outer_out.at[pl.ds(0, n)]
        pltpu.make_async_copy(part, part, outer_sem.at[0, 0]).wait()

    pl.when(is_last)(lambda: outers(3))
    pl.when(not_last)(lambda: outers(4))
    arrived(ret, come_sem.at[1])
    order = [packed_rows(ret, place_of(r, group), 8) for r in range(4) for group in range(2)]
    block = unpack(jnp.concatenate(order, axis=0))
    for r in range(4):
        for v in range(5):
            out[v, r] = jnp.where(lane40 < NRING, block(v, 16 * r)[3:43], second[v, r])
    arrived(back.at[1], come_sem.at[0])


def local(state, shock_flags):
    fwd, inv, twiddle, band = filter_tables()
    tables = [jnp.stack(split(jnp.asarray(t))) for t in (fwd, inv)]
    tables += [jnp.asarray(twiddle), jnp.asarray(band)]
    vmem = pl.BlockSpec(memory_space=pltpu.VMEM)
    f32, i32 = jnp.float32, jnp.int32
    dma = pltpu.SemaphoreType.DMA
    in_hbm = [pltpu.with_memory_space_constraint(x, pltpu.HBM) for x in (state, shock_flags, *tables)]
    after = pl.pallas_call(
        kernel,
        out_shape=jax.ShapeDtypeStruct(state.shape, f32),
        in_specs=[pl.BlockSpec(memory_space=pltpu.HBM)] * 6,
        out_specs=vmem,
        scratch_shapes=[
            pltpu.VMEM((5, 4, 40, 128), f32),
            pltpu.VMEM((2, 4, 40, 128), i32),
            pltpu.VMEM((2, 80, 64), jnp.bfloat16),
            pltpu.VMEM((2, 64, 80), jnp.bfloat16),
            pltpu.VMEM((4, 40, 256), f32),
            pltpu.VMEM((4, 48, 256), f32),
            pltpu.VMEM((4, 256, 256), jnp.bfloat16),
            pltpu.VMEM((4, 256, 256), jnp.bfloat16),
            pltpu.VMEM((5, 4, 48, 128), f32),
            pltpu.VMEM((2, 4, 48, 128), f32),
            pltpu.VMEM((5, 4, 40, 128), f32),
            pltpu.VMEM((5, 4, 40, 128), f32),
            pltpu.VMEM((5, 4, 40, 128), f32),
            pltpu.VMEM((2, 20, 4, 128), f32),
            pltpu.VMEM((2, 2, 20, 4, 128), f32),
            pltpu.VMEM((2, 8, 4, 128), i32),
            pltpu.VMEM((2, 8, 4, 128), i32),
            pltpu.VMEM((2, 5, 3, 40, 128), f32),
            pltpu.VMEM((2, 5, 3, 40, 128), f32),
            pltpu.VMEM((2, 3, 40, 128), i32),
            pltpu.VMEM((2, 3, 40, 128), i32),
            pltpu.VMEM((2, 64, 256), f32),
            pltpu.VMEM((64, 256), f32),
            pltpu.VMEM((48, 256), f32),
            pltpu.VMEM((48, 256), f32),
            pltpu.VMEM((2, 32, 256), f32),
            pltpu.VMEM((2, 16, 256), f32),
            pltpu.VMEM((2, 16, 256), f32),
            pltpu.VMEM((2, 64, 128), f32),
            pltpu.VMEM((48, 128), f32),
            pltpu.VMEM((48, 128), f32),
            pltpu.VMEM((2, 16, 128), f32),
            pltpu.VMEM((2, 16, 128), f32),
            pltpu.VMEM((2, 4, 2, 128), f32),
            pltpu.VMEM((2, 4, 2, 128), f32),
            pltpu.VMEM((1, 64, 2, 128), f32),
            pltpu.VMEM((2, 64, 2, 128), f32),
            pltpu.VMEM((2, 64, 2, 128), f32),
            pltpu.VMEM((64, 2, 128), f32),
            pltpu.VMEM((8, 64, 2, 128), f32),
            pltpu.VMEM((64, 4, 128), f32),
            pltpu.VMEM((64, 4, 128), f32),
            pltpu.VMEM((4, 2, 128), f32),
            pltpu.VMEM((4, 2, 128), f32),
            pltpu.VMEM((256, 640), jnp.bfloat16),
            pltpu.VMEM((128, 256), jnp.bfloat16),
            dma((6,)),
            dma((2, 2, 2)),
            dma((2, 2)),
            dma((2, 2, 2)),
            dma((2, 2)),
            dma((2, 2)),
            dma((2, 2)),
            dma((2, 2)),
            dma((2, 2)),
            dma((2, 2, 1)),
            dma((1, 2)),
            dma((2,)),
            dma((2, 8)),
            dma((2,)),
            dma((2, 1)),
            dma((2, 1)),
        ],
        compiler_params=pltpu.CompilerParams(
            collective_id=0, has_side_effects=True, vmem_limit_bytes=40 * 1024 * 1024
        ),
    )(*in_hbm)
    return after - state


def solution(mesh):
    in_specs = (P(None, "ax", "az", None), P(None, "ax", "az", None))
    out_specs = P(None, "ax", "az", None)
    return jax.shard_map(local, mesh=mesh, in_specs=in_specs, out_specs=out_specs, check_vma=False)
```

```python
import math

import jax
import jax.numpy as jnp
import numpy as np
from jax import lax
from jax.experimental import pallas as pl
from jax.experimental.pallas import tpu as pltpu
from jax.sharding import PartitionSpec as P

NRING = 16
MESH = pl.DeviceIdType.MESH

split_speed = 3.0
small_eps = 1e-06
time_step = 0.004


def filter_tables():
    d, k1 = np.arange(64), np.arange(33)
    angle = 2 * np.pi * np.outer(k1, d) / 64
    fwd = np.zeros((80, 64))
    fwd[:33], fwd[40:73] = np.cos(angle), -np.sin(angle)
    inv = np.zeros((64, 80))
    inv[:, :33], inv[:, 40:73] = np.cos(angle.T), -np.sin(angle.T)
    twiddle = np.zeros((4, 40, 256))
    m_in, m_out = np.arange(40), np.arange(-3, 43)
    scale = np.where((k1 == 0) | (k1 == 32), 1.0, 2.0)[:, None] / 2560
    for v in range(5):
        angle = 2 * np.pi * np.outer(k1, m_in) / 2560
        twiddle[0, :33, v * 48 + 3 : v * 48 + 43] = np.cos(angle)
        twiddle[1, :33, v * 48 + 3 : v * 48 + 43] = -np.sin(angle)
        angle = 2 * np.pi * np.outer(k1, m_out) / 2560
        twiddle[2, :33, v * 48 : v * 48 + 46] = np.cos(angle) * scale
        twiddle[3, :33, v * 48 : v * 48 + 46] = np.sin(angle) * scale
    band = np.zeros((16, 4, 48, 256))
    delta = m_out[None, :] - m_in[:, None]
    for j in range(16):
        if j % 2:
            q = (j + 1) // 2
            modes, extra = np.arange(-q, q), -q
        else:
            q = j // 2
            modes, extra = np.arange(-q, q + 1), q
        kept = sum(np.exp(2j * np.pi * k * delta / 40) for k in modes)
        twin = np.exp(2j * np.pi * extra * delta / 40)
        for k, part in enumerate((kept.real, kept.imag, twin.real, twin.imag)):
            band[j, k, 3:43, :46] = part
    return [a.astype(np.float32) for a in (fwd, inv, twiddle, band)]


def split(x):
    high = x.astype(jnp.bfloat16)
    return high, (x - high.astype(jnp.float32)).astype(jnp.bfloat16)


def dot(a, b):
    return jnp.dot(a, b, preferred_element_type=jnp.float32)


def by_left(a_high, a_low, b):
    high, low = split(b)
    return dot(a_high, high) + (dot(a_high, low) + dot(a_low, high))


def by_right(a, b_high, b_low):
    high, low = split(a)
    rows = a.shape[0]
    both = dot(jnp.concatenate([high, low], axis=0), b_high)
    return both[:rows] + (both[rows:] + dot(high, b_low))


def inverse(x):
    return pltpu.reciprocal(x, approx=True)


class Rows:
    def __init__(self, cells):
        self.cells = list(cells)

    def _with(self, other, op):
        if isinstance(other, Rows):
            pairs = zip(self.cells, other.cells)
            return Rows([None if a is None or b is None else op(a, b) for a, b in pairs])
        return Rows([None if a is None else op(a, other) for a in self.cells])

    def __add__(self, other):
        return self._with(other, lambda a, b: a + b)

    def __sub__(self, other):
        return self._with(other, lambda a, b: a - b)

    def __mul__(self, other):
        return self._with(other, lambda a, b: a * b)

    def map(self, op):
        return Rows([None if a is None else op(a) for a in self.cells])

    def shifted(self, by):
        n = len(self.cells)
        return Rows([self.cells[k + by] if 0 <= k + by < n else None for k in range(n)])


def at(x, by):
    if isinstance(x, Rows):
        return x.shifted(by)
    axis = 1 if x.shape[1] == 256 else 0
    n = x.shape[axis]
    return pltpu.roll(x, (n - by) % n, axis)


def inverse_of(x):
    return x.map(inverse) if isinstance(x, Rows) else inverse(x)


def indicators(f):
    d = at(f, 1) - f
    s = d - at(d, -1)
    s_next = at(s, 1)
    e = s - s_next
    h = s * 0.5
    q = s * s * (13.0 / 12.0) + small_eps
    mid = d - h
    up = d + h
    down = mid - s
    x = inverse_of(q + up * up)
    y = inverse_of(q + mid * mid)
    z = inverse_of(q + down * down)
    return d, s, s_next, e, x * x, y * y, z * z


def faces(flux, state, switch, choose):
    half = flux * 0.5
    lift = state * (0.5 * split_speed)
    d_p, s_p, sn_p, e_p, x_p, y_p, z_p = indicators(half + lift)
    zn_p = at(z_p, 1)
    top = at(x_p * e_p, -1) * 2.0 + zn_p * e_p * 3.0
    total = at(x_p, -1) + y_p * 6.0 + zn_p * 3.0
    plus = top * inverse_of(total)
    d_m, s_m, sn_m, e_m, x_m, y_m, z_m = indicators(half - lift)
    zn_m = at(z_m, 1)
    top = at(zn_m * e_m, 1) * 2.0 + x_m * e_m * 3.0
    total = at(zn_m, 1) + at(y_m, 1) * 6.0 + x_m * 3.0
    minus = top * inverse_of(total)
    middle = flux + (d_p + d_m) * 0.5
    own = s_p + sn_m
    weno = (plus - minus - own) * (1.0 / 6.0)
    central = (own + s_m + sn_p) * (-1.0 / 12.0)
    return middle + choose(switch, weno, central)


def pick(switch, a, b):
    if isinstance(a, Rows):
        triples = zip(switch.cells, a.cells, b.cells)
        return Rows([None if s is None or p is None or q is None else jnp.where(s, p, q) for s, p, q in triples])
    return jnp.where(switch, a, b)


def largest(a, b):
    if isinstance(a, Rows):
        return a._with(b, jnp.maximum)
    return jnp.maximum(a, b)


def peak(flags):
    pair = largest(flags, at(flags, 1))
    four = largest(pair, at(pair, 2))
    return at(largest(four, at(pair, 4)), -2)


def window(flags):
    six = peak(flags)
    return six.map(lambda a: a > 0.5) if isinstance(six, Rows) else six > 0.5


def fluxes(u, q, p, component):
    parts = [u[1 + component], u[1] * q, u[2] * q, u[3] * q, (u[4] + p) * q]
    parts[1 + component] = parts[1 + component] + p
    return parts


def pressure(u, inv_rho):
    return (u[4] - (u[1] * u[1] + u[2] * u[2] + u[3] * u[3]) * inv_rho * 0.5) * 0.4


def lanes(shape):
    return lax.broadcasted_iota(jnp.int32, shape, len(shape) - 1)


def radius(rows):
    return lanes((rows, 128)).astype(jnp.float32) + 0.5


def azimuthal(padded, flags, section, rate):
    scale = -1.0 / (radius(40) * (2.0 * math.pi / 2560))

    def row(r, carry):
        u = [padded[v, r] for v in range(5)]
        inv_rho = inverse(u[0])
        q = u[3] * inv_rho
        f = fluxes(u, q, pressure(u, inv_rho), 2)
        switch = window(flags[section, r])
        for v in range(5):
            face = faces(f[v], u[v], switch, pick)
            rate[v, r] = rate[v, r] + (at(face, 3)[:40] - at(face, 2)[:40]) * scale
        return carry

    lax.fori_loop(0, 4, row, 0)


def radial_terms(own, rate):
    inv_r = 1.0 / radius(8)
    lane = lanes((8, 128))

    def chunk(c, carry):
        at8 = pl.ds(pl.multiple_of(c * 8, 8), 8)
        for r in range(4):
            here = [own[v, r, at8, :] for v in range(5)]
            inv_here = inverse(here[0])
            p_here = pressure(here, inv_here)
            g = fluxes(here, here[2] * inv_here, p_here, 1)
            swirl = here[3] * inv_here
            extra = [None, None, here[3] * swirl + p_here, -here[2] * swirl, None]
            for v in range(5):
                before = pltpu.roll(g[v], 1, 1)
                after = jnp.where(lane == 127, g[v], pltpu.roll(g[v], 127, 1))
                away = g[v] if extra[v] is None else g[v] - extra[v]
                rate[v, r, at8, :] = (before - after) * 0.5 - away * inv_r
        return carry

    lax.fori_loop(0, 5, chunk, 0)


def finish(own, low, high, flags, flags_low, flags_high, section, rate, combine):
    def chunk(c, carry):
        at8 = pl.ds(pl.multiple_of(c * 8, 8), 8)
        u = [
            Rows(
                [low[v, k, at8, :] for k in range(3)]
                + [own[v, k, at8, :] for k in range(4)]
                + [high[v, k, at8, :] for k in range(3)]
            )
            for v in range(5)
        ]
        marks = Rows(
            [flags_low[section, k, at8, :] for k in range(3)]
            + [flags[section, k, at8, :] for k in range(4)]
            + [flags_high[section, k, at8, :] for k in range(3)]
        ).map(lambda a: a.astype(jnp.float32))
        switch = window(marks)
        inv_rho = u[0].map(inverse)
        f = fluxes(u, u[1] * inv_rho, pressure(u, inv_rho), 0)
        for v in range(5):
            face = faces(f[v], u[v], switch, pick).cells
            for r in range(4):
                slope = rate[v, r, at8, :] - (face[3 + r] - face[2 + r])
                combine(v, r, at8, u[v].cells[3 + r], slope)
        return carry

    lax.fori_loop(0, 5, chunk, 0, unroll=5)


def cell_of(width):
    return lax.rem(lanes((16, width)), 48)


def side_by_side(blocks):
    lane = lanes(blocks[0].shape)
    packed = blocks[0]
    for r in range(1, 4):
        packed = jnp.where(lane >= 32 * r, pltpu.roll(blocks[r], 32 * r, 1), packed)
    return packed


def pack_state(padded):
    stacks = []
    for r in range(4):
        rest = jnp.zeros((16, 128), jnp.float32)
        stacks.append(jnp.concatenate([padded[v, r] for v in range(5)] + [rest], axis=0))
    return jnp.transpose(side_by_side(stacks))


def pack_flags(padded_flags):
    stacks = []
    for r in range(4):
        rest = jnp.zeros((32, 128), jnp.float32)
        stacks.append(jnp.concatenate([padded_flags[0, r], padded_flags[1, r], rest], axis=0))
    return jnp.transpose(side_by_side(stacks))


def fold_ends(blocks, width):
    cell = cell_of(width)
    to_right = jnp.zeros((16, width), jnp.float32)
    to_left = to_right
    for r in range(4):
        moved = pltpu.roll(blocks[r], (width - 40 + 3 * r) % width, 1)
        to_right = jnp.where((cell >= 3 * r) & (cell < 3 * r + 3), moved, to_right)
        moved = pltpu.roll(blocks[r], 31 + 3 * r, 1)
        to_left = jnp.where((cell >= 34 + 3 * r) & (cell < 37 + 3 * r), moved, to_left)
    return to_right, to_left


def with_ends(block, from_left, from_right, r):
    width = block.shape[1]
    cell = cell_of(width)
    before = pltpu.roll(from_left, width - 3 * r, 1) if r else from_left
    after = pltpu.roll(from_right, 9 - 3 * r, 1) if r < 3 else from_right
    return jnp.where(cell < 3, before, jnp.where(cell < 43, block, jnp.where(cell < 46, after, 0.0)))


def replicate(x):
    x = jnp.where(lanes(x.shape) < 48, x, 0.0)
    one = jnp.concatenate([x, jnp.zeros_like(x)], axis=1)
    two = one + pltpu.roll(one, 48, 1)
    four = two + pltpu.roll(two, 96, 1)
    return four + pltpu.roll(one, 192, 1)


def slot(shape, k):
    lane = lanes(shape)
    return (lane >= 48 * k) & (lane < 48 * k + 48)


def packed_flux(u, q, p, component):
    own, energy = slot(u.shape, 1 + component), slot(u.shape, 4)
    return u * q + jnp.where(own, p, jnp.where(energy, p * q, 0.0))


def near_azimuthal(own, marks, rate, apart, copies):
    blocks = [own(r) for r in range(4)]
    (_, _, q_t), p = stacked_primitives(blocks, apart)
    wide = select(jnp.concatenate([p, q_t], axis=0), copies[...])
    every = dot(jnp.concatenate([marks(r) for r in range(4)], axis=0).astype(jnp.bfloat16), copies[...])
    cycle = lax.broadcasted_iota(jnp.int32, (16, 256), 0).astype(jnp.float32) + 0.5
    inv_rh = 1.0 / (cycle * (2.0 * math.pi / 2560))
    for r, u in enumerate(blocks):
        wide_p, wide_t = wide[16 * r : 16 * r + 16], wide[64 + 16 * r : 80 + 16 * r]
        f = packed_flux(u, wide_t, wide_p, 2)
        face = faces(f, u, window(every[16 * r : 16 * r + 16]), pick)
        rate[16 * r : 16 * r + 16, :] = (at(face, -1) - face) * inv_rh


def near_finish(low, own, high, outer, ghost, marks, rate, apart, copies, combine):
    blocks = [low(k) for k in range(3)] + [own(r) for r in range(4)] + [high(k) for k in range(3)]
    row = lax.broadcasted_iota(jnp.int32, (8, 256), 0)
    negated = slot((8, 256), 2) | slot((8, 256), 3)
    beyond = []
    for r in range(4):
        mirrored = jnp.broadcast_to(ghost(r), (8, 256))
        beyond.append(jnp.where(row == 7, jnp.where(negated, -mirrored, mirrored), outer(r)))
    (q_x, q_r, q_t), p = stacked_primitives(blocks + beyond, apart)
    stacked = jnp.concatenate([p, q_x[:160], q_r[48:112], q_r[160:], q_t[48:112]], axis=0)
    wide = select(stacked, copies[...])
    every = dot(jnp.concatenate(marks, axis=0).astype(jnp.bfloat16), copies[...])
    switches = [every[16 * k : 16 * k + 16] for k in range(10)]
    f = [
        packed_flux(u, wide[192 + 16 * k : 208 + 16 * k], wide[16 * k : 16 * k + 16], 0)
        for k, u in enumerate(blocks)
    ]
    cycle = lax.broadcasted_iota(jnp.int32, (16, 256), 0).astype(jnp.float32) + 0.5
    inv_r = 1.0 / cycle
    radial = []
    for r in range(4):
        u, wide_p = blocks[3 + r], wide[48 + 16 * r : 64 + 16 * r]
        g = packed_flux(u, wide[352 + 16 * r : 368 + 16 * r], wide_p, 1)
        g_beyond = packed_flux(beyond[r], wide[416 + 8 * r : 424 + 8 * r], wide[160 + 8 * r : 168 + 8 * r], 1)
        drag = drag_of(u, wide[448 + 16 * r : 464 + 16 * r], wide_p)
        ring = jnp.concatenate([g, g_beyond], axis=0)
        after, before = pltpu.roll(ring, 23, 0)[:16], pltpu.roll(ring, 1, 0)[:16]
        radial.append((after - before) * 0.5 + (g - drag) * inv_r)
    slopes = [[[None, None], [None, None]] for _ in range(4)]
    for h in range(2):
        for w in range(2):
            part = (slice(8 * h, 8 * h + 8), slice(128 * w, 128 * w + 128))
            face = faces(
                Rows([x[part] for x in f]),
                Rows([x[part] for x in blocks]),
                window(Rows([x[part] for x in switches])),
                pick,
            ).cells
            for r in range(4):
                slopes[r][h][w] = face[2 + r] - face[3 + r]
    lane = lanes((16, 256))
    cell = lax.rem(lane, 48)
    valid = (cell >= 3) & (cell < 43) & (lane < 240)
    for r in range(4):
        rows = [jnp.concatenate(pair, axis=1) for pair in slopes[r]]
        slope = jnp.concatenate(rows, axis=0) - radial[r] + rate[16 * r : 16 * r + 16, :]
        combine(r, jnp.where(valid, slope, 0.0), valid)


def packed_rows(ref, first, count):
    rows = pl.ds(first, count)
    return jnp.concatenate([ref[rows, 0, :], ref[rows, 1, :]], axis=1)


def place_of(r, group):
    return 32 * group + 8 * r


def build_selectors(apart, copies):
    to, source = lanes((256, 640)), lax.broadcasted_iota(jnp.int32, (256, 640), 0)
    cell = lax.rem(to, 128)
    hit = (cell < 48) & (source == cell + 48 * (to // 128))
    apart[...] = jnp.where(hit, 1.0, 0.0).astype(jnp.bfloat16)
    to, source = lanes((128, 256)), lax.broadcasted_iota(jnp.int32, (128, 256), 0)
    hit = (source == lax.rem(to, 48)) & (to < 240)
    copies[...] = jnp.where(hit, 1.0, 0.0).astype(jnp.bfloat16)


def select(values, selector):
    high, low = split(values)
    both = dot(jnp.concatenate([high, low], axis=0), selector)
    n = values.shape[0]
    return both[:n] + both[n:]


def stacked_primitives(blocks, apart):
    every = select(jnp.concatenate(blocks, axis=0), apart[...])
    parts = [every[:, 128 * k : 128 * k + 128] for k in range(5)]
    inv_rho = inverse(jnp.where(parts[0] == 0.0, 1.0, parts[0]))
    return [parts[k] * inv_rho for k in (1, 2, 3)], pressure(parts, inv_rho)


def drag_of(u, q_t, p):
    turned = jnp.where(slot(u.shape, 3), -pltpu.roll(u, 48, 1) * q_t, 0.0)
    return jnp.where(slot(u.shape, 2), pltpu.roll(u, 256 - 48, 1) * q_t + p, turned)


def line_alone(own_line, extra, cycle, partial, apart, copies):
    radius_here = jnp.full((16, 256), cycle, jnp.int32).astype(jnp.float32) + 0.5
    inv_r = 1.0 / radius_here
    inv_rh = 1.0 / (radius_here * (2.0 * math.pi / 2560))
    blocks = [packed_rows(own_line, 16 * c, 16) for c in range(4)]
    (_, q_r, q_t), p = stacked_primitives(blocks, apart)
    wide = select(jnp.concatenate([p, q_r, q_t], axis=0), copies[...])
    marks = jnp.concatenate([extra[:, 2, :], extra[:, 3, :]], axis=1)
    marks = pltpu.roll(marks, 256 - 96, 1)[:, :128].astype(jnp.bfloat16)
    marks = dot(marks, copies[...]) > 0.5
    for c, own in enumerate(blocks):
        wide_p, wide_r, wide_t = [wide[64 * k + 16 * c : 64 * k + 16 * c + 16] for k in range(3)]
        g = packed_flux(own, wide_r, wide_p, 1)
        turn = packed_flux(own, wide_t, wide_p, 2)
        face = faces(turn, own, marks[16 * c : 16 * c + 16], pick)
        slope = (at(face, -1) - face) * inv_rh - (g - drag_of(own, wide_t, wide_p)) * inv_r
        partial[16 * c : 16 * c + 16, :] = slope


def line_rates(own_line, lines, extra, partial, target, apart, copies):
    lane = lanes((16, 256))
    cell = lax.rem(lane, 48)
    valid = (cell >= 3) & (cell < 43) & (lane < 240)
    for c in range(4):
        first = 16 * c
        own = packed_rows(own_line, first, 16)
        blocks = [packed_rows(lines.at[k], first, 16) for k in range(3)] + [own]
        blocks += [packed_rows(lines.at[k], first, 16) for k in range(3, 8)]
        (q_x, q_r, _), p = stacked_primitives(blocks, apart)
        stacked = jnp.concatenate([p, q_x[:112], q_r[112:]], axis=0)
        spread_out = select(stacked, copies[...])
        wide = [spread_out[16 * k : 16 * k + 16] for k in range(18)]
        f = [packed_flux(blocks[k], wide[9 + k], wide[k], 0) for k in range(7)]
        sides = [packed_flux(blocks[7 + k], wide[16 + k], wide[7 + k], 1) for k in range(2)]
        blocks = blocks[:7]
        rows = pl.ds(first, 16)
        marks = jnp.concatenate([extra[rows, 2, :], extra[rows, 3, :]], axis=1)
        marks = jnp.concatenate([marks[:, :128], pltpu.roll(marks, 256 - 48, 1)[:, :128]], axis=0)
        marks = dot(marks.astype(jnp.bfloat16), copies[...]) > 0.5
        below, above = marks[:16], marks[16:]
        halves = []
        for h in range(2):
            pair = []
            for w in range(2):
                part = (slice(8 * h, 8 * h + 8), slice(128 * w, 128 * w + 128))
                face = faces(
                    Rows([x[part] for x in f]),
                    Rows([x[part] for x in blocks]),
                    Rows([None, None, below[part], above[part], None, None, None]),
                    pick,
                ).cells
                pair.append(face[2] - face[3])
            halves.append(jnp.concatenate(pair, axis=1))
        slope = jnp.concatenate(halves, axis=0) + partial[rows, :] - (sides[1] - sides[0]) * 0.5
        before = jnp.concatenate([extra[rows, 0, :], extra[rows, 1, :]], axis=1)
        value = jnp.where(valid, before * 0.75 + (own + slope * time_step) * 0.25, 0.0)
        target[rows, 0, :] = value[:, :128]
        target[rows, 1, :] = value[:, 128:]


def unpack(rows):
    n = rows.shape[0]
    turned = jnp.transpose(jnp.concatenate([rows, jnp.zeros((128 - n, 256), jnp.float32)], axis=0))

    def block(v, k):
        cells = turned[48 * v : 48 * v + 48]
        return pltpu.roll(cells, (128 - k) % 128, 1) if k % 128 else cells

    return block


def others(me):
    y, x, z = me // 32, lax.rem(me // 8, 4), lax.rem(me, 8)
    ys = {d: lax.rem(y + d, 2) * 32 for d in (1, 0)}
    xs = {d: lax.rem(x + d, 4) * 8 for d in (2, 1, 3, 0)}
    zs = {d: lax.rem(z + d, 8) for d in (4, 3, 5, 2, 6, 1, 7, 0)}
    steps = [(dy, dx, dz) for dz in zs for dx in xs for dy in ys]
    steps.sort(key=lambda s: -(s[0] + min(s[1], 4 - s[1]) + min(s[2], 8 - s[2])))
    return [ys[dy] + xs[dx] + zs[dz] for dy, dx, dz in steps[:-1]]


def spread(send, recv, me, peers, send_sem, recv_sem):
    for to in peers:
        pltpu.make_async_remote_copy(
            src_ref=send.at[to],
            dst_ref=recv.at[me],
            send_sem=send_sem,
            recv_sem=recv_sem,
            device_id={"az": to},
            device_id_type=MESH,
        ).start()
    recv[pl.ds(me, 1)] = send[pl.ds(me, 1)]


def arrived(buffer, sem):
    rows = buffer.at[pl.ds(0, 63)]
    pltpu.make_async_copy(rows, rows, sem).wait()


def build_mix(mine, mix_high, mix_low):
    mix_high[...] = jnp.zeros_like(mix_high)
    mix_low[...] = jnp.zeros_like(mix_low)
    for k in range(4):
        rows = []
        for v in range(5):
            rows.append(pltpu.roll(mine[k], 48 * v, 1) if v else mine[k])
        rows.append(jnp.zeros((16, 256), jnp.float32))
        mix_high[k], mix_low[k] = split(jnp.concatenate(rows, axis=0))


def project(recv, back, me, fwd, inv, twiddle, mix_high, mix_low):
    x = jnp.concatenate([recv[:, 0, :], recv[:, 1, :]], axis=1)
    a = by_left(fwd[0], fwd[1], x)
    re, im = a[:40], a[40:]
    re, im = re * twiddle[0] - im * twiddle[1], re * twiddle[1] + im * twiddle[0]
    odd = lax.rem(me, 2) == 1
    first_row = lax.broadcasted_iota(jnp.int32, (8, 256), 0) == 0

    def twin_row(x):
        return jnp.where(first_row, jnp.where(odd, x[:8], x[32:40]), 0.0)

    main = jnp.concatenate([re, im], axis=0)
    twin = jnp.concatenate([twin_row(re), twin_row(im)], axis=0)
    c, s = by_right(main, mix_high[0], mix_low[0]), by_right(main, mix_high[1], mix_low[1])
    tc, ts = by_right(twin, mix_high[2], mix_low[2]), by_right(twin, mix_high[3], mix_low[3])
    re, im = c[:40] - s[40:], s[:40] + c[40:]
    t_re, t_im = tc[:8] - ts[8:], ts[:8] + tc[8:]

    def with_twin(x, t):
        top = x[:8] + jnp.where(odd, t, 0.0)
        return jnp.concatenate([top, x[8:32], x[32:40] + jnp.where(odd, 0.0, t)], axis=0)

    re, im = with_twin(re, t_re), with_twin(im, t_im)
    re, im = re * twiddle[2] - im * twiddle[3], re * twiddle[3] + im * twiddle[2]
    y = by_left(inv[0], inv[1], jnp.concatenate([re, im], axis=0))
    back[:, 0, :] = y[:, :128]
    back[:, 1, :] = y[:, 128:]


def kernel(
    state_hbm, flags_hbm, fwd_hbm, inv_hbm, twiddle_hbm, band, out,
    state, flags, fwd, inv, twiddle, mine, mix_high, mix_low, padded, padded_flags, rate, first, second,
    az_out, az_in, azf_out, azf_in, low, high, flow, fhigh,
    near, near_rate, near_low, near_high, near_outer, ends_out, ends_in, marks, marks_low, marks_high,
    mark_ends_out, mark_ends_in, ghost_out, ghost_in,
    send, recv, back, ret, lines, extra_out, extra_in, outer_out, rim_in, apart, copies,
    sem, az_sem, azf_sem, ax_sem, axf_sem, end_sem, mark_end_sem, row_sem, mark_row_sem, ghost_sem,
    go_sem, come_sem, line_sem, extra_sem, outer_sem, rim_sem,
):
    me, row = lax.axis_index("az"), lax.axis_index("ax")
    right, left = lax.rem(me + 1, 64), lax.rem(me + 63, 64)
    upper, lower = lax.rem(row + 1, 4), lax.rem(row + 3, 4)
    opposite = lax.rem(me + 32, 64)
    z, x, y = lax.rem(me, 8), lax.rem(me // 8, 4), me // 32
    level, cycle = x, 8 * y + z
    pairs = [
        (state_hbm, state),
        (flags_hbm, flags),
        (fwd_hbm, fwd),
        (inv_hbm, inv),
        (twiddle_hbm, twiddle),
        (band.at[cycle], mine),
    ]
    loads = [pltpu.make_async_copy(a, b, sem.at[k]) for k, (a, b) in enumerate(pairs)]
    for item in loads:
        item.start()
    barrier = pltpu.get_barrier_semaphore()
    peers = others(me)
    for peer in peers:
        pl.semaphore_signal(barrier, inc=1, device_id={"az": peer}, device_id_type=MESH)
    for peer in (upper, lower):
        pl.semaphore_signal(barrier, inc=1, device_id={"ax": peer}, device_id_type=MESH)

    def copy(src, dst, sems, k, **place):
        return pltpu.make_async_remote_copy(
            src_ref=src,
            dst_ref=dst,
            send_sem=sems.at[0, k],
            recv_sem=sems.at[1, k],
            device_id=place,
            device_id_type=MESH,
        )

    def along_az(source, target, sems):
        return [
            copy(source.at[0], target.at[0], sems, 0, az=right),
            copy(source.at[1], target.at[1], sems, 1, az=left),
        ]

    def along_ax(up_from, to_low, down_from, to_high, sems):
        return copy(up_from, to_low, sems, 0, ax=upper), copy(down_from, to_high, sems, 1, ax=lower)

    def wide_ax(field, to_low, to_high, sems):
        return along_ax(field.at[:, pl.ds(1, 3)], to_low, field.at[:, pl.ds(0, 3)], to_high, sems)

    def stage(field, staging, fields):
        for f in range(fields):
            for r in range(4):
                staging[0, f * 4 + r, 0:3] = field[f, r, 37:40]
                staging[1, f * 4 + r, 0:3] = field[f, r, 0:3]

    def when_up(action):
        pl.when(row < 3)(action)

    def when_down(action):
        pl.when(row > 0)(action)

    def start_ax(pair):
        when_up(pair[0].start)
        when_down(pair[1].start)

    def sent_ax(pair):
        when_up(pair[0].wait_send)
        when_down(pair[1].wait_send)

    def came_ax(pair):
        when_down(pair[0].wait_recv)
        when_up(pair[1].wait_recv)

    def start_all(items):
        for item in items:
            item.start()

    def came_all(items):
        for item in items:
            item.wait_recv()

    def sent_all(items):
        for item in items:
            item.wait_send()

    padded[...] = jnp.zeros_like(padded)
    padded_flags[...] = jnp.zeros_like(padded_flags)
    loads[0].wait()
    loads[1].wait()
    for v in range(5):
        for r in range(4):
            padded[v, r, 3:43] = state[v, r]
    for s in range(2):
        for r in range(4):
            padded_flags[s, r, 3:43] = flags[s, r].astype(jnp.float32)
    packed = pack_state(padded)
    for r in range(4):
        near[0, 16 * r : 16 * r + 16, :] = packed[32 * r : 32 * r + 16]
        near_outer[0, 8 * r : 8 * r + 8, :] = packed[32 * r + 16 : 32 * r + 24]
        ghost_out[0, r, 0:1, :] = packed[32 * r : 32 * r + 1, :128]
        ghost_out[0, r, 1:2, :] = packed[32 * r : 32 * r + 1, 128:]
    ends_out[0], ends_out[1] = fold_ends([packed[32 * r : 32 * r + 16] for r in range(4)], 256)
    packed = pack_flags(padded_flags)
    for r in range(4):
        marks[0, 16 * r : 16 * r + 16, :] = packed[32 * r : 32 * r + 16]
    mark_ends_out[0], mark_ends_out[1] = fold_ends([packed[32 * r : 32 * r + 16] for r in range(4)], 128)
    ends = along_az(ends_out, ends_in, end_sem)
    mark_ends = along_az(mark_ends_out, mark_ends_in, mark_end_sem)
    rows = along_ax(near.at[0, pl.ds(16, 48)], near_low, near.at[0, pl.ds(0, 48)], near_high, row_sem)
    mark_rows = along_ax(marks.at[0, pl.ds(16, 48)], marks_low, marks.at[0, pl.ds(0, 48)], marks_high, mark_row_sem)
    ghost = copy(ghost_out.at[0], ghost_in.at[0], ghost_sem.at[0], 0, az=opposite)
    stage(state, az_out, 5)
    stage(flags, azf_out, 2)
    az = along_az(az_out, az_in.at[0], az_sem.at[0])
    azf = along_az(azf_out, azf_in, azf_sem)
    ax = wide_ax(state, low.at[0], high.at[0], ax_sem.at[0])
    axf = wide_ax(flags, flow, fhigh, axf_sem)
    radial_terms(state, rate)
    pl.semaphore_wait(barrier, 65)
    start_all(ends)
    start_all(mark_ends)
    ghost.start()
    start_ax(rows)
    start_ax(mark_rows)
    start_all(az)
    start_all(azf)
    start_ax(ax)
    start_ax(axf)
    for item in loads[2:]:
        item.wait()
    build_mix(mine, mix_high, mix_low)
    build_selectors(apart, copies)

    came_all(ends)
    came_all(mark_ends)
    for r in range(4):
        at_row = slice(16 * r, 16 * r + 16)
        near[1, at_row, :] = with_ends(near[0, at_row, :], ends_in[0], ends_in[1], r)
        marks[1, at_row, :] = with_ends(marks[0, at_row, :], mark_ends_in[0], mark_ends_in[1], r)

    def own_state(r):
        return near[1, 16 * r : 16 * r + 16, :]

    def own_marks(r):
        return marks[1, 16 * r : 16 * r + 16, :]

    near_azimuthal(own_state, own_marks, near_rate, apart, copies)
    came_ax(rows)
    came_ax(mark_rows)

    def low_rim():
        for k in range(3):
            near_low[16 * k : 16 * k + 16, :] = near[1, 0:16, :]
            marks_low[16 * k : 16 * k + 16, :] = marks[1, 0:16, :]

    def high_rim():
        for k in range(3):
            near_high[16 * k : 16 * k + 16, :] = near[1, 48:64, :]
            marks_high[16 * k : 16 * k + 16, :] = marks[1, 48:64, :]

    pl.when(row == 0)(low_rim)
    pl.when(row == 3)(high_rim)
    ghost.wait_recv()

    def mark_list():
        below = [marks_low[16 * k : 16 * k + 16, :] for k in range(3)]
        above = [marks_high[16 * k : 16 * k + 16, :] for k in range(3)]
        return below + [own_marks(r) for r in range(4)] + above

    def ghost_row(section):
        return lambda r: jnp.concatenate([ghost_in[section, r, 0:1, :], ghost_in[section, r, 1:2, :]], axis=1)

    def outer_rows(section):
        return lambda r: near_outer[section, 8 * r : 8 * r + 8, :]

    def hand_in(section, r, value):
        for group in range(2):
            first_place = place_of(r, group)
            for h in range(2):
                part = value[8 * group : 8 * group + 8, 128 * h : 128 * h + 128]
                send[section, first_place : first_place + 8, h, :] = part

    def near_first(r, slope, valid):
        hand_in(0, r, jnp.where(valid, own_state(r) + slope * time_step, 0.0))

    near_finish(
        lambda k: near_low[16 * k : 16 * k + 16, :],
        own_state,
        lambda k: near_high[16 * k : 16 * k + 16, :],
        outer_rows(0),
        ghost_row(0),
        mark_list(),
        near_rate,
        apart,
        copies,
        near_first,
    )
    spread(send.at[0], recv.at[0], me, peers, go_sem.at[0, 0], go_sem.at[0, 1])

    tall = Rows(mark_list()).map(lambda a: replicate(pltpu.roll(a, 80, 1)))
    axial_marks = peak(tall).cells
    for r in range(4):
        low_part, high_part, turn_part = axial_marks[2 + r], axial_marks[3 + r], peak(tall.cells[3 + r])
        own_slot = [slot((16, 256), k) for k in range(3)]
        row_marks = jnp.where(own_slot[1], high_part, jnp.where(own_slot[2], turn_part, 0.0))
        row_marks = jnp.where(own_slot[0], low_part, row_marks)
        whole_row = [own_state(r)[:, :128], own_state(r)[:, 128:], row_marks[:, :128], row_marks[:, 128:]]
        for group in range(2):
            first_place = place_of(r, group)
            for k in range(4):
                extra_out[first_place : first_place + 8, k, :] = whole_row[k][8 * group : 8 * group + 8]
    spread(extra_out, extra_in, me, peers, extra_sem.at[0], extra_sem.at[1])

    sent_ax(rows)
    sent_ax(mark_rows)
    sent_all(ends + mark_ends + [ghost])

    def fill_az(section):
        for v in range(5):
            for r in range(4):
                padded[v, r, 0:3] = az_in[section, 0, v * 4 + r, 0:3]
                padded[v, r, 43:46] = az_in[section, 1, v * 4 + r, 0:3]

    came_all(az)
    came_all(azf)
    fill_az(0)
    for s in range(2):
        for r in range(4):
            padded_flags[s, r, 0:3] = azf_in[0, s * 4 + r, 0:3].astype(jnp.float32)
            padded_flags[s, r, 43:46] = azf_in[1, s * 4 + r, 0:3].astype(jnp.float32)
    azimuthal(padded, padded_flags, 0, rate)
    came_ax(ax)
    came_ax(axf)

    def rims(field, section):
        def low_rim():
            for v in range(5):
                for k in range(3):
                    low[section, v, k] = field[v, 0]

        def high_rim():
            for v in range(5):
                for k in range(3):
                    high[section, v, k] = field[v, 3]

        pl.when(row == 0)(low_rim)
        pl.when(row == 3)(high_rim)

    def flag_low_rim():
        for s in range(2):
            for k in range(3):
                flow[s, k] = flags[s, 0]

    def flag_high_rim():
        for s in range(2):
            for k in range(3):
                fhigh[s, k] = flags[s, 3]

    rims(state, 0)
    pl.when(row == 0)(flag_low_rim)
    pl.when(row == 3)(flag_high_rim)

    def combine_first(v, r, rows, here, slope):
        first[v, r, rows, :] = here + slope * time_step

    finish(state, low.at[0], high.at[0], flags, flow, fhigh, 0, rate, combine_first)
    sent_all(az + azf)
    for v in range(5):
        for r in range(4):
            padded[v, r, 3:43] = first[v, r]
    packed = pack_state(padded)
    for r in range(4):
        outer_out[r, 0:1, :] = packed[32 * r + 16 : 32 * r + 17, :128]
        outer_out[r, 1:2, :] = packed[32 * r + 16 : 32 * r + 17, 128:]
    for r in range(4):
        last = place_of(r, 1) + 7
        beyond = copy(outer_out.at[r], lines.at[7, me], outer_sem, 0, az=last)
        pl.when(me != last)(beyond.start)
    is_last, is_first = cycle == 15, cycle == 0

    def keep_outer():
        lines[7, pl.ds(me, 1)] = outer_out[pl.ds(level, 1)]

    pl.when(is_last)(keep_outer)
    arrived(recv.at[0], go_sem.at[0, 1])
    project(recv.at[0], back.at[0], me, fwd, inv, twiddle, mix_high, mix_low)

    column = 32 * y + z
    meets = []
    for step in range(1, 4):
        over, under = level + step, level + 4 - step
        to_row, to_level = row + over // 4, lax.rem(over, 4)
        to = 8 * to_level + column
        item = copy(back.at[0], lines.at[3 - step], line_sem, 3 - step, ax=to_row, az=to)
        has_over, has_under = (row < 3) | (over < 4), (row > 0) | (under >= 4)
        meets.append((item, has_over, has_under))
        to_row, to_level = row - 1 + under // 4, lax.rem(under, 4)
        to = 8 * to_level + column
        item = copy(back.at[0], lines.at[2 + step], line_sem, 2 + step, ax=to_row, az=to)
        meets.append((item, has_under, has_over))
    base = 8 * level
    ahead, behind = cycle + 1, cycle + 15
    to = base + 32 * (ahead // 8) + lax.rem(ahead, 8)
    item = copy(back.at[0], lines.at[6], line_sem, 6, az=to)
    not_first, not_last = jnp.logical_not(is_first), jnp.logical_not(is_last)
    meets.append((item, not_last, not_first))
    behind = lax.rem(behind, 16)
    to = base + 32 * (behind // 8) + lax.rem(behind, 8)
    item = copy(back.at[0], lines.at[7], line_sem, 7, az=to)
    meets.append((item, not_first, not_last))
    for item, sends, _ in meets:
        pl.when(sends)(item.start)
    stage(first, az_out, 5)
    az = along_az(az_out, az_in.at[1], az_sem.at[1])
    start_all(az)

    def hand_rim():
        for to in peers:
            copy(back.at[0, to], rim_in.at[level], rim_sem, 0, az=to).start()
        rim_in[pl.ds(level, 1)] = back[0, pl.ds(me, 1)]

    pl.when(is_last)(hand_rim)

    def mirror():
        lane = lanes((64, 128))
        for h in range(2):
            flipped = (lane + 128 * h >= 96) & (lane + 128 * h < 192)
            turned = jnp.concatenate([back[0, 32:64, h, :], back[0, 0:32, h, :]], axis=0)
            lines[6, :, h, :] = jnp.where(flipped, -turned, turned)

    pl.when(is_first)(mirror)
    arrived(extra_in, extra_sem.at[1])
    line_alone(back.at[0], extra_in, cycle, near_rate, apart, copies)
    for item, _, comes in meets:
        pl.when(comes)(item.wait_recv)
    pl.when(is_last)(lambda: arrived(lines.at[7], outer_sem.at[1, 0]))
    for r in range(3):

        def clamp_low():
            for step in range(r + 1, 4):
                lines[3 - step] = lines[3 - r] if r else back[0]

        def clamp_high():
            for step in range(r + 1, 4):
                lines[2 + step] = lines[2 + r] if r else back[0]

        pl.when((row == 0) & (level == r))(clamp_low)
        pl.when((row == 3) & (level == 3 - r))(clamp_high)
    ax2 = wide_ax(first, low.at[1], high.at[1], ax_sem.at[1])
    start_ax(ax2)
    line_rates(back.at[0], lines, extra_in, near_rate, recv.at[1], apart, copies)
    project(recv.at[1], back.at[1], me, fwd, inv, twiddle, mix_high, mix_low)
    spread(back.at[1], ret, me, peers, come_sem.at[0], come_sem.at[1])

    sent_ax(ax)
    sent_ax(axf)
    came_all(az)
    sent_all(az)
    fill_az(1)
    sent_ax(ax2)
    def rim_but_own():
        part = rim_in.at[pl.ds(0, 3)]
        pltpu.make_async_copy(part, part, rim_sem.at[1, 0]).wait()

    pl.when(is_last)(rim_but_own)
    pl.when(not_last)(pltpu.make_async_copy(rim_in, rim_in, rim_sem.at[1, 0]).wait)
    block = unpack(jnp.concatenate([packed_rows(rim_in, 0, 4), jnp.zeros((4, 256), jnp.float32)], axis=0))
    lane40 = lanes((40, 128))
    for r in range(4):
        for v in range(5):
            first[v, r] = jnp.where(lane40 == 15, block(v, r - 15)[3:43], first[v, r])

    radial_terms(first, rate)
    azimuthal(padded, padded_flags, 1, rate)
    came_ax(ax2)
    rims(first, 1)

    def combine_second(v, r, rows, here, slope):
        second[v, r, rows, :] = state[v, r, rows, :] * 0.75 + (here + slope * time_step) * 0.25

    finish(first, low.at[1], high.at[1], flags, flow, fhigh, 1, rate, combine_second)
    arrived(send.at[0], go_sem.at[0, 0])
    arrived(extra_out, extra_sem.at[0])
    for item, sends, _ in meets:
        pl.when(sends)(item.wait_send)
    pl.when(is_last)(lambda: arrived(back.at[0], rim_sem.at[0, 0]))

    def outers(n):
        part = outer_out.at[pl.ds(0, n)]
        pltpu.make_async_copy(part, part, outer_sem.at[0, 0]).wait()

    pl.when(is_last)(lambda: outers(3))
    pl.when(not_last)(lambda: outers(4))
    arrived(ret, come_sem.at[1])
    order = [packed_rows(ret, place_of(r, group), 8) for r in range(4) for group in range(2)]
    block = unpack(jnp.concatenate(order, axis=0))
    for r in range(4):
        for v in range(5):
            out[v, r] = jnp.where(lane40 < NRING, block(v, 16 * r)[3:43], second[v, r])
    arrived(back.at[1], come_sem.at[0])


def local(state, shock_flags):
    fwd, inv, twiddle, band = filter_tables()
    tables = [jnp.stack(split(jnp.asarray(t))) for t in (fwd, inv)]
    tables += [jnp.asarray(twiddle), jnp.asarray(band)]
    vmem = pl.BlockSpec(memory_space=pltpu.VMEM)
    f32, i32 = jnp.float32, jnp.int32
    dma = pltpu.SemaphoreType.DMA
    in_hbm = [pltpu.with_memory_space_constraint(x, pltpu.HBM) for x in (state, shock_flags, *tables)]
    after = pl.pallas_call(
        kernel,
        out_shape=jax.ShapeDtypeStruct(state.shape, f32),
        in_specs=[pl.BlockSpec(memory_space=pltpu.HBM)] * 6,
        out_specs=vmem,
        scratch_shapes=[
            pltpu.VMEM((5, 4, 40, 128), f32),
            pltpu.VMEM((2, 4, 40, 128), i32),
            pltpu.VMEM((2, 80, 64), jnp.bfloat16),
            pltpu.VMEM((2, 64, 80), jnp.bfloat16),
            pltpu.VMEM((4, 40, 256), f32),
            pltpu.VMEM((4, 48, 256), f32),
            pltpu.VMEM((4, 256, 256), jnp.bfloat16),
            pltpu.VMEM((4, 256, 256), jnp.bfloat16),
            pltpu.VMEM((5, 4, 48, 128), f32),
            pltpu.VMEM((2, 4, 48, 128), f32),
            pltpu.VMEM((5, 4, 40, 128), f32),
            pltpu.VMEM((5, 4, 40, 128), f32),
            pltpu.VMEM((5, 4, 40, 128), f32),
            pltpu.VMEM((2, 20, 4, 128), f32),
            pltpu.VMEM((2, 2, 20, 4, 128), f32),
            pltpu.VMEM((2, 8, 4, 128), i32),
            pltpu.VMEM((2, 8, 4, 128), i32),
            pltpu.VMEM((2, 5, 3, 40, 128), f32),
            pltpu.VMEM((2, 5, 3, 40, 128), f32),
            pltpu.VMEM((2, 3, 40, 128), i32),
            pltpu.VMEM((2, 3, 40, 128), i32),
            pltpu.VMEM((2, 64, 256), f32),
            pltpu.VMEM((64, 256), f32),
            pltpu.VMEM((48, 256), f32),
            pltpu.VMEM((48, 256), f32),
            pltpu.VMEM((2, 32, 256), f32),
            pltpu.VMEM((2, 16, 256), f32),
            pltpu.VMEM((2, 16, 256), f32),
            pltpu.VMEM((2, 64, 128), f32),
            pltpu.VMEM((48, 128), f32),
            pltpu.VMEM((48, 128), f32),
            pltpu.VMEM((2, 16, 128), f32),
            pltpu.VMEM((2, 16, 128), f32),
            pltpu.VMEM((2, 4, 2, 128), f32),
            pltpu.VMEM((2, 4, 2, 128), f32),
            pltpu.VMEM((1, 64, 2, 128), f32),
            pltpu.VMEM((2, 64, 2, 128), f32),
            pltpu.VMEM((2, 64, 2, 128), f32),
            pltpu.VMEM((64, 2, 128), f32),
            pltpu.VMEM((8, 64, 2, 128), f32),
            pltpu.VMEM((64, 4, 128), f32),
            pltpu.VMEM((64, 4, 128), f32),
            pltpu.VMEM((4, 2, 128), f32),
            pltpu.VMEM((4, 2, 128), f32),
            pltpu.VMEM((256, 640), jnp.bfloat16),
            pltpu.VMEM((128, 256), jnp.bfloat16),
            dma((6,)),
            dma((2, 2, 2)),
            dma((2, 2)),
            dma((2, 2, 2)),
            dma((2, 2)),
            dma((2, 2)),
            dma((2, 2)),
            dma((2, 2)),
            dma((2, 2)),
            dma((2, 2, 1)),
            dma((1, 2)),
            dma((2,)),
            dma((2, 8)),
            dma((2,)),
            dma((2, 1)),
            dma((2, 1)),
        ],
        compiler_params=pltpu.CompilerParams(
            collective_id=0, has_side_effects=True, vmem_limit_bytes=40 * 1024 * 1024
        ),
    )(*in_hbm)
    return after - state


def solution(mesh):
    in_specs = (P(None, "ax", "az", None), P(None, "ax", "az", None))
    out_specs = P(None, "ax", "az", None)
    return jax.shard_map(local, mesh=mesh, in_specs=in_specs, out_specs=out_specs, check_vma=False)
```
